32 devices in a mesh: section: 4 (over y, x), batch: 8 (over z, core).
Axes of the slice: x: 2, y: 2, z: 4, core: 2. Of those that a mesh axis runs over, the one named last changes fastest.
Arguments:
- tokens: bfloat16 [32, 416, 384], P(('section', 'batch')), may hold values from -6 to 6
- levels: int32 [32], P(('section', 'batch')), may hold values from 5 to 13, as said below
- lead: int32 [32], P(('section', 'batch')), may hold values from 0 to 39
- w_qkv: bfloat16 [4, 384, 1152], P('section', 'batch'), may hold values from -0.3125 to 0.3125
- w_o: bfloat16 [4, 384, 384], P('section', 'batch'), may hold values from -2 to 2
- b_o: bfloat16 [4, 384], P('section', 'batch'), may hold values from -1.796875 to 1.796875
- w_up: bfloat16 [4, 384, 1536], P('section', 'batch'), may hold values from -0.3125 to 0.3125
- b_up: bfloat16 [4, 1536], P('section', 'batch'), may hold values from -1.796875 to 1.796875
- w_down: bfloat16 [4, 1536, 384], P('section', 'batch'), may hold values from -0.15625 to 0.15625
- b_down: bfloat16 [4, 384], P('section', 'batch'), may hold values from -1.796875 to 1.796875
- w_ada: bfloat16 [4, 384, 2304], P('section', 'batch'), may hold values from -0.625 to 0.625
- b_ada: bfloat16 [4, 2304], P('section', 'batch'), may hold values from -1.796875 to 1.796875
- cotangent: bfloat16 [32, 416, 384], P(('section', 'batch')), may hold values from -6 to 6
Outputs:
- result: bfloat16 [32, 416, 384], P(('section', 'batch'))
- grad_tokens: bfloat16 [32, 416, 384], P(('section', 'batch'))
- grad_w_qkv: float32 [4, 384, 1152], P('section', 'batch')
- grad_w_o: float32 [4, 384, 384], P('section', 'batch')
- grad_b_o: float32 [4, 384], P('section', 'batch')
- grad_w_up: float32 [4, 384, 1536], P('section', 'batch')
- grad_b_up: float32 [4, 1536], P('section', 'batch')
- grad_w_down: float32 [4, 1536, 384], P('section', 'batch')
- grad_b_down: float32 [4, 384], P('section', 'batch')
- grad_w_ada: float32 [4, 384, 2304], P('section', 'batch')
- grad_b_ada: float32 [4, 2304], P('section', 'batch')
The draws below stay inside these ranges and needn't reach their ends.
Inputs may be any that keep to these rules, and one draw needn't show every extreme that they name: Count of pressure levels present in each item; keys of levels at or above it are masked. Some item has 13 and some has 5.
All inputs are finite; a program needn't handle non-finite values.
Results may differ from the reference program's by a relative error of at most 0.019.
Values may be sent and summed in bfloat16 or wider, within the bound.
No kernel may reach another device: no remote copies, remote signals or barrier semaphores. Data moves between devices by JAX's collectives and lax.ppermute only.
A program may use at most 320 MiB of HBM per device.

```python
import math
import jax
import jax.numpy as jnp
from jax import lax

D = 384
HEADS = 6
HEAD = 64
FF = 1536
LEVELS = 13
LEADS = 40
PATCH = 32
SEQ = 416
LAYERS = 4
ITEMS = 32


def draw_levels(key, part):
    key = jax.random.fold_in(key, 11)
    first, second, third = jax.random.split(key, 3)
    counts = jax.random.randint(first, (ITEMS,), 5, LEVELS + 1)
    top_slot = jax.random.randint(second, (), 0, ITEMS)
    low_slot = (top_slot + 1 + jax.random.randint(third, (), 0, ITEMS - 1)) % ITEMS
    places = jnp.arange(ITEMS)
    counts = jnp.where(places == top_slot, LEVELS, counts)
    counts = jnp.where(places == low_slot, 5, counts)
    return counts.astype(jnp.int32)


def touch_ends(entries, own_key, low, largest):
    longest = entries.shape.index(max(entries.shape))
    spots = []
    for shift in (0, 1):
        where = [jax.random.randint(jax.random.fold_in(own_key, axis), (), 0, length) for axis, length in enumerate(entries.shape)]
        where[longest] = (where[longest] + shift) % entries.shape[longest]
        spots.append(tuple(where))
    return entries.at[spots[0]].set(low).at[spots[1]].set(largest)


def block_levels(key, extent, cuts, low, largest):
    loudness = 1.0
    for position, shards_of in cuts:
        heights = jax.random.uniform(jax.random.fold_in(jax.random.fold_in(key, 6), position), (shards_of,), jnp.float32, low / len(cuts), largest / len(cuts))
        loudness = loudness * jnp.repeat(jnp.exp(heights), extent[position] // shards_of).reshape((-1,) + (1,) * (len(extent) - 1 - position))
    return loudness


def bell_draw(key, shape, width, limit, shards=(), held_as=jnp.bfloat16):
    level = block_levels(key, shape, shards, -0.22, 0.18) if shards else 1.0
    result = jax.random.normal(key, shape, jnp.float32) * width * level
    return jnp.minimum(jnp.maximum(result, -limit), limit).astype(held_as)


def setup_inputs(seed: int = 0) -> dict:
    streams_of = jax.random.split(jax.random.key(seed), 14)
    tokens = bell_draw(streams_of[0], (ITEMS, SEQ, D), 1.0, 6.0, ((0, 32),))
    levels = draw_levels(jax.random.fold_in(streams_of[13], 71), 0)
    lead = touch_ends(jax.random.randint(streams_of[2], (ITEMS,), 0, LEADS), jax.random.fold_in(streams_of[2], 1), 0, LEADS - 1).astype(jnp.int32)
    w_qkv = bell_draw(streams_of[3], (LAYERS, D, 3 * D), D ** -0.5, 0.3125, ((0, 4), (1, 8)))
    w_o = bell_draw(streams_of[4], (LAYERS, D, D), (max(8 * D // SEQ, 1)) ** -0.5, 2.0, ((0, 4), (1, 8)))
    b_o = bell_draw(streams_of[5], (LAYERS, D), 0.3, 1.796875, ((0, 4), (1, 8)))
    w_up = bell_draw(streams_of[6], (LAYERS, D, FF), D ** -0.5, 0.3125, ((0, 4), (1, 8)))
    b_up = bell_draw(streams_of[7], (LAYERS, FF), 0.3, 1.796875, ((0, 4), (1, 8)))
    w_down = bell_draw(streams_of[8], (LAYERS, FF, D), FF ** -0.5, 0.15625, ((0, 4), (1, 8)))
    b_down = bell_draw(streams_of[9], (LAYERS, D), 0.3, 1.796875, ((0, 4), (1, 8)))
    w_ada = bell_draw(streams_of[10], (LAYERS, D, 6 * D), (D // 4) ** -0.5, 0.625, ((0, 4), (1, 8)))
    b_ada = bell_draw(streams_of[11], (LAYERS, 6 * D), 0.3, 1.796875, ((0, 4), (1, 8)))
    cotangent = bell_draw(streams_of[12], (ITEMS, SEQ, D), 1.0, 6.0, ((0, 32),))
    return dict(tokens=tokens, levels=levels, lead=lead, w_qkv=w_qkv, w_o=w_o, b_o=b_o, w_up=w_up, b_up=b_up, w_down=w_down, b_down=b_down, w_ada=w_ada, b_ada=b_ada, cotangent=cotangent)


@jax.custom_vjp
def low(v):
    return lax.optimization_barrier(v.astype(jnp.bfloat16)).astype(jnp.float32)

@jax.custom_vjp
def low_back(v):
    return v

def low_keep(v):
    return (low(v), None)

def low_pass(kept, grad):
    return (grad,)

def back_keep(v):
    return (v, None)

def back_low(kept, grad):
    return (low(grad),)
low.defvjp(low_keep, low_pass)
low_back.defvjp(back_keep, back_low)
HIGH = lax.Precision.HIGHEST

def normalize(value):
    centered = value - lax.optimization_barrier(jnp.mean(value, -1, keepdims=True))
    return centered * lax.rsqrt(lax.optimization_barrier(jnp.mean(centered * centered, -1, keepdims=True)) + 1e-06)

def embed_lead(step):
    half = D // 2
    freq = jnp.exp(-math.log(10000.0) * jnp.arange(half, dtype=jnp.float32) / half)
    angle = 6.0 * step.astype(jnp.float32) * freq
    return jnp.concatenate([jnp.sin(angle), jnp.cos(angle)])

def layer(value, mod, key_ok, wq, wo, bo, wu, bu, wd, bd):
    shift_a, scale_a, gate_a, shift_b, scale_b, gate_b = jnp.split(mod, 6)
    value = low(low_back(value))
    hidden_a = low(normalize(value) * (1.0 + scale_a) + shift_a)
    qkv = low(low_back(jnp.dot(hidden_a, wq, precision=HIGH)))
    query = qkv[:, :D].reshape(SEQ, HEADS, HEAD)
    keys = qkv[:, D:2 * D].reshape(SEQ, HEADS, HEAD)
    values = qkv[:, 2 * D:].reshape(SEQ, HEADS, HEAD)
    raw = low_back(jnp.einsum('qhe,khe->hqk', query, keys, precision=HIGH))
    scores = jnp.where(key_ok[None, None, :], raw * HEAD ** (-0.5), -1e+30)
    probs = low(jax.nn.softmax(scores, -1))
    mixed = jnp.einsum('hqk,khe->qhe', probs, values, precision=HIGH).reshape(SEQ, D)
    mixed = low(low_back(mixed))
    branch_a = low_back(jnp.dot(mixed, wo, precision=HIGH) + bo)
    middle = value + gate_a * branch_a
    hidden_b = low(normalize(middle) * (1.0 + scale_b) + shift_b)
    pre = low_back(jnp.dot(hidden_b, wu, precision=HIGH) + bu)
    act = low(jax.nn.gelu(pre))
    branch_b = low_back(jnp.dot(act, wd, precision=HIGH) + bd)
    return middle + gate_b * branch_b

def run_item(value, count, step, weights):
    wq, wo, bo, wu, bu, wd, bd, wa, ba = weights
    cond = jax.nn.silu(embed_lead(step))
    key_ok = jnp.arange(SEQ) // PATCH < count
    for index in range(LAYERS):
        mod = jnp.dot(cond, wa[index], precision=HIGH) + ba[index]
        value = layer(value, mod, key_ok, wq[index], wo[index], bo[index], wu[index], bu[index], wd[index], bd[index])
    return value

def reference(tokens, levels, lead, w_qkv, w_o, b_o, w_up, b_up, w_down, b_down, w_ada, b_ada, cotangent):
    floats = (w_qkv.astype(jnp.float32), w_o.astype(jnp.float32), b_o.astype(jnp.float32), w_up.astype(jnp.float32), b_up.astype(jnp.float32), w_down.astype(jnp.float32), b_down.astype(jnp.float32), w_ada.astype(jnp.float32), b_ada.astype(jnp.float32))
    saved_item = jax.checkpoint(run_item)

    def model(value, wq, wo, bo, wu, bu, wd, bd, wa, ba):
        weights = (wq, wo, bo, wu, bu, wd, bd, wa, ba)
        return lax.map(lambda item: saved_item(item[0], item[1], item[2], weights), (value, levels, lead))
    output, pullback = jax.vjp(model, tokens.astype(jnp.float32), *floats)
    grads = pullback(cotangent.astype(jnp.float32))
    return (output.astype(jnp.bfloat16), grads[0].astype(jnp.bfloat16), grads[1], grads[2], grads[3], grads[4], grads[5], grads[6], grads[7], grads[8], grads[9])
```

```python
import math

import jax
import jax.numpy as jnp
from jax import lax
from jax.sharding import PartitionSpec as P

HEADS = 6
LEVELS = 13


EPS = 1e-06
NEG = -1e30
HIGH = lax.Precision.HIGHEST


def shifted(array, axis, by):
    devices = lax.axis_size(axis)
    pairs = [(i, i + by) for i in range(devices) if 0 <= i + by < devices]
    return lax.ppermute(array, axis, pairs)


def normalize(value):
    centered = value - jnp.mean(value, -1, keepdims=True)
    rstd = lax.rsqrt(jnp.mean(centered * centered, -1, keepdims=True) + EPS)
    return (centered * rstd, rstd)


def normalize_back(grad, normed, rstd):
    return rstd * (
        grad
        - jnp.mean(grad, -1, keepdims=True)
        - normed * jnp.mean(grad * normed, -1, keepdims=True)
    )


def contract_rows(left, right):
    return lax.dot_general(
        left, right, (((0,), (0,)), ((), ())), preferred_element_type=jnp.float32
    )


def contract_cols(left, right):
    return lax.dot_general(
        left, right, (((1,), (1,)), ((), ())), preferred_element_type=jnp.float32
    )


def embed_lead(steps, width):
    half = width // 2
    freq = jnp.exp(-math.log(10000.0) * jnp.arange(half, dtype=jnp.float32) / half)
    angle = 6.0 * steps.astype(jnp.float32)[:, None] * freq[None, :]
    return jnp.concatenate([jnp.sin(angle), jnp.cos(angle)], -1)


def head_probs(query, keys, key_ok, factor):
    raw = jnp.einsum("qe,ke->qk", query, keys, preferred_element_type=jnp.float32) * factor
    return jax.nn.softmax(jnp.where(key_ok[None, :], raw, NEG), -1)


def head_cols(qkv16, part, head, width):
    size = width // HEADS
    return qkv16[:, part * width + head * size : part * width + (head + 1) * size]


def layer_forward(value16, mod, key_ok, weights):
    w_qkv, w_o, b_o, w_up, b_up, w_down, b_down = weights
    width = value16.shape[1]
    factor = (width // HEADS) ** (-0.5)
    shift_a, scale_a, gate_a, shift_b, scale_b, gate_b = jnp.split(mod, 6)
    inputs = value16.astype(jnp.float32)
    normed_a, rstd_a = normalize(inputs)
    hidden_a = (normed_a * (1.0 + scale_a) + shift_a).astype(jnp.bfloat16)
    qkv16 = jnp.dot(hidden_a, w_qkv, preferred_element_type=jnp.float32).astype(jnp.bfloat16)
    pieces = []
    for head in range(HEADS):
        probs = head_probs(
            head_cols(qkv16, 0, head, width), head_cols(qkv16, 1, head, width), key_ok, factor
        )
        pieces.append(
            jnp.dot(
                probs.astype(jnp.bfloat16),
                head_cols(qkv16, 2, head, width),
                preferred_element_type=jnp.float32,
            )
        )
    mixed16 = jnp.concatenate(pieces, -1).astype(jnp.bfloat16)
    branch_a = jnp.dot(mixed16, w_o, preferred_element_type=jnp.float32) + b_o.astype(jnp.float32)
    middle = inputs + gate_a * branch_a
    normed_b, rstd_b = normalize(middle)
    hidden_b = (normed_b * (1.0 + scale_b) + shift_b).astype(jnp.bfloat16)
    pre = jnp.dot(hidden_b, w_up, preferred_element_type=jnp.float32) + b_up.astype(jnp.float32)
    act, act_back = jax.vjp(jax.nn.gelu, pre)
    act16 = act.astype(jnp.bfloat16)
    branch_b = jnp.dot(act16, w_down, preferred_element_type=jnp.float32) + b_down.astype(
        jnp.float32
    )
    result = middle + gate_b * branch_b
    saved = (
        normed_a,
        rstd_a,
        hidden_a,
        qkv16,
        mixed16,
        branch_a,
        normed_b,
        rstd_b,
        hidden_b,
        act_back,
        act16,
        branch_b,
    )
    return (result, saved)


def layer_backward(value16, grad16, mod, cond_row, key_ok, weights):
    w_qkv, w_o, b_o, w_up, b_up, w_down, b_down = weights
    width = value16.shape[1]
    factor = (width // HEADS) ** (-0.5)
    shift_a, scale_a, gate_a, shift_b, scale_b, gate_b = jnp.split(mod, 6)
    result, saved = layer_forward(value16, mod, key_ok, weights)
    (
        normed_a,
        rstd_a,
        hidden_a,
        qkv16,
        mixed16,
        branch_a,
        normed_b,
        rstd_b,
        hidden_b,
        act_back,
        act16,
        branch_b,
    ) = saved
    grad_out = grad16.astype(jnp.float32)
    grad_gate_b = jnp.sum(grad_out * branch_b, 0)
    grad_bb = (grad_out * gate_b).astype(jnp.bfloat16)
    g_w_down = contract_rows(act16, grad_bb)
    g_b_down = jnp.sum(grad_bb.astype(jnp.float32), 0)
    grad_act = contract_cols(grad_bb, w_down)
    grad_pre = act_back(grad_act)[0].astype(jnp.bfloat16)
    g_w_up = contract_rows(hidden_b, grad_pre)
    g_b_up = jnp.sum(grad_pre.astype(jnp.float32), 0)
    grad_hb = contract_cols(grad_pre, w_up)
    grad_shift_b = jnp.sum(grad_hb, 0)
    grad_scale_b = jnp.sum(grad_hb * normed_b, 0)
    grad_middle = grad_out + normalize_back(grad_hb * (1.0 + scale_b), normed_b, rstd_b)
    grad_gate_a = jnp.sum(grad_middle * branch_a, 0)
    grad_ba = (grad_middle * gate_a).astype(jnp.bfloat16)
    g_w_o = contract_rows(mixed16, grad_ba)
    g_b_o = jnp.sum(grad_ba.astype(jnp.float32), 0)
    grad_mixed = contract_cols(grad_ba, w_o).astype(jnp.bfloat16)
    size = width // HEADS
    query_parts, key_parts, value_parts = ([], [], [])
    for head in range(HEADS):
        query = head_cols(qkv16, 0, head, width)
        keys = head_cols(qkv16, 1, head, width)
        values = head_cols(qkv16, 2, head, width)
        grad_head = grad_mixed[:, head * size : (head + 1) * size]
        probs = head_probs(query, keys, key_ok, factor)
        value_parts.append(contract_rows(probs.astype(jnp.bfloat16), grad_head))
        grad_probs = jnp.einsum("qe,ke->qk", grad_head, values, preferred_element_type=jnp.float32)
        grad_raw = (
            probs * (grad_probs - jnp.sum(grad_probs * probs, -1, keepdims=True)) * factor
        ).astype(jnp.bfloat16)
        query_parts.append(jnp.dot(grad_raw, keys, preferred_element_type=jnp.float32))
        key_parts.append(contract_rows(grad_raw, query))
    grad_qkv = jnp.concatenate(query_parts + key_parts + value_parts, -1).astype(jnp.bfloat16)
    g_w_qkv = contract_rows(hidden_a, grad_qkv)
    grad_ha = contract_cols(grad_qkv, w_qkv)
    grad_shift_a = jnp.sum(grad_ha, 0)
    grad_scale_a = jnp.sum(grad_ha * normed_a, 0)
    grad_inputs = grad_middle + normalize_back(grad_ha * (1.0 + scale_a), normed_a, rstd_a)
    grad_mod = jnp.concatenate(
        [grad_shift_a, grad_scale_a, grad_gate_a, grad_shift_b, grad_scale_b, grad_gate_b]
    )
    g_w_ada = cond_row[:, None] * grad_mod[None, :]
    grads = (g_w_qkv, g_w_o, g_b_o, g_w_up, g_b_up, g_w_down, g_b_down, g_w_ada, grad_mod)
    return (grad_inputs.astype(jnp.bfloat16), grads)


BOTH = ("section", "batch")


def body(
    tokens, levels, lead, w_qkv, w_o, b_o, w_up, b_up, w_down, b_down, w_ada, b_ada, cotangent
):
    batch = lax.axis_index("batch")
    sections, batches = lax.axis_size("section"), lax.axis_size("batch")
    width, seq_len = tokens.shape[2], tokens.shape[1]
    rows = width // batches

    def whole(piece):
        full = lax.all_gather(piece, "batch", axis=1, tiled=True)
        return lax.all_gather(full, "section", axis=0, tiled=True)

    def blocks_of(piece):
        return jnp.stack(jnp.split(piece, piece.shape[1] // width, axis=1))

    shard = jnp.concatenate(
        [
            blocks_of(w_qkv[0]),
            w_o,
            blocks_of(w_up[0]),
            w_down[0].reshape(4, rows, width),
        ]
    )
    shards = lax.all_gather(shard, BOTH, axis=0, tiled=False)
    shards = shards.reshape(sections, batches, 12, rows, width)
    front = jnp.swapaxes(shards[:, :, :8], 1, 2).reshape(sections, 8, width, width)
    downs = shards[:, :, 8:].reshape(sections, 4 * width, width)
    small = jnp.concatenate([b_o[0], b_up[0], b_down[0]])
    smalls = lax.all_gather(small, BOTH, axis=0, tiled=False).reshape(sections, batches, -1)
    bias_o = smalls[:, :, :rows].reshape(sections, width)
    bias_up = smalls[:, :, rows : 5 * rows].reshape(sections, 4 * width)
    bias_down = smalls[:, :, 5 * rows :].reshape(sections, width)

    leads = lax.all_gather(lead, BOTH, axis=0, tiled=True)
    conds = jax.nn.silu(embed_lead(leads, width))
    mine = lax.dynamic_slice_in_dim(conds, batch * rows, rows, axis=1)
    part = jnp.dot(mine, w_ada[0].astype(jnp.float32), precision=HIGH)
    bias = jnp.zeros((6 * width,), jnp.float32)
    bias = lax.dynamic_update_slice_in_dim(
        bias, b_ada[0].astype(jnp.float32), batch * 6 * rows, axis=0
    )
    part = (part + bias).reshape(sections, batches, 6 * width)
    part = lax.psum_scatter(part, "batch", scatter_dimension=1, tiled=True)
    mods = lax.all_to_all(part[:, 0], "section", 0, 0, tiled=True)

    patch = seq_len // LEVELS
    key_ok = (jnp.arange(seq_len) // patch) < levels[0]
    cond_row = jnp.zeros((1,), jnp.float32)

    def weights_of(layer):
        return (
            jnp.concatenate([front[layer, 0], front[layer, 1], front[layer, 2]], axis=1),
            front[layer, 3],
            bias_o[layer],
            jnp.concatenate([front[layer, 4 + j] for j in range(4)], axis=1),
            bias_up[layer],
            downs[layer],
            bias_down[layer],
        )

    value = tokens[0]
    kept = []
    for layer in range(sections):
        kept.append(value)
        value = layer_forward(value, mods[layer], key_ok, weights_of(layer))[0].astype(jnp.bfloat16)
    result = value[None]
    grad = cotangent[0]
    all_grads = [None] * sections
    for layer in reversed(range(sections)):
        grad, all_grads[layer] = layer_backward(
            kept[layer], grad, mods[layer], cond_row, key_ok, weights_of(layer)
        )
    outs = []
    for k in range(7):
        full = jnp.stack([grads[k] for grads in all_grads])
        if full.ndim == 3:
            full = full.astype(jnp.bfloat16)
        total = lax.psum_scatter(full, "section", scatter_dimension=0, tiled=True)
        total = lax.psum_scatter(total, "batch", scatter_dimension=1, tiled=True)
        outs.append(total.astype(jnp.float32))
    grad_mods = jnp.stack([grads[8] for grads in all_grads])
    grad_mods = lax.all_to_all(grad_mods, "section", 0, 0, tiled=True)
    every = lax.all_gather(grad_mods, "batch", axis=1, tiled=False)
    every = every.reshape(sections * batches, 6 * width)
    g_ada = jnp.dot(mine.T, every, precision=HIGH)[None]
    g_bada = lax.dynamic_slice_in_dim(jnp.sum(every, 0), batch * 6 * rows, 6 * rows)[None]
    return (result, grad[None], *outs, g_ada, g_bada)


def solution(mesh):
    in_specs = (
        P(("section", "batch"), None, None),
        P(("section", "batch")),
        P(("section", "batch")),
        P("section", "batch", None),
        P("section", "batch", None),
        P("section", "batch"),
        P("section", "batch", None),
        P("section", "batch"),
        P("section", "batch", None),
        P("section", "batch"),
        P("section", "batch", None),
        P("section", "batch"),
        P(("section", "batch"), None, None),
    )
    out_specs = (
        P(("section", "batch"), None, None),
        P(("section", "batch"), None, None),
        P("section", "batch", None),
        P("section", "batch", None),
        P("section", "batch"),
        P("section", "batch", None),
        P("section", "batch"),
        P("section", "batch", None),
        P("section", "batch"),
        P("section", "batch", None),
        P("section", "batch"),
    )
    return jax.shard_map(body, mesh=mesh, in_specs=in_specs, out_specs=out_specs, check_vma=False)
```

```python
import functools
import math

import jax
import jax.numpy as jnp
from jax import lax
from jax.experimental import pallas as pl
from jax.experimental.pallas import tpu as pltpu
from jax.sharding import PartitionSpec as P

HEADS = 6
LEVELS = 13
BLOCKS = 12
SHARDS = 8
EPS = 1e-06
NEG = -1e30
BF = jnp.bfloat16
F32 = jnp.float32
HIGH = lax.Precision.HIGHEST
C0 = math.sqrt(2.0 / math.pi)
C1 = 0.044715
VMEM_LIMIT = 60 * 2**20


def dot(left, right, over=(1, 0)):
    return lax.dot_general(
        left, right, (((over[0],), (over[1],)), ((), ())), preferred_element_type=F32
    )


def standard(value):
    centered = value - jnp.mean(value, -1, keepdims=True)
    rstd = lax.rsqrt(jnp.mean(centered * centered, -1, keepdims=True) + EPS)
    return centered * rstd, rstd


def standard_back(grad, normed, rstd):
    return rstd * (
        grad
        - jnp.mean(grad, -1, keepdims=True)
        - normed * jnp.mean(grad * normed, -1, keepdims=True)
    )


def forward_kernel(plan, ids, tokens, mods, biases, *refs):
    count = len({part[0] for parts in plan.values() for part in parts})
    sources, refs = refs[:count], refs[count:]
    result, w_out, xs, qkv, probs, mixed, branch_a, act, slope, branch_b = refs[:10]
    value, hidden, acc, w, in_sem, out_sem = refs[10:]
    layer = pl.program_id(0)
    layers = pl.num_programs(0)
    seq, width = value.shape
    size = width // HEADS
    section, place, core = ids[0], ids[1], ids[2]

    @pl.when(layer == 0)
    def _():
        value[...] = tokens[0]

        @pl.loop(0, layers)
        def _(target):
            for away in range(4):

                @pl.when(jnp.bitwise_xor(section, target) == away)
                def _():
                    for (sx, zx, cx), parts in plan.items():
                        if sx != away:
                            continue
                        shard = 2 * jnp.bitwise_xor(place, zx) + jnp.bitwise_xor(core, cx)
                        for index, lead, low, high in parts:
                            ref = sources[index]
                            top = min(high, 8)
                            if low < top:
                                pltpu.make_async_copy(
                                    ref.at[pl.ds(lead, top - low)],
                                    w.at[target, pl.ds(low, top - low), shard],
                                    in_sem.at[target],
                                ).start()
                            if high > 8:
                                pltpu.make_async_copy(
                                    ref.at[pl.ds(lead + 8 - low, 4)],
                                    w.at[target, 8 + shard // 2, pl.ds(4 * (shard % 2), 4)],
                                    in_sem.at[target],
                                ).start()

    pltpu.make_async_copy(w.at[layer], w.at[layer], in_sem.at[layer]).wait()
    pltpu.make_async_copy(w.at[layer], w_out.at[layer], out_sem.at[layer]).start()

    def weight(j):
        return w[layer, j].reshape(width, width)

    here = jnp.bitwise_xor(section, layer)
    mod = mods[here]
    bias = biases[here]
    xs[0] = value[...]
    x = value[...].astype(F32)
    normed, _ = standard(x)
    hidden[...] = (normed * (1.0 + mod[1:2]) + mod[0:1]).astype(BF)
    for j in range(3):
        qkv[0, :, j * width : (j + 1) * width] = dot(hidden[...], weight(j)).astype(BF)
    limit = ids[3] * (seq // LEVELS)
    row = lax.broadcasted_iota(jnp.int32, (seq, 1), 0)
    mask = jnp.where(row < limit, 0.0, NEG)
    for h in range(HEADS):
        q = qkv[0, :, h * size : (h + 1) * size] * (size**-0.5)
        k = qkv[0, :, width + h * size : width + (h + 1) * size]
        v = qkv[0, :, 2 * width + h * size : 2 * width + (h + 1) * size]
        raw = dot(k, q, (1, 1)) + mask
        top = jnp.max(raw, axis=0, keepdims=True)
        e = jnp.exp(raw - top)
        p = (e * (1.0 / jnp.sum(e, axis=0, keepdims=True))).astype(BF)
        probs[0, h] = p
        mixed[0, h * size : (h + 1) * size, :] = dot(v, p, (0, 0)).astype(BF)
    ba = dot(mixed[0], weight(3), (0, 0)) + bias[0:1]
    branch_a[0] = ba
    middle = value[...].astype(F32) + mod[2:3] * ba
    acc[...] = middle
    normed, _ = standard(middle)
    hidden[...] = (normed * (1.0 + mod[4:5]) + mod[3:4]).astype(BF)
    down = None
    for j in range(4):
        cols = slice(j * width, (j + 1) * width)
        pre = dot(hidden[...], weight(4 + j)) + bias[1 + j : 2 + j]
        square = pre * pre
        t = jnp.tanh(pre * (C0 + (C0 * C1) * square))
        half = 0.5 + 0.5 * t
        a = pre * half
        slope[0, :, cols] = (half + a * (1.0 - t) * (C0 + (3.0 * C0 * C1) * square)).astype(BF)
        act[0, :, cols] = a.astype(BF)
        part = dot(act[0, :, cols], weight(8 + j))
        down = part if down is None else down + part
    bb = down + bias[5:6]
    branch_b[0] = bb.astype(BF)
    out = (acc[...] + mod[5:6] * bb).astype(BF)
    value[...] = out
    result[0] = out

    @pl.when(layer == layers - 1)
    def _():
        @pl.loop(0, layers)
        def _(target):
            pltpu.make_async_copy(w.at[target], w_out.at[target], out_sem.at[target]).wait()


def forward(plan, sources, ids, tokens, mods, biases):
    layers = mods.shape[0]
    _, seq, width = tokens.shape
    rows = width // SHARDS

    def per_layer(*shape):
        return pl.BlockSpec((1,) + shape, lambda l: (l,) + (0,) * len(shape))

    def same(*shape):
        return pl.BlockSpec(shape, lambda l: (0,) * len(shape))

    shapes = [
        ((seq, width), BF),
        ((seq, 3 * width), BF),
        ((HEADS, seq, seq), BF),
        ((width, seq), BF),
        ((seq, width), F32),
        ((seq, 4 * width), BF),
        ((seq, 4 * width), BF),
        ((seq, width), BF),
    ]
    hbm = pl.BlockSpec(memory_space=pl.ANY)
    return pl.pallas_call(
        functools.partial(forward_kernel, plan),
        grid=(layers,),
        in_specs=[
            pl.BlockSpec(memory_space=pltpu.SMEM),
            same(1, seq, width),
            same(layers, 6, width),
            same(layers, 6, width),
        ]
        + [hbm] * len(sources),
        out_specs=[same(1, seq, width), hbm] + [per_layer(*s) for s, _ in shapes],
        out_shape=[
            jax.ShapeDtypeStruct((1, seq, width), BF),
            jax.ShapeDtypeStruct((layers, BLOCKS, SHARDS, rows, width), BF),
        ]
        + [jax.ShapeDtypeStruct((layers,) + s, d) for s, d in shapes],
        scratch_shapes=[
            pltpu.VMEM((seq, width), BF),
            pltpu.VMEM((seq, width), BF),
            pltpu.VMEM((seq, width), F32),
            pltpu.VMEM((layers, BLOCKS, SHARDS, rows, width), BF),
            pltpu.SemaphoreType.DMA((layers,)),
            pltpu.SemaphoreType.DMA((layers,)),
        ],
        compiler_params=pltpu.CompilerParams(vmem_limit_bytes=VMEM_LIMIT),
        cost_estimate=pl.CostEstimate(
            flops=layers * 1_740_000_000, bytes_accessed=80_000_000, transcendentals=0
        ),
        name="forward",
    )(ids, tokens, mods, biases, *sources)


def backward_kernel(
    layer, ids, grad, mods, w, xs, qkv, probs, mixed, branch_a, act, slope, branch_b,
    grad_in, kept, sent, vec, gbb, hid, gsum, gmix, gqkv, dqt, halves, sems,
):
    seq, width = gbb.shape
    size = width // HEADS
    section, place, core = ids[0], ids[1], ids[2]
    rows = width // SHARDS

    def weight(j):
        return w[0, j].reshape(width, width)

    def keep(shard, block, value):
        half = jnp.bitwise_xor(core, shard % 2)
        halves[half, jnp.bitwise_xor(place, shard // 2), block] = value

    def keep_front(block, value):
        for shard in range(SHARDS):
            keep(shard, block, value[shard * rows : (shard + 1) * rows])

    def keep_down(j, value):
        for part in range(SHARDS):
            keep(2 * j + part // 4, 8 + part % 4, value[part * rows : (part + 1) * rows])

    mod = mods[jnp.bitwise_xor(section, layer)]
    shift_a, scale_a, gate_a, shift_b, scale_b, gate_b = (mod[i : i + 1] for i in range(6))
    gout = grad[0].astype(F32)
    vec[5:6] = jnp.sum(gout * branch_b[0].astype(F32), 0, keepdims=True)
    gb = (gout * gate_b).astype(BF)
    gbb[...] = gb
    vec[11:12] = jnp.sum(gb.astype(F32), 0, keepdims=True)
    x = xs[0].astype(F32)
    middle = x + gate_a * branch_a[0]
    normed_b, rstd_b = standard(middle)
    hid[...] = (normed_b * (1.0 + scale_b) + shift_b).astype(BF)
    total = None
    for j in range(4):
        cols = slice(j * width, (j + 1) * width)
        keep_down(j, dot(act[0, :, cols], gbb[...], (0, 0)).astype(BF))
        gact = dot(gbb[...], weight(8 + j), (1, 1))
        gpre = (gact * slope[0, :, cols].astype(F32)).astype(BF)
        vec[7 + j : 8 + j] = jnp.sum(gpre.astype(F32), 0, keepdims=True)
        keep_front(4 + j, dot(hid[...], gpre, (0, 0)).astype(BF))
        part = dot(gpre, weight(4 + j), (1, 1))
        total = part if total is None else total + part
    ghb = total
    vec[3:4] = jnp.sum(ghb, 0, keepdims=True)
    vec[4:5] = jnp.sum(ghb * normed_b, 0, keepdims=True)
    gmid = gout + standard_back(ghb * (1.0 + scale_b), normed_b, rstd_b)
    gsum[...] = gmid
    vec[2:3] = jnp.sum(gmid * branch_a[0], 0, keepdims=True)
    gba = (gmid * gate_a).astype(BF)
    gbb[...] = gba
    vec[6:7] = jnp.sum(gba.astype(F32), 0, keepdims=True)
    keep_front(3, dot(mixed[0], gbb[...]).astype(BF))
    gmix[...] = dot(gbb[...], weight(3), (1, 1)).astype(BF)
    factor = size ** -0.5
    for h in range(HEADS):
        q = qkv[0, :, h * size : (h + 1) * size]
        k = qkv[0, :, width + h * size : width + (h + 1) * size]
        v = qkv[0, :, 2 * width + h * size : 2 * width + (h + 1) * size]
        g = gmix[:, h * size : (h + 1) * size]
        p = probs[0, h]
        pf = p.astype(F32)
        dp = dot(v, g, (1, 1))
        inner = jnp.sum(dp * pf, axis=0, keepdims=True)
        ds = (pf * (dp - inner) * factor).astype(BF)
        gqkv[:, 2 * width + h * size : 2 * width + (h + 1) * size] = dot(p, g).astype(BF)
        gqkv[:, width + h * size : width + (h + 1) * size] = dot(ds, q).astype(BF)
        dqt[h * size : (h + 1) * size, :] = dot(k, ds, (0, 0)).astype(BF)
    gqkv[:, :width] = dqt[...].T
    normed_a, rstd_a = standard(xs[0].astype(F32))
    hid[...] = (normed_a * (1.0 + scale_a) + shift_a).astype(BF)
    total = None
    for j in range(3):
        cols = slice(j * width, (j + 1) * width)
        keep_front(j, dot(hid[...], gqkv[:, cols], (0, 0)).astype(BF))
        part = dot(gqkv[:, cols], weight(j), (1, 1))
        total = part if total is None else total + part
    gha = total
    copies = [
        pltpu.make_async_copy(halves.at[1], sent, sems.at[1]),
        pltpu.make_async_copy(halves.at[0], kept, sems.at[0]),
    ]
    for copy in copies:
        copy.start()
    vec[0:1] = jnp.sum(gha, 0, keepdims=True)
    vec[1:2] = jnp.sum(gha * normed_a, 0, keepdims=True)
    grad_in[0] = (gsum[...] + standard_back(gha * (1.0 + scale_a), normed_a, rstd_a)).astype(BF)
    for copy in copies:
        copy.wait()


def backward(layer, ids, grad, mods, w, saved):
    _, seq, width = grad.shape
    rows = width // SHARDS

    def at_layer(a):
        return pl.BlockSpec((1,) + a.shape[1:], lambda i: (layer,) + (0,) * (a.ndim - 1))

    def full(*shape):
        return pl.BlockSpec(shape, lambda i: (0,) * len(shape))

    half = (SHARDS // 2, BLOCKS, rows, width)
    hbm = pl.BlockSpec(memory_space=pl.ANY)
    return pl.pallas_call(
        functools.partial(backward_kernel, layer),
        grid=(1,),
        in_specs=[pl.BlockSpec(memory_space=pltpu.SMEM), full(1, seq, width), full(*mods.shape), at_layer(w)]
        + [at_layer(a) for a in saved],
        out_specs=[full(1, seq, width), hbm, hbm, full(12, width)],
        out_shape=[
            jax.ShapeDtypeStruct((1, seq, width), BF),
            jax.ShapeDtypeStruct(half, BF),
            jax.ShapeDtypeStruct(half, BF),
            jax.ShapeDtypeStruct((12, width), F32),
        ],
        scratch_shapes=[
            pltpu.VMEM((seq, width), BF),
            pltpu.VMEM((seq, width), BF),
            pltpu.VMEM((seq, width), F32),
            pltpu.VMEM((seq, width), BF),
            pltpu.VMEM((seq, 3 * width), BF),
            pltpu.VMEM((width, seq), BF),
            pltpu.VMEM((2,) + half, BF),
            pltpu.SemaphoreType.DMA((2,)),
        ],
        compiler_params=pltpu.CompilerParams(vmem_limit_bytes=VMEM_LIMIT),
        cost_estimate=pl.CostEstimate(
            flops=3_480_000_000, bytes_accessed=20_000_000, transcendentals=0
        ),
        name=f"backward_{layer}",
    )(ids, grad, mods, w, *saved)


def embed_lead(steps, width):
    half = width // 2
    freq = jnp.exp(-math.log(10000.0) * jnp.arange(half, dtype=F32) / half)
    angle = 6.0 * steps.astype(F32)[:, None] * freq[None, :]
    return jnp.concatenate([jnp.sin(angle), jnp.cos(angle)], -1)


def over_core(value):
    return lax.ppermute(value, "batch", [(i, i ^ 1) for i in range(8)])


def over_z(value, away):
    return lax.ppermute(value, "batch", [(i, i ^ (2 * away)) for i in range(8)])


def over_section(value, away):
    return lax.ppermute(value, "section", [(i, i ^ away) for i in range(4)])


def after(value, *others):
    return lax.optimization_barrier((value,) + others)[0]


def gather_shards(w):
    x0, y0, z1 = over_section(w, 1), over_section(w, 2), over_z(w, 1)
    z2 = over_z(w, 2)
    x1, y1 = over_section(z1, 1), over_section(z1, 2)
    z3 = over_z(after(w, z1), 3)
    p0 = over_section(after(y0, z1)[:6], 1)
    q0 = over_section(after(x0, z1)[6:], 2)
    x2, y2 = over_section(after(z2, x1), 1), over_section(after(z2, y1), 2)
    p1, q1 = over_section(y1[:6], 1), over_section(x1[6:], 2)
    x3, y3 = over_section(after(z3, x2), 1), over_section(after(z3, y2), 2)
    p2, q2 = over_section(y2[:6], 1), over_section(x2[6:], 2)
    p3, q3 = over_section(y3[:6], 1), over_section(x3[6:], 2)
    names = {}
    for zx, group in enumerate(
        [(w, x0, y0, p0, q0), (z1, x1, y1, p1, q1), (z2, x2, y2, p2, q2), (z3, x3, y3, p3, q3)]
    ):
        names[0, zx], names[1, zx], names[2, zx] = [(group[0], 0)], [(group[1], 0)], [(group[2], 0)]
        names[3, zx] = [(group[3], 0), (group[4], 6)]
    sources, plan = [], {}
    for keys in (
        [(0, 0), (0, 1), (1, 0), (2, 0), (1, 1), (2, 1), (3, 0)],
        [(0, 2), (0, 3), (3, 1), (1, 2), (2, 2)],
        [(1, 3), (2, 3), (3, 2), (3, 3)],
    ):
        bundle = []
        for key in keys:
            plan[key + (0,)], plan[key + (1,)] = [], []
            for array, low in names[key]:
                plan[key + (0,)].append((len(sources), low, 0))
                sources.append(array)
                bundle.append((key, array, low))
        other = over_core(jnp.concatenate([array for _, array, _ in bundle]))
        start = 0
        for key, array, low in bundle:
            plan[key + (1,)].append((len(sources), low, start))
            start += array.shape[0]
        sources.append(other)
    sizes = {}
    final = {}
    for key, parts in plan.items():
        final[key] = []
        for index, low, start in parts:
            high = BLOCKS if key[0] != 3 else low + 6
            final[key].append((index, start, low, high))
    return final, sources


def sum_shards(parts):
    def add(*values):
        total = values[0].astype(F32)
        for value in values[1:]:
            total = total + value.astype(F32)
        return total

    stage = None
    received = []
    own = None
    p, q = {}, {}

    def corners(zx, gate):
        p[zx] = over_section(after(parts[3, zx][:6], *gate), 1)
        q[zx] = over_section(after(parts[3, zx][6:], *gate), 2)

    corners(3, ())
    corners(2, ())
    gate = ()
    for zx in (3, 2, 1, 0):
        left = parts[1, zx]
        left = jnp.concatenate([left[:6], add(left[6:], q[zx]).astype(BF)])
        right = parts[2, zx]
        right = jnp.concatenate([add(right[:6], p[zx]).astype(BF), right[6:]])
        x, y = over_section(after(left, *gate), 1), over_section(after(right, *gate), 2)
        if zx >= 2:
            corners(zx - 2, (p[zx], q[zx]) + gate)
        total = add(parts[0, zx], x, y)
        gate = (x, y)
        if zx:
            received.append(over_z(total.astype(BF), zx))
        else:
            own = total
    return add(own, *received)


def gather_small(row):
    cores = jnp.stack([row, over_core(row)])
    places = jnp.stack([cores] + [over_z(cores, i) for i in (1, 2, 3)])
    return jnp.stack([places] + [over_section(places, i) for i in (1, 2, 3)])


def body_permuted(
    tokens, levels, lead, w_qkv, w_o, b_o, w_up, b_up, w_down, b_down, w_ada, b_ada, cotangent
):
    section, batch = lax.axis_index("section"), lax.axis_index("batch")
    place, core = batch // 2, batch % 2
    width = tokens.shape[2]
    rows = width // SHARDS
    ids = jnp.stack([section, place, core, levels[0]]).astype(jnp.int32)
    plan, sources = gather_shards(local_shard(w_qkv, w_o, w_up, w_down))

    small = jnp.concatenate([b_o[0], b_up[0], b_down[0], lead.astype(BF)])
    small = jnp.pad(small, (0, width - small.shape[0]))
    smalls = gather_small(small)
    leads = smalls[..., 6 * rows].reshape(-1)
    order = jnp.arange(SHARDS) ^ batch
    smalls = jnp.take(smalls.reshape(4, SHARDS, width), order, axis=1).astype(F32)
    biases = jnp.stack(
        [smalls[:, :, :rows].reshape(4, width)]
        + [
            smalls[:, 2 * j : 2 * j + 2, rows : 5 * rows].reshape(4, width)
            for j in range(4)
        ]
        + [smalls[:, :, 5 * rows : 6 * rows].reshape(4, width)],
        axis=1,
    )
    conds = jax.nn.silu(embed_lead(leads, width))
    mine = lax.dynamic_slice_in_dim(conds, batch * rows, rows, axis=1)
    part = jnp.dot(mine, w_ada[0].astype(F32), precision=HIGH)
    bias = jnp.zeros((6 * width,), F32)
    bias = lax.dynamic_update_slice_in_dim(
        bias, b_ada[0].astype(F32), batch * 6 * rows, axis=0
    )
    part = (part + bias).reshape(4, 4, 2, 6 * width)
    part = part[:, :, 0] + over_core(part[:, :, 1])
    part = part[:, 0] + over_z(part[:, 1], 1) + over_z(part[:, 2], 2) + over_z(part[:, 3], 3)
    mods = jnp.stack([part[0]] + [over_section(part[i], i) for i in (1, 2, 3)])
    mods = mods.reshape(4, 6, width)

    result, w, *saved = forward(plan, sources, ids, tokens, mods, biases)
    grad = cotangent
    sums = jnp.zeros((4, 4, BLOCKS, rows, width), BF)
    vecs = [None] * 4
    for layer in reversed(range(4)):
        grad, kept, sent, vecs[layer] = backward(layer, ids, grad, mods, w, saved)
        both = (kept.astype(F32) + over_core(sent).astype(F32)).astype(BF)
        sums = lax.dynamic_update_index_in_dim(sums, both, section ^ layer, 0)
    total = sum_shards({(i, j): sums[i, j] for i in range(4) for j in range(4)})

    vec = jnp.take(jnp.stack(vecs), jnp.arange(4) ^ section, axis=0)
    vec = jnp.stack([vec[0]] + [over_section(vec[i], i) for i in (1, 2, 3)])
    vec = jnp.stack([vec] + [over_z(vec, i) for i in (1, 2, 3)], axis=1)
    vec = jnp.stack([vec, over_core(vec)], axis=2).reshape(32, 12, width)
    g_ada = jnp.dot(mine.T, vec[:, :6].reshape(32, 6 * width), precision=HIGH)[None]
    flat = jnp.sum(vec, 0)

    def slot(low, high, count):
        return lax.dynamic_slice_in_dim(
            flat[low:high].reshape(-1), batch * count, count, axis=0
        )[None]

    return (
        result,
        grad,
        jnp.concatenate([total[0], total[1], total[2]], axis=1)[None],
        total[3][None],
        slot(6, 7, rows),
        jnp.concatenate([total[4 + j] for j in range(4)], axis=1)[None],
        slot(7, 11, 4 * rows),
        total[8:].reshape(1, 4 * rows, width),
        slot(11, 12, rows),
        g_ada,
        slot(0, 6, 6 * rows),
    )


def local_shard(w_qkv, w_o, w_up, w_down):
    _, rows, width = w_o.shape

    def blocks_of(piece):
        return jnp.stack(jnp.split(piece, piece.shape[1] // width, axis=1))

    return jnp.concatenate(
        [blocks_of(w_qkv[0]), w_o, blocks_of(w_up[0]), w_down[0].reshape(4, rows, width)]
    )


BOTH = ("section", "batch")


def body_general(
    tokens, levels, lead, w_qkv, w_o, b_o, w_up, b_up, w_down, b_down, w_ada, b_ada, cotangent
):
    batch = lax.axis_index("batch")
    sections, batches = lax.axis_size("section"), lax.axis_size("batch")
    width = tokens.shape[2]
    rows, tall = width // batches, width // SHARDS
    zero = jnp.zeros((), jnp.int32)
    ids = jnp.stack([zero, zero, zero, levels[0]])

    shards = lax.all_gather(local_shard(w_qkv, w_o, w_up, w_down), BOTH, axis=0, tiled=False)
    shards = shards.reshape(sections, batches, BLOCKS, rows, width)
    front = jnp.swapaxes(shards[:, :, :8], 1, 2).reshape(sections, 8, SHARDS, tall, width)
    downs = shards[:, :, 8:].reshape(sections, SHARDS, 4, tall, width)
    source = jnp.concatenate([jnp.swapaxes(front, 1, 2), downs], axis=2)
    source = source.reshape(sections * SHARDS * BLOCKS, tall, width)
    plan = {
        (l, z, c): [(0, ((l * 4 + z) * 2 + c) * BLOCKS, 0, BLOCKS)]
        for l in range(4)
        for z in range(4)
        for c in range(2)
    }
    small = jnp.concatenate([b_o[0], b_up[0], b_down[0]])
    smalls = lax.all_gather(small, BOTH, axis=0, tiled=False).reshape(sections, batches, -1)
    smalls = smalls.astype(F32)
    biases = jnp.concatenate(
        [
            smalls[:, :, :rows].reshape(sections, 1, width),
            smalls[:, :, rows : 5 * rows].reshape(sections, 4, width),
            smalls[:, :, 5 * rows :].reshape(sections, 1, width),
        ],
        axis=1,
    )
    leads = lax.all_gather(lead, BOTH, axis=0, tiled=True)
    conds = jax.nn.silu(embed_lead(leads, width))
    mine = lax.dynamic_slice_in_dim(conds, batch * rows, rows, axis=1)
    part = jnp.dot(mine, w_ada[0].astype(F32), precision=HIGH)
    bias = jnp.zeros((6 * width,), F32)
    bias = lax.dynamic_update_slice_in_dim(
        bias, b_ada[0].astype(F32), batch * 6 * rows, axis=0
    )
    part = (part + bias).reshape(sections, batches, 6 * width)
    part = lax.psum_scatter(part, "batch", scatter_dimension=1, tiled=True)
    mods = lax.all_to_all(part[:, 0], "section", 0, 0, tiled=True)
    mods = mods.reshape(sections, 6, width)

    result, w, *saved = forward(plan, [source], ids, tokens, mods, biases)
    grad = cotangent
    grads, vecs = [None] * sections, [None] * sections
    for layer in reversed(range(sections)):
        grad, kept, sent, vecs[layer] = backward(layer, ids, grad, mods, w, saved)
        grads[layer] = jnp.stack([kept, sent], axis=1).reshape(SHARDS, BLOCKS, tall, width)
    grads = jnp.stack(grads)
    front = jnp.swapaxes(grads[:, :, :8], 1, 2).reshape(sections, 8, batches, rows, width)
    downs = grads[:, :, 8:].reshape(sections, batches, 4, rows, width)
    total = jnp.concatenate([jnp.swapaxes(front, 1, 2), downs], axis=2)
    total = total.reshape(sections, batches, BLOCKS * rows, width)
    total = lax.psum_scatter(total, "section", scatter_dimension=0, tiled=True)
    total = lax.psum_scatter(total, "batch", scatter_dimension=1, tiled=True)
    total = total.astype(F32).reshape(BLOCKS, rows, width)

    vec = lax.all_to_all(jnp.stack(vecs), "section", 0, 0, tiled=True)
    vec = lax.all_gather(vec, "batch", axis=1, tiled=False)
    vec = vec.reshape(sections * batches, 12, width)
    g_ada = jnp.dot(mine.T, vec[:, :6].reshape(-1, 6 * width), precision=HIGH)[None]
    flat = jnp.sum(vec, 0)

    def slot(low, high, count):
        return lax.dynamic_slice_in_dim(
            flat[low:high].reshape(-1), batch * count, count, axis=0
        )[None]

    return (
        result,
        grad,
        jnp.concatenate([total[0], total[1], total[2]], axis=1)[None],
        total[3][None],
        slot(6, 7, rows),
        jnp.concatenate([total[4 + j] for j in range(4)], axis=1)[None],
        slot(7, 11, 4 * rows),
        total[8:].reshape(1, 4 * rows, width),
        slot(11, 12, rows),
        g_ada,
        slot(0, 6, 6 * rows),
    )


def solution(mesh):
    in_specs = (
        P(("section", "batch"), None, None),
        P(("section", "batch")),
        P(("section", "batch")),
        P("section", "batch", None),
        P("section", "batch", None),
        P("section", "batch"),
        P("section", "batch", None),
        P("section", "batch"),
        P("section", "batch", None),
        P("section", "batch"),
        P("section", "batch", None),
        P("section", "batch"),
        P(("section", "batch"), None, None),
    )
    out_specs = (
        P(("section", "batch"), None, None),
        P(("section", "batch"), None, None),
        P("section", "batch", None),
        P("section", "batch", None),
        P("section", "batch"),
        P("section", "batch", None),
        P("section", "batch"),
        P("section", "batch", None),
        P("section", "batch"),
        P("section", "batch", None),
        P("section", "batch"),
    )
    permuted = mesh.shape["section"] == 4 and mesh.shape["batch"] == SHARDS
    body = body_permuted if permuted else body_general
    return jax.shard_map(body, mesh=mesh, in_specs=in_specs, out_specs=out_specs, check_vma=False)
```

```python
import functools
import math

import jax
import jax.numpy as jnp
from jax import lax
from jax.experimental import pallas as pl
from jax.experimental.pallas import tpu as pltpu
from jax.sharding import PartitionSpec as P

HEADS = 6
LEVELS = 13
BLOCKS = 12
SHARDS = 8
EPS = 1e-06
NEG = -1e30
BF = jnp.bfloat16
F32 = jnp.float32
HIGH = lax.Precision.HIGHEST
BOTH = ("section", "batch")
C0 = math.sqrt(2.0 / math.pi)
C1 = 0.044715
VMEM_LIMIT = 60 * 2**20


def dot(left, right, over=(1, 0)):
    return lax.dot_general(
        left, right, (((over[0],), (over[1],)), ((), ())), preferred_element_type=F32
    )


def standard(value):
    centered = value - jnp.mean(value, -1, keepdims=True)
    rstd = lax.rsqrt(jnp.mean(centered * centered, -1, keepdims=True) + EPS)
    return centered * rstd, rstd


def standard_back(grad, normed, rstd):
    return rstd * (
        grad
        - jnp.mean(grad, -1, keepdims=True)
        - normed * jnp.mean(grad * normed, -1, keepdims=True)
    )


def forward_kernel(plan, ids, tokens, mods, biases, *refs):
    count = len({part[0] for parts in plan.values() for part in parts})
    sources, refs = refs[:count], refs[count:]
    result, w_out, xs, qkv, probs, mixed, branch_a, act, slope, branch_b = refs[:10]
    value, hidden, acc, w, in_sem, out_sem = refs[10:]
    layer = pl.program_id(0)
    layers = pl.num_programs(0)
    seq, width = value.shape
    size = width // HEADS
    section, place, core = ids[0], ids[1], ids[2]

    @pl.when(layer == 0)
    def _():
        value[...] = tokens[0]

        @pl.loop(0, layers)
        def _(target):
            for away in range(4):

                @pl.when(jnp.bitwise_xor(section, target) == away)
                def _():
                    for (sx, zx, cx), parts in plan.items():
                        if sx != away:
                            continue
                        shard = 2 * jnp.bitwise_xor(place, zx) + jnp.bitwise_xor(core, cx)
                        for index, lead, low, high in parts:
                            ref = sources[index]
                            top = min(high, 8)
                            if low < top:
                                pltpu.make_async_copy(
                                    ref.at[pl.ds(lead, top - low)],
                                    w.at[target, pl.ds(low, top - low), shard],
                                    in_sem.at[target],
                                ).start()
                            if high > 8:
                                pltpu.make_async_copy(
                                    ref.at[pl.ds(lead + 8 - low, 4)],
                                    w.at[target, 8 + shard // 2, pl.ds(4 * (shard % 2), 4)],
                                    in_sem.at[target],
                                ).start()

    pltpu.make_async_copy(w.at[layer], w.at[layer], in_sem.at[layer]).wait()
    pltpu.make_async_copy(w.at[layer], w_out.at[layer], out_sem.at[layer]).start()

    def weight(j):
        return w[layer, j].reshape(width, width)

    mod = mods[layer]
    bias = biases[layer]
    xs[0] = value[...]
    x = value[...].astype(F32)
    normed, _ = standard(x)
    hidden[...] = (normed * (1.0 + mod[1:2]) + mod[0:1]).astype(BF)
    for j in range(3):
        qkv[0, :, j * width : (j + 1) * width] = dot(hidden[...], weight(j)).astype(BF)
    limit = ids[3] * (seq // LEVELS)
    row = lax.broadcasted_iota(jnp.int32, (seq, 1), 0)
    mask = jnp.where(row < limit, 0.0, NEG)
    for h in range(HEADS):
        q = qkv[0, :, h * size : (h + 1) * size] * (size**-0.5)
        k = qkv[0, :, width + h * size : width + (h + 1) * size]
        v = qkv[0, :, 2 * width + h * size : 2 * width + (h + 1) * size]
        raw = dot(k, q, (1, 1)) + mask
        top = jnp.max(raw, axis=0, keepdims=True)
        e = jnp.exp(raw - top)
        p = (e * (1.0 / jnp.sum(e, axis=0, keepdims=True))).astype(BF)
        probs[0, h] = p
        mixed[0, h * size : (h + 1) * size, :] = dot(v, p, (0, 0)).astype(BF)
    ba = dot(mixed[0], weight(3), (0, 0)) + bias[0:1]
    branch_a[0] = ba
    middle = value[...].astype(F32) + mod[2:3] * ba
    acc[...] = middle
    normed, _ = standard(middle)
    hidden[...] = (normed * (1.0 + mod[4:5]) + mod[3:4]).astype(BF)
    down = None
    for j in range(4):
        cols = slice(j * width, (j + 1) * width)
        pre = dot(hidden[...], weight(4 + j)) + bias[1 + j : 2 + j]
        square = pre * pre
        t = jnp.tanh(pre * (C0 + (C0 * C1) * square))
        half = 0.5 + 0.5 * t
        a = pre * half
        slope[0, :, cols] = (half + a * (1.0 - t) * (C0 + (3.0 * C0 * C1) * square)).astype(BF)
        act[0, :, cols] = a.astype(BF)
        part = dot(act[0, :, cols], weight(8 + j))
        down = part if down is None else down + part
    bb = down + bias[5:6]
    branch_b[0] = bb.astype(BF)
    out = (acc[...] + mod[5:6] * bb).astype(BF)
    value[...] = out
    result[0] = out

    @pl.when(layer == layers - 1)
    def _():
        @pl.loop(0, layers)
        def _(target):
            pltpu.make_async_copy(w.at[target], w_out.at[target], out_sem.at[target]).wait()


def forward(plan, sources, ids, tokens, mods, biases):
    layers = mods.shape[0]
    _, seq, width = tokens.shape
    rows = width // SHARDS

    def per_layer(*shape):
        return pl.BlockSpec((1,) + shape, lambda l: (l,) + (0,) * len(shape))

    def same(*shape):
        return pl.BlockSpec(shape, lambda l: (0,) * len(shape))

    shapes = [
        ((seq, width), BF),
        ((seq, 3 * width), BF),
        ((HEADS, seq, seq), BF),
        ((width, seq), BF),
        ((seq, width), F32),
        ((seq, 4 * width), BF),
        ((seq, 4 * width), BF),
        ((seq, width), BF),
    ]
    hbm = pl.BlockSpec(memory_space=pl.ANY)
    return pl.pallas_call(
        functools.partial(forward_kernel, plan),
        grid=(layers,),
        in_specs=[
            pl.BlockSpec(memory_space=pltpu.SMEM),
            same(1, seq, width),
            same(layers, 6, width),
            same(layers, 6, width),
        ]
        + [hbm] * len(sources),
        out_specs=[same(1, seq, width), hbm] + [per_layer(*s) for s, _ in shapes],
        out_shape=[
            jax.ShapeDtypeStruct((1, seq, width), BF),
            jax.ShapeDtypeStruct((layers, BLOCKS, SHARDS, rows, width), BF),
        ]
        + [jax.ShapeDtypeStruct((layers,) + s, d) for s, d in shapes],
        scratch_shapes=[
            pltpu.VMEM((seq, width), BF),
            pltpu.VMEM((seq, width), BF),
            pltpu.VMEM((seq, width), F32),
            pltpu.VMEM((layers, BLOCKS, SHARDS, rows, width), BF),
            pltpu.SemaphoreType.DMA((layers,)),
            pltpu.SemaphoreType.DMA((layers,)),
        ],
        compiler_params=pltpu.CompilerParams(vmem_limit_bytes=VMEM_LIMIT),
        cost_estimate=pl.CostEstimate(
            flops=layers * 1_740_000_000, bytes_accessed=80_000_000, transcendentals=0
        ),
        name="forward",
    )(ids, tokens, mods, biases, *sources)


def backward_kernel(
    layer, ids, grad, mods, w, xs, qkv, probs, mixed, branch_a, act, slope, branch_b,
    grad_in, kept, sent, vec, gbb, hid, gsum, gmix, gqkv, dqt, halves, sems,
):
    seq, width = gbb.shape
    size = width // HEADS
    place, core = ids[1], ids[2]
    rows = width // SHARDS

    def weight(j):
        return w[0, j].reshape(width, width)

    def keep(shard, block, value):
        half = jnp.bitwise_xor(core, shard % 2)
        halves[half, jnp.bitwise_xor(place, shard // 2), block] = value

    def keep_front(block, value):
        for shard in range(SHARDS):
            keep(shard, block, value[shard * rows : (shard + 1) * rows])

    def keep_down(j, value):
        for part in range(SHARDS):
            keep(2 * j + part // 4, 8 + part % 4, value[part * rows : (part + 1) * rows])

    mod = mods[layer]
    shift_a, scale_a, gate_a, shift_b, scale_b, gate_b = (mod[i : i + 1] for i in range(6))
    gout = grad[0].astype(F32)
    vec[5:6] = jnp.sum(gout * branch_b[0].astype(F32), 0, keepdims=True)
    gb = (gout * gate_b).astype(BF)
    gbb[...] = gb
    vec[11:12] = jnp.sum(gb.astype(F32), 0, keepdims=True)
    x = xs[0].astype(F32)
    middle = x + gate_a * branch_a[0]
    normed_b, rstd_b = standard(middle)
    hid[...] = (normed_b * (1.0 + scale_b) + shift_b).astype(BF)
    total = None
    for j in range(4):
        cols = slice(j * width, (j + 1) * width)
        keep_down(j, dot(act[0, :, cols], gbb[...], (0, 0)).astype(BF))
        gact = dot(gbb[...], weight(8 + j), (1, 1))
        gpre = (gact * slope[0, :, cols].astype(F32)).astype(BF)
        vec[7 + j : 8 + j] = jnp.sum(gpre.astype(F32), 0, keepdims=True)
        keep_front(4 + j, dot(hid[...], gpre, (0, 0)).astype(BF))
        part = dot(gpre, weight(4 + j), (1, 1))
        total = part if total is None else total + part
    ghb = total
    vec[3:4] = jnp.sum(ghb, 0, keepdims=True)
    vec[4:5] = jnp.sum(ghb * normed_b, 0, keepdims=True)
    gmid = gout + standard_back(ghb * (1.0 + scale_b), normed_b, rstd_b)
    gsum[...] = gmid
    vec[2:3] = jnp.sum(gmid * branch_a[0], 0, keepdims=True)
    gba = (gmid * gate_a).astype(BF)
    gbb[...] = gba
    vec[6:7] = jnp.sum(gba.astype(F32), 0, keepdims=True)
    keep_front(3, dot(mixed[0], gbb[...]).astype(BF))
    gmix[...] = dot(gbb[...], weight(3), (1, 1)).astype(BF)
    factor = size ** -0.5
    for h in range(HEADS):
        q = qkv[0, :, h * size : (h + 1) * size]
        k = qkv[0, :, width + h * size : width + (h + 1) * size]
        v = qkv[0, :, 2 * width + h * size : 2 * width + (h + 1) * size]
        g = gmix[:, h * size : (h + 1) * size]
        p = probs[0, h]
        pf = p.astype(F32)
        dp = dot(v, g, (1, 1))
        inner = jnp.sum(dp * pf, axis=0, keepdims=True)
        ds = (pf * (dp - inner) * factor).astype(BF)
        gqkv[:, 2 * width + h * size : 2 * width + (h + 1) * size] = dot(p, g).astype(BF)
        gqkv[:, width + h * size : width + (h + 1) * size] = dot(ds, q).astype(BF)
        dqt[h * size : (h + 1) * size, :] = dot(k, ds, (0, 0)).astype(BF)
    gqkv[:, :width] = dqt[...].T
    normed_a, rstd_a = standard(xs[0].astype(F32))
    hid[...] = (normed_a * (1.0 + scale_a) + shift_a).astype(BF)
    total = None
    for j in range(3):
        cols = slice(j * width, (j + 1) * width)
        keep_front(j, dot(hid[...], gqkv[:, cols], (0, 0)).astype(BF))
        part = dot(gqkv[:, cols], weight(j), (1, 1))
        total = part if total is None else total + part
    gha = total
    copies = [
        pltpu.make_async_copy(halves.at[1], sent, sems.at[1]),
        pltpu.make_async_copy(halves.at[0], kept, sems.at[0]),
    ]
    for copy in copies:
        copy.start()
    vec[0:1] = jnp.sum(gha, 0, keepdims=True)
    vec[1:2] = jnp.sum(gha * normed_a, 0, keepdims=True)
    grad_in[0] = (gsum[...] + standard_back(gha * (1.0 + scale_a), normed_a, rstd_a)).astype(BF)
    for copy in copies:
        copy.wait()


def backward(layer, ids, grad, mods, w, saved):
    _, seq, width = grad.shape
    rows = width // SHARDS

    def at_layer(a):
        return pl.BlockSpec((1,) + a.shape[1:], lambda i: (layer,) + (0,) * (a.ndim - 1))

    def full(*shape):
        return pl.BlockSpec(shape, lambda i: (0,) * len(shape))

    half = (SHARDS // 2, BLOCKS, rows, width)
    hbm = pl.BlockSpec(memory_space=pl.ANY)
    return pl.pallas_call(
        functools.partial(backward_kernel, layer),
        grid=(1,),
        in_specs=[pl.BlockSpec(memory_space=pltpu.SMEM), full(1, seq, width), full(*mods.shape), at_layer(w)]
        + [at_layer(a) for a in saved],
        out_specs=[full(1, seq, width), hbm, hbm, full(12, width)],
        out_shape=[
            jax.ShapeDtypeStruct((1, seq, width), BF),
            jax.ShapeDtypeStruct(half, BF),
            jax.ShapeDtypeStruct(half, BF),
            jax.ShapeDtypeStruct((12, width), F32),
        ],
        scratch_shapes=[
            pltpu.VMEM((seq, width), BF),
            pltpu.VMEM((seq, width), BF),
            pltpu.VMEM((seq, width), F32),
            pltpu.VMEM((seq, width), BF),
            pltpu.VMEM((seq, 3 * width), BF),
            pltpu.VMEM((width, seq), BF),
            pltpu.VMEM((2,) + half, BF),
            pltpu.SemaphoreType.DMA((2,)),
        ],
        compiler_params=pltpu.CompilerParams(vmem_limit_bytes=VMEM_LIMIT),
        cost_estimate=pl.CostEstimate(
            flops=3_480_000_000, bytes_accessed=20_000_000, transcendentals=0
        ),
        name=f"backward_{layer}",
    )(ids, grad, mods, w, *saved)


def embed_lead(steps, width):
    half = width // 2
    freq = jnp.exp(-math.log(10000.0) * jnp.arange(half, dtype=F32) / half)
    angle = 6.0 * steps.astype(F32)[:, None] * freq[None, :]
    return jnp.concatenate([jnp.sin(angle), jnp.cos(angle)], -1)


def over_core(value):
    return lax.ppermute(value, "batch", [(i, i ^ 1) for i in range(8)])


def over_z(value, away):
    return lax.ppermute(value, "batch", [(i, i ^ (2 * away)) for i in range(8)])


def over_section(value, away):
    return lax.ppermute(value, "section", [(i, i ^ away) for i in range(4)])


def after(value, *others):
    return lax.optimization_barrier((value,) + others)[0]


def gather_shards(w, small, exchange):
    x0, y0, z1 = over_section(w, 1), over_section(w, 2), over_z(w, 1)
    z2 = over_z(w, 2)
    z1, small = lax.optimization_barrier((z1, small))
    small = lax.all_to_all(small, BOTH, 0, 0, tiled=True)
    x1, y1 = over_section(z1, 1), over_section(z1, 2)
    z3 = over_z(z2, 1)
    p0, q0 = over_section(y0[:6], 1), over_section(x0[6:], 2)
    x1, small = lax.optimization_barrier((x1, small))
    part = exchange(small)
    x2, y2 = over_section(z2, 1), over_section(z2, 2)
    p1, q1 = over_section(y1[:6], 1), over_section(x1[6:], 2)
    x3, y3 = over_section(z3, 1), over_section(z3, 2)
    p2, q2 = over_section(y2[:6], 1), over_section(x2[6:], 2)
    x3, part = lax.optimization_barrier((x3, part))
    p3, q3 = over_section(y3[:6], 1), over_section(x3[6:], 2)
    names = {}
    for zx, group in enumerate(
        [(w, x0, y0, p0, q0), (z1, x1, y1, p1, q1), (z2, x2, y2, p2, q2), (z3, x3, y3, p3, q3)]
    ):
        names[0, zx], names[1, zx], names[2, zx] = [(group[0], 0)], [(group[1], 0)], [(group[2], 0)]
        names[3, zx] = [(group[3], 0), (group[4], 6)]
    sources, plan = [], {}
    for keys in (
        [(0, 0), (0, 1), (1, 0), (2, 0), (1, 1), (2, 1), (3, 0)],
        [(0, 2), (0, 3), (3, 1), (1, 2), (2, 2)],
        [(1, 3), (2, 3), (3, 2), (3, 3)],
    ):
        bundle = []
        for key in keys:
            plan[key + (0,)], plan[key + (1,)] = [], []
            for array, low in names[key]:
                plan[key + (0,)].append((len(sources), low, 0))
                sources.append(array)
                bundle.append((key, array, low))
        other = over_core(jnp.concatenate([array for _, array, _ in bundle]))
        start = 0
        for key, array, low in bundle:
            plan[key + (1,)].append((len(sources), low, start))
            start += array.shape[0]
        sources.append(other)
    final = {}
    for key, parts in plan.items():
        final[key] = []
        for index, low, start in parts:
            high = BLOCKS if key[0] != 3 else low + 6
            final[key].append((index, start, low, high))
    return final, sources, small, part


def sum_shards(parts, vec):
    def add(*values):
        total = values[0].astype(F32)
        for value in values[1:]:
            total = total + value.astype(F32)
        return total

    def joined(zx, p, q):
        left = jnp.concatenate([parts[1, zx][:6], add(parts[1, zx][6:], q).astype(BF)])
        right = jnp.concatenate([add(parts[2, zx][:6], p).astype(BF), parts[2, zx][6:]])
        return left, right

    p3, q3 = over_section(parts[3, 3][:6], 1), over_section(parts[3, 3][6:], 2)
    d2, d1 = over_section(parts[3, 2], 1), over_section(parts[3, 1], 2)
    left, right = joined(3, p3, q3)
    x3, y3 = over_section(left, 1), over_section(right, 2)
    p0, q0 = over_section(parts[3, 0][:6], 1), over_section(parts[3, 0][6:], 2)
    left, right = parts[1, 2], add(parts[2, 2], d2).astype(BF)
    x3, vec = lax.optimization_barrier((x3, vec))
    vec = lax.all_to_all(vec, BOTH, 0, 0, tiled=True)
    total = add(parts[0, 3], x3, y3).astype(BF)
    left, right, total = lax.optimization_barrier((left, right, total))
    z3 = over_z(total, 1)
    x2, y2 = over_section(left, 1), over_section(right, 2)
    left, right = add(parts[1, 1], d1).astype(BF), parts[2, 1]
    total = add(parts[0, 2], x2, y2, z3).astype(BF)
    left, right, total = lax.optimization_barrier((left, right, total))
    z2, s2 = over_z(total[:6], 2), over_z(total[6:], 2)
    x1, y1 = over_section(left, 1), over_section(right, 2)
    left, right = joined(0, p0, q0)
    total = add(parts[0, 1], x1, y1).astype(BF)
    left, right, total, z2 = lax.optimization_barrier((left, right, total, z2))
    x0, y0 = over_section(left, 1), over_section(right, 2)
    z1 = over_z(total, 1)
    return unpacked(parts[0, 0], x0, y0, z1, z2, s2), vec


def body_permuted(
    tokens, levels, lead, w_qkv, w_o, b_o, w_up, b_up, w_down, b_down, w_ada, b_ada, cotangent
):
    section, batch = lax.axis_index("section"), lax.axis_index("batch")
    place, core = batch // 2, batch % 2
    width = tokens.shape[2]
    rows = width // SHARDS
    ids = jnp.stack([section, place, core, levels[0]]).astype(jnp.int32)
    shard, small = packed(lead, w_qkv, w_o, w_up, w_down, b_o, b_up, b_down)
    mine = []

    def exchange(smalls):
        conds = jax.nn.silu(embed_lead(smalls[:, 512], width))
        mine.append(lax.dynamic_slice_in_dim(conds, batch * rows, rows, axis=1))
        part = jnp.dot(mine[0], w_ada[0].astype(F32), precision=HIGH)
        bias = jnp.zeros((6 * width,), F32)
        bias = lax.dynamic_update_slice_in_dim(
            bias, b_ada[0].astype(F32), batch * 6 * rows, axis=0
        )
        return lax.all_to_all(part + bias, BOTH, 0, 0, tiled=True)

    plan, sources, smalls, part = gather_shards(shard, small, exchange)
    mine = mine[0]
    mods = jnp.sum(part.reshape(4, SHARDS, 6 * width), axis=1).reshape(4, 6, width)
    vectors = smalls.reshape(4, SHARDS, 640).astype(F32)
    biases = jnp.concatenate(
        [
            vectors[:, :, :rows].reshape(4, 1, width),
            vectors[:, :, 128 : 128 + 4 * rows].reshape(4, 4, width),
            vectors[:, :, 384 : 384 + rows].reshape(4, 1, width),
        ],
        axis=1,
    )
    result, w, *saved = forward(plan, sources, ids, tokens, mods, biases)
    grad = cotangent
    sums = jnp.zeros((4, 4, BLOCKS, rows, width), BF)
    vecs = [None] * 4
    for layer in reversed(range(4)):
        grad, kept, sent, vecs[layer] = backward(layer, ids, grad, mods, w, saved)
        both = (kept.astype(F32) + over_core(sent).astype(F32)).astype(BF)
        sums = lax.dynamic_update_index_in_dim(sums, both, section ^ layer, 0)
    vec = jnp.stack(vecs)[:, None].astype(BF)
    vec = jnp.broadcast_to(vec, (4, SHARDS) + vec.shape[2:]).reshape(32, 12 * width)
    totals, vec = sum_shards({(i, j): sums[i, j] for i in range(4) for j in range(4)}, vec)
    vec = vec.astype(F32).reshape(32, 12, width)
    g_ada = jnp.dot(mine.T, vec[:, :6].reshape(32, 6 * width), precision=HIGH)[None]
    flat = jnp.sum(vec, 0)

    def slot(low, high, count):
        return lax.dynamic_slice_in_dim(
            flat[low:high].reshape(-1), batch * count, count, axis=0
        )[None]

    return (
        result,
        grad,
        totals[0],
        totals[1],
        slot(6, 7, rows),
        totals[2],
        slot(7, 11, 4 * rows),
        totals[3],
        slot(11, 12, rows),
        g_ada,
        slot(0, 6, 6 * rows),
    )


def pack_kernel(lead, w_qkv, w_o, w_up, w_down, b_o, b_up, b_down, out, small):
    _, rows, width = w_o.shape
    for j in range(3):
        out[j] = w_qkv[0, :, j * width : (j + 1) * width]
    out[3] = w_o[0]
    for j in range(4):
        out[4 + j] = w_up[0, :, j * width : (j + 1) * width]
        out[8 + j] = w_down[0, j * rows : (j + 1) * rows]
    peers = small.shape[0]
    small[...] = jnp.full(small.shape, lead[0].astype(F32), F32).astype(BF)
    for start, bias in zip((0, 128, 384), (b_o, b_up, b_down)):
        count = bias.shape[1]
        small[:, start : start + count] = jnp.broadcast_to(
            bias[...].astype(F32), (peers, count)
        ).astype(BF)


def packed(lead, w_qkv, w_o, w_up, w_down, b_o, b_up, b_down):
    _, rows, width = w_o.shape
    vmem = pl.BlockSpec(memory_space=pltpu.VMEM)
    return pl.pallas_call(
        pack_kernel,
        in_specs=[pl.BlockSpec(memory_space=pltpu.SMEM)] + [vmem] * 7,
        out_shape=[
            jax.ShapeDtypeStruct((BLOCKS, rows, width), BF),
            jax.ShapeDtypeStruct((32, 640), BF),
        ],
        name="pack",
    )(lead, w_qkv, w_o, w_up, w_down, b_o, b_up, b_down)


def unpack_kernel(own, x, y, z, low, high, g_qkv, g_o, g_up, g_down):
    _, rows, width = g_o.shape
    for j in range(BLOCKS):
        last = low[j] if j < 6 else high[j - 6]
        total = own[j].astype(F32) + x[j].astype(F32) + y[j].astype(F32)
        total = total + z[j].astype(F32) + last.astype(F32)
        if j < 3:
            g_qkv[0, :, j * width : (j + 1) * width] = total
        elif j == 3:
            g_o[0] = total
        elif j < 8:
            g_up[0, :, (j - 4) * width : (j - 3) * width] = total
        else:
            g_down[0, (j - 8) * rows : (j - 7) * rows] = total


def unpacked(own, x, y, z, low, high):
    _, rows, width = own.shape
    return pl.pallas_call(
        unpack_kernel,
        out_shape=[
            jax.ShapeDtypeStruct((1, rows, 3 * width), F32),
            jax.ShapeDtypeStruct((1, rows, width), F32),
            jax.ShapeDtypeStruct((1, rows, 4 * width), F32),
            jax.ShapeDtypeStruct((1, 4 * rows, width), F32),
        ],
        name="unpack",
    )(own, x, y, z, low, high)


def local_shard(w_qkv, w_o, w_up, w_down):
    _, rows, width = w_o.shape

    def blocks_of(piece):
        return jnp.stack(jnp.split(piece, piece.shape[1] // width, axis=1))

    return jnp.concatenate(
        [blocks_of(w_qkv[0]), w_o, blocks_of(w_up[0]), w_down[0].reshape(4, rows, width)]
    )


def body_general(
    tokens, levels, lead, w_qkv, w_o, b_o, w_up, b_up, w_down, b_down, w_ada, b_ada, cotangent
):
    batch = lax.axis_index("batch")
    sections, batches = lax.axis_size("section"), lax.axis_size("batch")
    width = tokens.shape[2]
    rows, tall = width // batches, width // SHARDS
    zero = jnp.zeros((), jnp.int32)
    ids = jnp.stack([zero, zero, zero, levels[0]])

    shards = lax.all_gather(local_shard(w_qkv, w_o, w_up, w_down), BOTH, axis=0, tiled=False)
    shards = shards.reshape(sections, batches, BLOCKS, rows, width)
    front = jnp.swapaxes(shards[:, :, :8], 1, 2).reshape(sections, 8, SHARDS, tall, width)
    downs = shards[:, :, 8:].reshape(sections, SHARDS, 4, tall, width)
    source = jnp.concatenate([jnp.swapaxes(front, 1, 2), downs], axis=2)
    source = source.reshape(sections * SHARDS * BLOCKS, tall, width)
    plan = {
        (l, z, c): [(0, ((l * 4 + z) * 2 + c) * BLOCKS, 0, BLOCKS)]
        for l in range(4)
        for z in range(4)
        for c in range(2)
    }
    small = jnp.concatenate([b_o[0], b_up[0], b_down[0]])
    smalls = lax.all_gather(small, BOTH, axis=0, tiled=False).reshape(sections, batches, -1)
    smalls = smalls.astype(F32)
    biases = jnp.concatenate(
        [
            smalls[:, :, :rows].reshape(sections, 1, width),
            smalls[:, :, rows : 5 * rows].reshape(sections, 4, width),
            smalls[:, :, 5 * rows :].reshape(sections, 1, width),
        ],
        axis=1,
    )
    leads = lax.all_gather(lead, BOTH, axis=0, tiled=True)
    conds = jax.nn.silu(embed_lead(leads, width))
    mine = lax.dynamic_slice_in_dim(conds, batch * rows, rows, axis=1)
    part = jnp.dot(mine, w_ada[0].astype(F32), precision=HIGH)
    bias = jnp.zeros((6 * width,), F32)
    bias = lax.dynamic_update_slice_in_dim(
        bias, b_ada[0].astype(F32), batch * 6 * rows, axis=0
    )
    part = (part + bias).reshape(sections, batches, 6 * width)
    part = lax.psum_scatter(part, "batch", scatter_dimension=1, tiled=True)
    mods = lax.all_to_all(part[:, 0], "section", 0, 0, tiled=True)
    mods = mods.reshape(sections, 6, width)

    result, w, *saved = forward(plan, [source], ids, tokens, mods, biases)
    grad = cotangent
    grads, vecs = [None] * sections, [None] * sections
    for layer in reversed(range(sections)):
        grad, kept, sent, vecs[layer] = backward(layer, ids, grad, mods, w, saved)
        grads[layer] = jnp.stack([kept, sent], axis=1).reshape(SHARDS, BLOCKS, tall, width)
    grads = jnp.stack(grads)
    front = jnp.swapaxes(grads[:, :, :8], 1, 2).reshape(sections, 8, batches, rows, width)
    downs = grads[:, :, 8:].reshape(sections, batches, 4, rows, width)
    total = jnp.concatenate([jnp.swapaxes(front, 1, 2), downs], axis=2)
    total = total.reshape(sections, batches, BLOCKS * rows, width)
    total = lax.psum_scatter(total, "section", scatter_dimension=0, tiled=True)
    total = lax.psum_scatter(total, "batch", scatter_dimension=1, tiled=True)
    total = total.astype(F32).reshape(BLOCKS, rows, width)

    vec = lax.all_to_all(jnp.stack(vecs), "section", 0, 0, tiled=True)
    vec = lax.all_gather(vec, "batch", axis=1, tiled=False)
    vec = vec.reshape(sections * batches, 12, width)
    g_ada = jnp.dot(mine.T, vec[:, :6].reshape(-1, 6 * width), precision=HIGH)[None]
    flat = jnp.sum(vec, 0)

    def slot(low, high, count):
        return lax.dynamic_slice_in_dim(
            flat[low:high].reshape(-1), batch * count, count, axis=0
        )[None]

    return (
        result,
        grad,
        jnp.concatenate([total[0], total[1], total[2]], axis=1)[None],
        total[3][None],
        slot(6, 7, rows),
        jnp.concatenate([total[4 + j] for j in range(4)], axis=1)[None],
        slot(7, 11, 4 * rows),
        total[8:].reshape(1, 4 * rows, width),
        slot(11, 12, rows),
        g_ada,
        slot(0, 6, 6 * rows),
    )


def solution(mesh):
    in_specs = (
        P(("section", "batch"), None, None),
        P(("section", "batch")),
        P(("section", "batch")),
        P("section", "batch", None),
        P("section", "batch", None),
        P("section", "batch"),
        P("section", "batch", None),
        P("section", "batch"),
        P("section", "batch", None),
        P("section", "batch"),
        P("section", "batch", None),
        P("section", "batch"),
        P(("section", "batch"), None, None),
    )
    out_specs = (
        P(("section", "batch"), None, None),
        P(("section", "batch"), None, None),
        P("section", "batch", None),
        P("section", "batch", None),
        P("section", "batch"),
        P("section", "batch", None),
        P("section", "batch"),
        P("section", "batch", None),
        P("section", "batch"),
        P("section", "batch", None),
        P("section", "batch"),
    )
    permuted = mesh.shape["section"] == 4 and mesh.shape["batch"] == SHARDS
    body = body_permuted if permuted else body_general
    return jax.shard_map(body, mesh=mesh, in_specs=in_specs, out_specs=out_specs, check_vma=False)
```

```python
import functools
import math

import jax
import jax.numpy as jnp
from jax import lax
from jax.experimental import pallas as pl
from jax.experimental.pallas import tpu as pltpu
from jax.sharding import PartitionSpec as P

HEADS = 6
LEVELS = 13
BLOCKS = 12
SHARDS = 8
EPS = 1e-06
NEG = -1e30
BF = jnp.bfloat16
F32 = jnp.float32
HIGH = lax.Precision.HIGHEST
BOTH = ("section", "batch")
C0 = math.sqrt(2.0 / math.pi)
C1 = 0.044715
VMEM_LIMIT = 60 * 2**20


def dot(left, right, over=(1, 0)):
    return lax.dot_general(
        left, right, (((over[0],), (over[1],)), ((), ())), preferred_element_type=F32
    )


def standard(value):
    centered = value - jnp.mean(value, -1, keepdims=True)
    rstd = lax.rsqrt(jnp.mean(centered * centered, -1, keepdims=True) + EPS)
    return centered * rstd, rstd


def standard_back(grad, normed, rstd):
    return rstd * (
        grad
        - jnp.mean(grad, -1, keepdims=True)
        - normed * jnp.mean(grad * normed, -1, keepdims=True)
    )


def forward_kernel(plan, ids, tokens, mods, biases, *refs):
    count = len({part[0] for parts in plan.values() for part in parts})
    sources, refs = refs[:count], refs[count:]
    result, w_out, outs, held = refs[0], refs[1], refs[2:10], refs[10:18]
    value, hidden, acc, w, in_sem, out_sem, save_sem = refs[18:]
    layer = pl.program_id(0)
    layers = pl.num_programs(0)
    seq, width = value.shape
    size = width // HEADS
    section, place, core = ids[0], ids[1], ids[2]

    @pl.when(layer == 0)
    def _():
        value[...] = tokens[0]

        @pl.loop(0, layers)
        def _(target):
            for away in range(4):

                @pl.when(jnp.bitwise_xor(section, target) == away)
                def _():
                    for (sx, zx, cx), parts in plan.items():
                        if sx != away:
                            continue
                        shard = 2 * jnp.bitwise_xor(place, zx) + jnp.bitwise_xor(core, cx)
                        for index, lead, low, high in parts:
                            ref = sources[index]
                            top = min(high, 8)
                            if low < top:
                                pltpu.make_async_copy(
                                    ref.at[pl.ds(lead, top - low)],
                                    w.at[target, pl.ds(low, top - low), shard],
                                    in_sem.at[target],
                                ).start()
                            if high > 8:
                                pltpu.make_async_copy(
                                    ref.at[pl.ds(lead + 8 - low, 4)],
                                    w.at[target, 8 + shard // 2, pl.ds(4 * (shard % 2), 4)],
                                    in_sem.at[target],
                                ).start()

    pltpu.make_async_copy(w.at[layer], w.at[layer], in_sem.at[layer]).wait()
    pltpu.make_async_copy(w.at[layer], w_out.at[layer], out_sem.at[layer]).start()

    slot = layer % 2
    xs, qkv, probs, mixed, branch_a, act, slope, branch_b = (ref.at[slot] for ref in held)

    def saving(i, half, target):
        return pltpu.make_async_copy(held[i].at[half], outs[i].at[target], save_sem.at[i, half])

    def reuse(*which):
        @pl.when(layer >= 2)
        def _():
            for i in which:
                saving(i, slot, layer).wait()

    def save(*which):
        for i in which:
            saving(i, slot, layer).start()

    def weight(j):
        return w[layer, j].reshape(width, width)

    def weights(low, high):
        return jnp.concatenate([weight(j) for j in range(low, high)], axis=1)

    mod = mods[layer]
    bias = biases[layer]
    reuse(*range(8))
    xs[...] = value[...]
    save(0)
    x = value[...].astype(F32)
    normed, _ = standard(x)
    hidden[...] = (normed * (1.0 + mod[1:2]) + mod[0:1]).astype(BF)
    qkv[...] = dot(hidden[...], weights(0, 3)).astype(BF)
    save(1)
    limit = ids[3] * (seq // LEVELS)
    row = lax.broadcasted_iota(jnp.int32, (seq, 1), 0)
    mask = jnp.where(row < limit, 0.0, NEG)
    for h in range(HEADS):
        q = qkv[:, h * size : (h + 1) * size] * (size**-0.5)
        k = qkv[:, width + h * size : width + (h + 1) * size]
        v = qkv[:, 2 * width + h * size : 2 * width + (h + 1) * size]
        raw = dot(k, q, (1, 1)) + mask
        top = jnp.max(raw, axis=0, keepdims=True)
        e = jnp.exp(raw - top)
        p = (e * (1.0 / jnp.sum(e, axis=0, keepdims=True))).astype(BF)
        probs[h] = p
        mixed[h * size : (h + 1) * size, :] = dot(v, p, (0, 0)).astype(BF)
    save(2, 3)
    ba = dot(mixed[...], weight(3), (0, 0)) + bias[0:1]
    branch_a[...] = ba
    save(4)
    middle = value[...].astype(F32) + mod[2:3] * ba
    acc[...] = middle
    normed, _ = standard(middle)
    hidden[...] = (normed * (1.0 + mod[4:5]) + mod[3:4]).astype(BF)
    for j in range(0, 4, 2):
        cols = slice(j * width, (j + 2) * width)
        shift = jnp.concatenate([bias[1 + i : 2 + i] for i in range(j, j + 2)], axis=1)
        pre = dot(hidden[...], weights(4 + j, 4 + j + 2)) + shift
        square = pre * pre
        t = jnp.tanh(pre * (C0 + (C0 * C1) * square))
        half = 0.5 + 0.5 * t
        a = pre * half
        slope[:, cols] = (half + a * (1.0 - t) * (C0 + (3.0 * C0 * C1) * square)).astype(BF)
        act[:, cols] = a.astype(BF)
    save(5, 6)
    bb = dot(act[...], w[layer, 8:12].reshape(4 * width, width)) + bias[5:6]
    branch_b[...] = bb.astype(BF)
    save(7)
    out = (acc[...] + mod[5:6] * bb).astype(BF)
    value[...] = out
    result[0] = out

    @pl.when(layer == layers - 1)
    def _():
        for i in range(8):
            for half in range(2):
                saving(i, half, layer).wait()

        @pl.loop(0, layers)
        def _(target):
            pltpu.make_async_copy(w.at[target], w_out.at[target], out_sem.at[target]).wait()


def forward(plan, sources, ids, tokens, mods, biases):
    layers = mods.shape[0]
    _, seq, width = tokens.shape
    rows = width // SHARDS

    def same(*shape):
        return pl.BlockSpec(shape, lambda l: (0,) * len(shape))

    shapes = [
        ((seq, width), BF),
        ((seq, 3 * width), BF),
        ((HEADS, seq, seq), BF),
        ((width, seq), BF),
        ((seq, width), F32),
        ((seq, 4 * width), BF),
        ((seq, 4 * width), BF),
        ((seq, width), BF),
    ]
    hbm = pl.BlockSpec(memory_space=pl.ANY)
    return pl.pallas_call(
        functools.partial(forward_kernel, plan),
        grid=(layers,),
        in_specs=[
            pl.BlockSpec(memory_space=pltpu.SMEM),
            same(1, seq, width),
            same(layers, 6, width),
            same(layers, 6, width),
        ]
        + [hbm] * len(sources),
        out_specs=[same(1, seq, width), hbm] + [hbm] * len(shapes),
        out_shape=[
            jax.ShapeDtypeStruct((1, seq, width), BF),
            jax.ShapeDtypeStruct((layers, BLOCKS, SHARDS, rows, width), BF),
        ]
        + [jax.ShapeDtypeStruct((layers,) + s, d) for s, d in shapes],
        scratch_shapes=[pltpu.VMEM((2,) + s, d) for s, d in shapes]
        + [
            pltpu.VMEM((seq, width), BF),
            pltpu.VMEM((seq, width), BF),
            pltpu.VMEM((seq, width), F32),
            pltpu.VMEM((layers, BLOCKS, SHARDS, rows, width), BF),
            pltpu.SemaphoreType.DMA((layers,)),
            pltpu.SemaphoreType.DMA((layers,)),
            pltpu.SemaphoreType.DMA((len(shapes), 2)),
        ],
        compiler_params=pltpu.CompilerParams(vmem_limit_bytes=VMEM_LIMIT),
        cost_estimate=pl.CostEstimate(
            flops=layers * 1_740_000_000, bytes_accessed=80_000_000, transcendentals=0
        ),
        name="forward",
    )(ids, tokens, mods, biases, *sources)


def backward_kernel(layer, ids, mods, *refs):
    tensors, refs = refs[:10], refs[10:]
    grad_in, kept, sent, vec_out, gbb, hid, gsum, gmix, gqkv, gpre, dqt, halves = refs[:12]
    held, vec, in_sem, out_sem = refs[12:22], refs[22], refs[23], refs[24]
    grad, w, xs, qkv, probs, mixed, branch_a, act, slope, branch_b = held
    seq, width = gbb.shape
    size = width // HEADS
    place, core = ids[1], ids[2]
    rows = width // SHARDS
    names = ("grad", "w", "xs", "qkv", "probs", "mixed", "branch_a", "act", "slope", "branch_b")
    pieces = {}
    for name, far, near in zip(names, tensors, held):
        far = far.at[0] if name == "grad" else far.at[layer]
        if name == "w":
            for low, high in ((8, 12), (4, 8), (3, 4), (0, 3)):
                cut = pl.ds(low, high - low)
                pieces[name, low] = (far.at[cut], near.at[cut])
        else:
            pieces[name] = (far, near)
    order = (
        "grad", "branch_b", "act", "xs", "branch_a", ("w", 8), "slope",
        ("w", 4), ("w", 3), "mixed", "qkv", "probs", ("w", 0),
    )
    loads = {
        name: pltpu.make_async_copy(*pieces[name], in_sem.at[i]) for i, name in enumerate(order)
    }
    for name in order:
        loads[name].start()

    def ready(*names):
        for name in names:
            loads[name].wait()

    def weight(j):
        return w[j].reshape(width, width)

    def keep(shard, block, value):
        half = jnp.bitwise_xor(core, shard % 2)
        halves[half, jnp.bitwise_xor(place, shard // 2), block] = value

    def keep_front(block, value):
        for shard in range(SHARDS):
            keep(shard, block, value[shard * rows : (shard + 1) * rows])

    def keep_down(j, value):
        for part in range(SHARDS):
            keep(2 * j + part // 4, 8 + part % 4, value[part * rows : (part + 1) * rows])

    def put(row, value):
        for part in range(width // 128):
            at = row * (width // 128) + part
            vec[at : at + 1] = value[:, part * 128 : (part + 1) * 128]

    stores = []

    def store(low, high):
        cut = pl.ds(low, high - low)
        for half, out in ((1, sent), (0, kept)):
            copy = pltpu.make_async_copy(
                halves.at[half, :, cut], out.at[:, cut], out_sem.at[len(stores)]
            )
            copy.start()
            stores.append(copy)

    mod = mods[layer]
    shift_a, scale_a, gate_a, shift_b, scale_b, gate_b = (mod[i : i + 1] for i in range(6))
    vec[...] = jnp.zeros_like(vec)
    ready("grad", "branch_b")
    gout = grad[...].astype(F32)
    put(5, jnp.sum(gout * branch_b[...].astype(F32), 0, keepdims=True))
    gb = (gout * gate_b).astype(BF)
    gbb[...] = gb
    put(11, jnp.sum(gb.astype(F32), 0, keepdims=True))
    ready("act")
    for j in range(4):
        cols = slice(j * width, (j + 1) * width)
        keep_down(j, dot(act[:, cols], gbb[...], (0, 0)).astype(BF))
    ready("xs", "branch_a")
    x = xs[...].astype(F32)
    middle = x + gate_a * branch_a[...]
    normed_b, rstd_b = standard(middle)
    hid[...] = (normed_b * (1.0 + scale_b) + shift_b).astype(BF).T
    ready(("w", 8), "slope")
    for j in range(4):
        cols = slice(j * width, (j + 1) * width)
        gact = dot(gbb[...], weight(8 + j), (1, 1))
        g = (gact * slope[:, cols].astype(F32)).astype(BF)
        gpre[:, cols] = g
        put(7 + j, jnp.sum(g.astype(F32), 0, keepdims=True))
    for j in range(4):
        cols = slice(j * width, (j + 1) * width)
        keep_front(4 + j, dot(hid[...], gpre[:, cols]).astype(BF))
    store(4, 12)
    ready(("w", 4))
    ghb = dot(gpre[...], jnp.concatenate([weight(4 + j) for j in range(4)], axis=1), (1, 1))
    put(3, jnp.sum(ghb, 0, keepdims=True))
    put(4, jnp.sum(ghb * normed_b, 0, keepdims=True))
    gmid = gout + standard_back(ghb * (1.0 + scale_b), normed_b, rstd_b)
    gsum[...] = gmid
    put(2, jnp.sum(gmid * branch_a[...], 0, keepdims=True))
    gba = (gmid * gate_a).astype(BF)
    gbb[...] = gba
    put(6, jnp.sum(gba.astype(F32), 0, keepdims=True))
    ready(("w", 3), "mixed")
    gmix[...] = dot(gbb[...], weight(3), (1, 1)).astype(BF)
    keep_front(3, dot(mixed[...], gbb[...]).astype(BF))
    factor = size**-0.5
    ready("qkv", "probs")
    for h in range(HEADS):
        q = qkv[:, h * size : (h + 1) * size]
        k = qkv[:, width + h * size : width + (h + 1) * size]
        v = qkv[:, 2 * width + h * size : 2 * width + (h + 1) * size]
        g = gmix[:, h * size : (h + 1) * size]
        p = probs[h]
        pf = p.astype(F32)
        dp = dot(v, g, (1, 1))
        inner = jnp.sum(dp * pf, axis=0, keepdims=True)
        ds = (pf * (dp - inner) * factor).astype(BF)
        gqkv[:, 2 * width + h * size : 2 * width + (h + 1) * size] = dot(p, g).astype(BF)
        gqkv[:, width + h * size : width + (h + 1) * size] = dot(ds, q).astype(BF)
        dqt[h * size : (h + 1) * size, :] = dot(k, ds, (0, 0)).astype(BF)
    gqkv[:, :width] = dqt[...].T
    normed_a, rstd_a = standard(xs[...].astype(F32))
    hid[...] = (normed_a * (1.0 + scale_a) + shift_a).astype(BF).T
    for j in range(3):
        cols = slice(j * width, (j + 1) * width)
        keep_front(j, dot(hid[...], gqkv[:, cols]).astype(BF))
    store(0, 4)
    ready(("w", 0))
    gha = dot(gqkv[...], jnp.concatenate([weight(j) for j in range(3)], axis=1), (1, 1))
    put(0, jnp.sum(gha, 0, keepdims=True))
    put(1, jnp.sum(gha * normed_a, 0, keepdims=True))
    grad_in[0] = (gsum[...] + standard_back(gha * (1.0 + scale_a), normed_a, rstd_a)).astype(BF)
    vec_out[...] = vec[...].astype(BF)
    for copy in stores:
        copy.wait()


def backward(layer, ids, grad, mods, w, saved):
    _, seq, width = grad.shape
    rows = width // SHARDS

    def full(*shape):
        return pl.BlockSpec(shape, lambda i: (0,) * len(shape))

    half = (SHARDS // 2, BLOCKS, rows, width)
    hbm = pl.BlockSpec(memory_space=pl.ANY)
    tensors = (grad, w, *saved)
    return pl.pallas_call(
        functools.partial(backward_kernel, layer),
        grid=(1,),
        in_specs=[pl.BlockSpec(memory_space=pltpu.SMEM), full(*mods.shape)] + [hbm] * len(tensors),
        out_specs=[full(1, seq, width), hbm, hbm, full(48, 128)],
        out_shape=[
            jax.ShapeDtypeStruct((1, seq, width), BF),
            jax.ShapeDtypeStruct(half, BF),
            jax.ShapeDtypeStruct(half, BF),
            jax.ShapeDtypeStruct((48, 128), BF),
        ],
        scratch_shapes=[
            pltpu.VMEM((seq, width), BF),
            pltpu.VMEM((width, seq), BF),
            pltpu.VMEM((seq, width), F32),
            pltpu.VMEM((seq, width), BF),
            pltpu.VMEM((seq, 3 * width), BF),
            pltpu.VMEM((seq, 4 * width), BF),
            pltpu.VMEM((width, seq), BF),
            pltpu.VMEM((2,) + half, BF),
        ]
        + [pltpu.VMEM(a.shape[1:], a.dtype) for a in tensors]
        + [
            pltpu.VMEM((48, 128), F32),
            pltpu.SemaphoreType.DMA((13,)),
            pltpu.SemaphoreType.DMA((4,)),
        ],
        compiler_params=pltpu.CompilerParams(vmem_limit_bytes=VMEM_LIMIT),
        cost_estimate=pl.CostEstimate(
            flops=3_480_000_000, bytes_accessed=20_000_000, transcendentals=0
        ),
        name=f"backward_{layer}",
    )(ids, mods, *tensors)


def embed_lead(steps, width):
    half = width // 2
    freq = jnp.exp(-math.log(10000.0) * jnp.arange(half, dtype=F32) / half)
    angle = 6.0 * steps.astype(F32)[:, None] * freq[None, :]
    return jnp.concatenate([jnp.sin(angle), jnp.cos(angle)], -1)


def over_core(value):
    return lax.ppermute(value, "batch", [(i, i ^ 1) for i in range(8)])


def over_z(value, away):
    return lax.ppermute(value, "batch", [(i, i ^ (2 * away)) for i in range(8)])


def over_section(value, away):
    return lax.ppermute(value, "section", [(i, i ^ away) for i in range(4)])


def after(value, *others):
    return lax.optimization_barrier((value,) + others)[0]


def gather_shards(w, small, exchange):
    x0, y0, z1 = over_section(w, 1), over_section(w, 2), over_z(w, 1)
    z2 = over_z(w, 2)
    z1, small = lax.optimization_barrier((z1, small))
    small = lax.all_to_all(small, BOTH, 0, 0, tiled=True)
    x1, y1 = over_section(z1, 1), over_section(z1, 2)
    z3 = over_z(z2, 1)
    p0, q0 = over_section(y0[:6], 1), over_section(x0[6:], 2)
    x1, small = lax.optimization_barrier((x1, small))
    part = exchange(small)
    x2, y2 = over_section(z2, 1), over_section(z2, 2)
    p1, q1 = over_section(y1[:6], 1), over_section(x1[6:], 2)
    x3, y3 = over_section(z3, 1), over_section(z3, 2)
    p2, q2 = over_section(y2[:6], 1), over_section(x2[6:], 2)
    x3, part = lax.optimization_barrier((x3, part))
    p3, q3 = over_section(y3[:6], 1), over_section(x3[6:], 2)
    names = {}
    for zx, group in enumerate(
        [(w, x0, y0, p0, q0), (z1, x1, y1, p1, q1), (z2, x2, y2, p2, q2), (z3, x3, y3, p3, q3)]
    ):
        names[0, zx], names[1, zx], names[2, zx] = [(group[0], 0)], [(group[1], 0)], [(group[2], 0)]
        names[3, zx] = [(group[3], 0), (group[4], 6)]
    sources, plan = [], {}
    for keys in (
        [(0, 0), (0, 1), (1, 0), (2, 0), (1, 1), (2, 1), (3, 0)],
        [(0, 2), (0, 3), (3, 1), (1, 2), (2, 2)],
        [(1, 3), (2, 3), (3, 2), (3, 3)],
    ):
        bundle = []
        for key in keys:
            plan[key + (0,)], plan[key + (1,)] = [], []
            for array, low in names[key]:
                plan[key + (0,)].append((len(sources), low, 0))
                sources.append(array)
                bundle.append((key, array, low))
        other = over_core(jnp.concatenate([array for _, array, _ in bundle]))
        start = 0
        for key, array, low in bundle:
            plan[key + (1,)].append((len(sources), low, start))
            start += array.shape[0]
        sources.append(other)
    final = {}
    for key, parts in plan.items():
        final[key] = []
        for index, low, start in parts:
            high = BLOCKS if key[0] != 3 else low + 6
            final[key].append((index, start, low, high))
    return final, sources, small, part


def sum_shards(parts, vec):
    def add(*values):
        total = values[0].astype(F32)
        for value in values[1:]:
            total = total + value.astype(F32)
        return total

    def joined(zx, p, q):
        left = jnp.concatenate([parts[1, zx][:6], add(parts[1, zx][6:], q).astype(BF)])
        right = jnp.concatenate([add(parts[2, zx][:6], p).astype(BF), parts[2, zx][6:]])
        return left, right

    p3, q3 = over_section(parts[3, 3][:6], 1), over_section(parts[3, 3][6:], 2)
    d2, d1 = over_section(parts[3, 2], 1), over_section(parts[3, 1], 2)
    left, right = joined(3, p3, q3)
    x3, y3 = over_section(left, 1), over_section(right, 2)
    p0, q0 = over_section(parts[3, 0][:6], 1), over_section(parts[3, 0][6:], 2)
    left, right = parts[1, 2], add(parts[2, 2], d2).astype(BF)
    x3, vec = lax.optimization_barrier((x3, vec))
    vec = lax.all_to_all(vec, BOTH, 0, 0, tiled=True)
    total = add(parts[0, 3], x3, y3).astype(BF)
    left, right, total = lax.optimization_barrier((left, right, total))
    z3 = over_z(total, 1)
    x2, y2 = over_section(left, 1), over_section(right, 2)
    left, right = add(parts[1, 1], d1).astype(BF), parts[2, 1]
    total = add(parts[0, 2], x2, y2, z3).astype(BF)
    left, right, total = lax.optimization_barrier((left, right, total))
    z2, s2 = over_z(total[:6], 2), over_z(total[6:], 2)
    x1, y1 = over_section(left, 1), over_section(right, 2)
    left, right = joined(0, p0, q0)
    total = add(parts[0, 1], x1, y1).astype(BF)
    left, right, total, z2 = lax.optimization_barrier((left, right, total, z2))
    x0, y0 = over_section(left, 1), over_section(right, 2)
    z1 = over_z(total, 1)
    return unpacked(parts[0, 0], x0, y0, z1, z2, s2), vec


def body_permuted(
    tokens, levels, lead, w_qkv, w_o, b_o, w_up, b_up, w_down, b_down, w_ada, b_ada, cotangent
):
    section, batch = lax.axis_index("section"), lax.axis_index("batch")
    place, core = batch // 2, batch % 2
    width = tokens.shape[2]
    rows = width // SHARDS
    ids = jnp.stack([section, place, core, levels[0]]).astype(jnp.int32)
    shard, small = packed(lead, w_qkv, w_o, w_up, w_down, b_o, b_up, b_down)
    mine = []

    def exchange(smalls):
        conds = jax.nn.silu(embed_lead(smalls[:, 4, 0], width))
        mine.append(lax.dynamic_slice_in_dim(conds, batch * rows, rows, axis=1))
        part = jnp.dot(mine[0], w_ada[0].astype(F32), precision=HIGH)
        bias = jnp.zeros((6 * width,), F32)
        bias = lax.dynamic_update_slice_in_dim(
            bias, b_ada[0].astype(F32), batch * 6 * rows, axis=0
        )
        return lax.all_to_all((part + bias).reshape(32, -1, 128), BOTH, 0, 0, tiled=True)

    plan, sources, smalls, part = gather_shards(shard, small, exchange)
    mine = mine[0]
    mods = jnp.sum(part.reshape(4, SHARDS, -1, 128), axis=1).reshape(4, 6, width)
    vectors = smalls.reshape(4, SHARDS, 16 * 128).astype(F32)
    biases = jnp.concatenate(
        [
            vectors[:, :, :rows].reshape(4, 1, width),
            vectors[:, :, 128 : 128 + 4 * rows].reshape(4, 4, width),
            vectors[:, :, 384 : 384 + rows].reshape(4, 1, width),
        ],
        axis=1,
    )

    result, w, *saved = forward(plan, sources, ids, tokens, mods, biases)
    grad = cotangent
    sums = jnp.zeros((4, 4, BLOCKS, rows, width), BF)
    vecs = [None] * 4
    for layer in reversed(range(4)):
        grad, kept, sent, vecs[layer] = backward(layer, ids, grad, mods, w, saved)
        both = (kept.astype(F32) + over_core(sent).astype(F32)).astype(BF)
        sums = lax.dynamic_update_index_in_dim(sums, both, section ^ layer, 0)
    vec = jnp.broadcast_to(jnp.stack(vecs)[:, None], (4, SHARDS, 48, 128)).reshape(32, 48, 128)
    totals, vec = sum_shards({(i, j): sums[i, j] for i in range(4) for j in range(4)}, vec)
    vec = vec[:, :36].astype(F32).reshape(32, 12, width)
    g_ada = jnp.dot(mine.T, vec[:, :6].reshape(32, 6 * width), precision=HIGH)[None]
    flat = jnp.sum(vec, 0)

    def slot(low, high, count):
        return lax.dynamic_slice_in_dim(
            flat[low:high].reshape(-1), batch * count, count, axis=0
        )[None]

    return (
        result,
        grad,
        totals[0],
        totals[1],
        slot(6, 7, rows),
        totals[2],
        slot(7, 11, 4 * rows),
        totals[3],
        slot(11, 12, rows),
        g_ada,
        slot(0, 6, 6 * rows),
    )


def pack_kernel(lead, w_qkv, w_o, w_up, w_down, b_o, b_up, b_down, out, small):
    _, rows, width = w_o.shape
    for j in range(3):
        out[j] = w_qkv[0, :, j * width : (j + 1) * width]
    out[3] = w_o[0]
    for j in range(4):
        out[4 + j] = w_up[0, :, j * width : (j + 1) * width]
        out[8 + j] = w_down[0, j * rows : (j + 1) * rows]
    small[...] = jnp.full(small.shape, lead[0].astype(F32), F32).astype(BF)
    peers = small.shape[0]
    for row, bias in zip((0, 1, 3), (b_o, b_up, b_down)):
        count = bias.shape[1]
        for start in range(0, count, 128):
            size = min(128, count - start)
            value = bias[0, start : start + size].astype(F32).reshape(1, 1, size)
            at = row + start // 128
            small[:, at : at + 1, :size] = jnp.broadcast_to(value, (peers, 1, size)).astype(BF)


def packed(lead, w_qkv, w_o, w_up, w_down, b_o, b_up, b_down):
    _, rows, width = w_o.shape
    vmem = pl.BlockSpec(memory_space=pltpu.VMEM)
    return pl.pallas_call(
        pack_kernel,
        in_specs=[pl.BlockSpec(memory_space=pltpu.SMEM)] + [vmem] * 7,
        out_shape=[
            jax.ShapeDtypeStruct((BLOCKS, rows, width), BF),
            jax.ShapeDtypeStruct((32, 16, 128), BF),
        ],
        name="pack",
    )(lead, w_qkv, w_o, w_up, w_down, b_o, b_up, b_down)


def unpack_kernel(own, x, y, z, low, high, g_qkv, g_o, g_up, g_down):
    _, rows, width = g_o.shape
    for j in range(BLOCKS):
        last = low[j] if j < 6 else high[j - 6]
        total = own[j].astype(F32) + x[j].astype(F32) + y[j].astype(F32)
        total = total + z[j].astype(F32) + last.astype(F32)
        if j < 3:
            g_qkv[0, :, j * width : (j + 1) * width] = total
        elif j == 3:
            g_o[0] = total
        elif j < 8:
            g_up[0, :, (j - 4) * width : (j - 3) * width] = total
        else:
            g_down[0, (j - 8) * rows : (j - 7) * rows] = total


def unpacked(own, x, y, z, low, high):
    _, rows, width = own.shape
    return pl.pallas_call(
        unpack_kernel,
        out_shape=[
            jax.ShapeDtypeStruct((1, rows, 3 * width), F32),
            jax.ShapeDtypeStruct((1, rows, width), F32),
            jax.ShapeDtypeStruct((1, rows, 4 * width), F32),
            jax.ShapeDtypeStruct((1, 4 * rows, width), F32),
        ],
        name="unpack",
    )(own, x, y, z, low, high)


def local_shard(w_qkv, w_o, w_up, w_down):
    _, rows, width = w_o.shape

    def blocks_of(piece):
        return jnp.stack(jnp.split(piece, piece.shape[1] // width, axis=1))

    return jnp.concatenate(
        [blocks_of(w_qkv[0]), w_o, blocks_of(w_up[0]), w_down[0].reshape(4, rows, width)]
    )


def body_general(
    tokens, levels, lead, w_qkv, w_o, b_o, w_up, b_up, w_down, b_down, w_ada, b_ada, cotangent
):
    batch = lax.axis_index("batch")
    sections, batches = lax.axis_size("section"), lax.axis_size("batch")
    width = tokens.shape[2]
    rows, tall = width // batches, width // SHARDS
    zero = jnp.zeros((), jnp.int32)
    ids = jnp.stack([zero, zero, zero, levels[0]])

    shards = lax.all_gather(local_shard(w_qkv, w_o, w_up, w_down), BOTH, axis=0, tiled=False)
    shards = shards.reshape(sections, batches, BLOCKS, rows, width)
    front = jnp.swapaxes(shards[:, :, :8], 1, 2).reshape(sections, 8, SHARDS, tall, width)
    downs = shards[:, :, 8:].reshape(sections, SHARDS, 4, tall, width)
    source = jnp.concatenate([jnp.swapaxes(front, 1, 2), downs], axis=2)
    source = source.reshape(sections * SHARDS * BLOCKS, tall, width)
    plan = {
        (l, z, c): [(0, ((l * 4 + z) * 2 + c) * BLOCKS, 0, BLOCKS)]
        for l in range(4)
        for z in range(4)
        for c in range(2)
    }
    small = jnp.concatenate([b_o[0], b_up[0], b_down[0]])
    smalls = lax.all_gather(small, BOTH, axis=0, tiled=False).reshape(sections, batches, -1)
    smalls = smalls.astype(F32)
    biases = jnp.concatenate(
        [
            smalls[:, :, :rows].reshape(sections, 1, width),
            smalls[:, :, rows : 5 * rows].reshape(sections, 4, width),
            smalls[:, :, 5 * rows :].reshape(sections, 1, width),
        ],
        axis=1,
    )
    leads = lax.all_gather(lead, BOTH, axis=0, tiled=True)
    conds = jax.nn.silu(embed_lead(leads, width))
    mine = lax.dynamic_slice_in_dim(conds, batch * rows, rows, axis=1)
    part = jnp.dot(mine, w_ada[0].astype(F32), precision=HIGH)
    bias = jnp.zeros((6 * width,), F32)
    bias = lax.dynamic_update_slice_in_dim(
        bias, b_ada[0].astype(F32), batch * 6 * rows, axis=0
    )
    part = (part + bias).reshape(sections, batches, 6 * width)
    part = lax.psum_scatter(part, "batch", scatter_dimension=1, tiled=True)
    mods = lax.all_to_all(part[:, 0], "section", 0, 0, tiled=True)
    mods = mods.reshape(sections, 6, width)

    result, w, *saved = forward(plan, [source], ids, tokens, mods, biases)
    grad = cotangent
    grads, vecs = [None] * sections, [None] * sections
    for layer in reversed(range(sections)):
        grad, kept, sent, vecs[layer] = backward(layer, ids, grad, mods, w, saved)
        grads[layer] = jnp.stack([kept, sent], axis=1).reshape(SHARDS, BLOCKS, tall, width)
    grads = jnp.stack(grads)
    front = jnp.swapaxes(grads[:, :, :8], 1, 2).reshape(sections, 8, batches, rows, width)
    downs = grads[:, :, 8:].reshape(sections, batches, 4, rows, width)
    total = jnp.concatenate([jnp.swapaxes(front, 1, 2), downs], axis=2)
    total = total.reshape(sections, batches, BLOCKS * rows, width)
    total = lax.psum_scatter(total, "section", scatter_dimension=0, tiled=True)
    total = lax.psum_scatter(total, "batch", scatter_dimension=1, tiled=True)
    total = total.astype(F32).reshape(BLOCKS, rows, width)

    vec = jnp.stack(vecs)[:, :36].reshape(sections, 12, width)
    vec = lax.all_to_all(vec, "section", 0, 0, tiled=True)
    vec = lax.all_gather(vec, "batch", axis=1, tiled=False).astype(F32)
    vec = vec.reshape(sections * batches, 12, width)
    g_ada = jnp.dot(mine.T, vec[:, :6].reshape(-1, 6 * width), precision=HIGH)[None]
    flat = jnp.sum(vec, 0)

    def slot(low, high, count):
        return lax.dynamic_slice_in_dim(
            flat[low:high].reshape(-1), batch * count, count, axis=0
        )[None]

    return (
        result,
        grad,
        jnp.concatenate([total[0], total[1], total[2]], axis=1)[None],
        total[3][None],
        slot(6, 7, rows),
        jnp.concatenate([total[4 + j] for j in range(4)], axis=1)[None],
        slot(7, 11, 4 * rows),
        total[8:].reshape(1, 4 * rows, width),
        slot(11, 12, rows),
        g_ada,
        slot(0, 6, 6 * rows),
    )


def solution(mesh):
    in_specs = (
        P(("section", "batch"), None, None),
        P(("section", "batch")),
        P(("section", "batch")),
        P("section", "batch", None),
        P("section", "batch", None),
        P("section", "batch"),
        P("section", "batch", None),
        P("section", "batch"),
        P("section", "batch", None),
        P("section", "batch"),
        P("section", "batch", None),
        P("section", "batch"),
        P(("section", "batch"), None, None),
    )
    out_specs = (
        P(("section", "batch"), None, None),
        P(("section", "batch"), None, None),
        P("section", "batch", None),
        P("section", "batch", None),
        P("section", "batch"),
        P("section", "batch", None),
        P("section", "batch"),
        P("section", "batch", None),
        P("section", "batch"),
        P("section", "batch", None),
        P("section", "batch"),
    )
    permuted = mesh.shape["section"] == 4 and mesh.shape["batch"] == SHARDS
    body = body_permuted if permuted else body_general
    return jax.shard_map(body, mesh=mesh, in_specs=in_specs, out_specs=out_specs, check_vma=False)
```

```python
import functools
import math

import jax
import jax.numpy as jnp
from jax import lax
from jax.experimental import pallas as pl
from jax.experimental.pallas import tpu as pltpu
from jax.sharding import PartitionSpec as P

HEADS = 6
LEVELS = 13
BLOCKS = 12
SHARDS = 8
EPS = 1e-06
NEG = -1e30
BF = jnp.bfloat16
F32 = jnp.float32
HIGH = lax.Precision.HIGHEST
BOTH = ("section", "batch")
C0 = math.sqrt(2.0 / math.pi)
C1 = 0.044715
VMEM_LIMIT = 60 * 2**20


def dot(left, right, over=(1, 0)):
    return lax.dot_general(
        left, right, (((over[0],), (over[1],)), ((), ())), preferred_element_type=F32
    )


def standard(value):
    centered = value - jnp.mean(value, -1, keepdims=True)
    rstd = lax.rsqrt(jnp.mean(centered * centered, -1, keepdims=True) + EPS)
    return centered * rstd, rstd


def standard_back(grad, normed, rstd):
    return rstd * (
        grad
        - jnp.mean(grad, -1, keepdims=True)
        - normed * jnp.mean(grad * normed, -1, keepdims=True)
    )


def forward_kernel(plan, ids, tokens, mods, biases, *refs):
    count = len({part[0] for parts in plan.values() for part in parts})
    sources, refs = refs[:count], refs[count:]
    result, w_out, outs, held = refs[0], refs[1], refs[2:10], refs[10:18]
    value, hidden, acc, w, in_sem, out_sem, save_sem = refs[18:]
    layer = pl.program_id(0)
    layers = pl.num_programs(0)
    seq, width = value.shape
    size = width // HEADS
    section, place, core = ids[0], ids[1], ids[2]

    @pl.when(layer == 0)
    def _():
        value[...] = tokens[0]

        @pl.loop(0, layers)
        def _(target):
            for away in range(4):

                @pl.when(jnp.bitwise_xor(section, target) == away)
                def _():
                    for (sx, zx, cx), parts in plan.items():
                        if sx != away:
                            continue
                        shard = 2 * jnp.bitwise_xor(place, zx) + jnp.bitwise_xor(core, cx)
                        for index, lead, low, high in parts:
                            ref = sources[index]
                            top = min(high, 8)
                            if low < top:
                                pltpu.make_async_copy(
                                    ref.at[pl.ds(lead, top - low)],
                                    w.at[target, pl.ds(low, top - low), shard],
                                    in_sem.at[target],
                                ).start()
                            if high > 8:
                                pltpu.make_async_copy(
                                    ref.at[pl.ds(lead + 8 - low, 4)],
                                    w.at[target, 8 + shard // 2, pl.ds(4 * (shard % 2), 4)],
                                    in_sem.at[target],
                                ).start()

    pltpu.make_async_copy(w.at[layer], w.at[layer], in_sem.at[layer]).wait()
    pltpu.make_async_copy(w.at[layer], w_out.at[layer], out_sem.at[layer]).start()

    slot = layer % 2
    xs, qkv, probs, mixed, branch_a, act, slope, branch_b = (ref.at[slot] for ref in held)

    def saving(i, half, target):
        return pltpu.make_async_copy(held[i].at[half], outs[i].at[target], save_sem.at[i, half])

    def reuse(*which):
        @pl.when(layer >= 2)
        def _():
            for i in which:
                saving(i, slot, layer).wait()

    def save(*which):
        for i in which:
            saving(i, slot, layer).start()

    def weight(j):
        return w[layer, j].reshape(width, width)

    def weights(low, high):
        return jnp.concatenate([weight(j) for j in range(low, high)], axis=1)

    mod = mods[layer]
    bias = biases[layer]
    reuse(*range(8))
    xs[...] = value[...]
    save(0)
    x = value[...].astype(F32)
    normed, _ = standard(x)
    hidden[...] = (normed * (1.0 + mod[1:2]) + mod[0:1]).astype(BF)
    qkv[...] = dot(hidden[...], weights(0, 3)).astype(BF)
    save(1)
    limit = ids[3] * (seq // LEVELS)
    row = lax.broadcasted_iota(jnp.int32, (seq, 1), 0)
    mask = jnp.where(row < limit, 0.0, NEG)
    def score(h):
        q = qkv[:, h * size : (h + 1) * size] * (size**-0.5)
        k = qkv[:, width + h * size : width + (h + 1) * size]
        return dot(k, q, (1, 1)) + mask

    def attend(h, raw):
        top = jnp.max(raw, axis=0, keepdims=True)
        e = jnp.exp(raw - top)
        p = (e * (1.0 / jnp.sum(e, axis=0, keepdims=True))).astype(BF)
        probs[h] = p
        return p

    def mix(h, p):
        v = qkv[:, 2 * width + h * size : 2 * width + (h + 1) * size]
        mixed[h * size : (h + 1) * size, :] = dot(v, p, (0, 0)).astype(BF)

    raws = {h: score(h) for h in range(2)}
    held_p = None
    for h in range(HEADS):
        if h + 2 < HEADS:
            raws[h + 2] = score(h + 2)
        p = attend(h, raws.pop(h))
        if held_p is not None:
            mix(h - 1, held_p)
        held_p = p
    mix(HEADS - 1, held_p)
    save(2, 3)
    ba = dot(mixed[...], weight(3), (0, 0)) + bias[0:1]
    branch_a[...] = ba
    save(4)
    middle = value[...].astype(F32) + mod[2:3] * ba
    acc[...] = middle
    normed, _ = standard(middle)
    hidden[...] = (normed * (1.0 + mod[4:5]) + mod[3:4]).astype(BF)
    for j in range(0, 4, 2):
        cols = slice(j * width, (j + 2) * width)
        shift = jnp.concatenate([bias[1 + i : 2 + i] for i in range(j, j + 2)], axis=1)
        pre = dot(hidden[...], weights(4 + j, 4 + j + 2)) + shift
        square = pre * pre
        t = jnp.tanh(pre * (C0 + (C0 * C1) * square))
        half = 0.5 + 0.5 * t
        a = pre * half
        slope[:, cols] = (half + a * (1.0 - t) * (C0 + (3.0 * C0 * C1) * square)).astype(BF)
        act[:, cols] = a.astype(BF)
    save(5, 6)
    bb = dot(act[...], w[layer, 8:12].reshape(4 * width, width)) + bias[5:6]
    branch_b[...] = bb.astype(BF)
    save(7)
    out = (acc[...] + mod[5:6] * bb).astype(BF)
    value[...] = out
    result[0] = out

    @pl.when(layer == layers - 1)
    def _():
        for i in range(8):
            for half in range(2):
                saving(i, half, layer).wait()

        @pl.loop(0, layers)
        def _(target):
            pltpu.make_async_copy(w.at[target], w_out.at[target], out_sem.at[target]).wait()


def forward(plan, sources, ids, tokens, mods, biases):
    layers = mods.shape[0]
    _, seq, width = tokens.shape
    rows = width // SHARDS

    def same(*shape):
        return pl.BlockSpec(shape, lambda l: (0,) * len(shape))

    shapes = [
        ((seq, width), BF),
        ((seq, 3 * width), BF),
        ((HEADS, seq, seq), BF),
        ((width, seq), BF),
        ((seq, width), F32),
        ((seq, 4 * width), BF),
        ((seq, 4 * width), BF),
        ((seq, width), BF),
    ]
    hbm = pl.BlockSpec(memory_space=pl.ANY)
    return pl.pallas_call(
        functools.partial(forward_kernel, plan),
        grid=(layers,),
        in_specs=[
            pl.BlockSpec(memory_space=pltpu.SMEM),
            same(1, seq, width),
            same(layers, 6, width),
            same(layers, 6, width),
        ]
        + [hbm] * len(sources),
        out_specs=[same(1, seq, width), hbm] + [hbm] * len(shapes),
        out_shape=[
            jax.ShapeDtypeStruct((1, seq, width), BF),
            jax.ShapeDtypeStruct((layers, BLOCKS, SHARDS, rows, width), BF),
        ]
        + [jax.ShapeDtypeStruct((layers,) + s, d) for s, d in shapes],
        scratch_shapes=[pltpu.VMEM((2,) + s, d) for s, d in shapes]
        + [
            pltpu.VMEM((seq, width), BF),
            pltpu.VMEM((seq, width), BF),
            pltpu.VMEM((seq, width), F32),
            pltpu.VMEM((layers, BLOCKS, SHARDS, rows, width), BF),
            pltpu.SemaphoreType.DMA((layers,)),
            pltpu.SemaphoreType.DMA((layers,)),
            pltpu.SemaphoreType.DMA((len(shapes), 2)),
        ],
        compiler_params=pltpu.CompilerParams(vmem_limit_bytes=VMEM_LIMIT),
        cost_estimate=pl.CostEstimate(
            flops=layers * 1_740_000_000, bytes_accessed=80_000_000, transcendentals=0
        ),
        name="forward",
    )(ids, tokens, mods, biases, *sources)


def backward_kernel(layer, ids, mods, *refs):
    tensors, refs = refs[:10], refs[10:]
    grad_in, kept, sent, vec_out, gbb, hid, gsum, gmix, gqkv, gpre, dqt, halves = refs[:12]
    held, vec, in_sem, out_sem = refs[12:22], refs[22], refs[23], refs[24]
    grad, w, xs, qkv, probs, mixed, branch_a, act, slope, branch_b = held
    seq, width = gbb.shape
    size = width // HEADS
    place, core = ids[1], ids[2]
    rows = width // SHARDS
    names = ("grad", "w", "xs", "qkv", "probs", "mixed", "branch_a", "act", "slope", "branch_b")
    pieces = {}
    for name, far, near in zip(names, tensors, held):
        far = far.at[0] if name == "grad" else far.at[layer]
        if name == "w":
            for low, high in ((8, 12), (4, 8), (3, 4), (0, 3)):
                cut = pl.ds(low, high - low)
                pieces[name, low] = (far.at[cut], near.at[cut])
        else:
            pieces[name] = (far, near)
    order = (
        "grad", "branch_b", "act", "xs", "branch_a", ("w", 8), "slope",
        ("w", 4), ("w", 3), "mixed", "qkv", "probs", ("w", 0),
    )
    loads = {
        name: pltpu.make_async_copy(*pieces[name], in_sem.at[i]) for i, name in enumerate(order)
    }
    for name in order:
        loads[name].start()

    def ready(*names):
        for name in names:
            loads[name].wait()

    def weight(j):
        return w[j].reshape(width, width)

    def keep(shard, block, value):
        half = jnp.bitwise_xor(core, shard % 2)
        halves[half, jnp.bitwise_xor(place, shard // 2), block] = value

    def keep_front(block, value):
        for shard in range(SHARDS):
            keep(shard, block, value[shard * rows : (shard + 1) * rows])

    def keep_down(j, value):
        for part in range(SHARDS):
            keep(2 * j + part // 4, 8 + part % 4, value[part * rows : (part + 1) * rows])

    def put(row, value):
        for part in range(width // 128):
            at = row * (width // 128) + part
            vec[at : at + 1] = value[:, part * 128 : (part + 1) * 128]

    stores = []

    def store(low, high):
        cut = pl.ds(low, high - low)
        for half, out in ((1, sent), (0, kept)):
            copy = pltpu.make_async_copy(
                halves.at[half, :, cut], out.at[:, cut], out_sem.at[len(stores)]
            )
            copy.start()
            stores.append(copy)

    mod = mods[layer]
    shift_a, scale_a, gate_a, shift_b, scale_b, gate_b = (mod[i : i + 1] for i in range(6))
    vec[...] = jnp.zeros_like(vec)
    ready("grad", "branch_b")
    gout = grad[...].astype(F32)
    put(5, jnp.sum(gout * branch_b[...].astype(F32), 0, keepdims=True))
    gb = (gout * gate_b).astype(BF)
    gbb[...] = gb
    put(11, jnp.sum(gb.astype(F32), 0, keepdims=True))
    ready("act")
    for j in range(4):
        cols = slice(j * width, (j + 1) * width)
        keep_down(j, dot(act[:, cols], gbb[...], (0, 0)).astype(BF))
    ready("xs", "branch_a")
    x = xs[...].astype(F32)
    middle = x + gate_a * branch_a[...]
    normed_b, rstd_b = standard(middle)
    hid[...] = (normed_b * (1.0 + scale_b) + shift_b).astype(BF).T
    ready(("w", 8), "slope")
    for j in range(4):
        cols = slice(j * width, (j + 1) * width)
        gact = dot(gbb[...], weight(8 + j), (1, 1))
        g = (gact * slope[:, cols].astype(F32)).astype(BF)
        gpre[:, cols] = g
        put(7 + j, jnp.sum(g.astype(F32), 0, keepdims=True))
    for j in range(4):
        cols = slice(j * width, (j + 1) * width)
        keep_front(4 + j, dot(hid[...], gpre[:, cols]).astype(BF))
    store(4, 12)
    ready(("w", 4))
    ghb = dot(gpre[...], jnp.concatenate([weight(4 + j) for j in range(4)], axis=1), (1, 1))
    put(3, jnp.sum(ghb, 0, keepdims=True))
    put(4, jnp.sum(ghb * normed_b, 0, keepdims=True))
    gmid = gout + standard_back(ghb * (1.0 + scale_b), normed_b, rstd_b)
    gsum[...] = gmid
    put(2, jnp.sum(gmid * branch_a[...], 0, keepdims=True))
    gba = (gmid * gate_a).astype(BF)
    gbb[...] = gba
    put(6, jnp.sum(gba.astype(F32), 0, keepdims=True))
    ready(("w", 3), "mixed")
    gmix[...] = dot(gbb[...], weight(3), (1, 1)).astype(BF)
    keep_front(3, dot(mixed[...], gbb[...]).astype(BF))
    factor = size**-0.5
    ready("qkv", "probs")
    def part(i, h):
        return qkv[:, i * width + h * size : i * width + (h + 1) * size]

    def probe(h):
        return dot(part(2, h), gmix[:, h * size : (h + 1) * size], (1, 1))

    def finish(h, ds):
        gqkv[:, 2 * width + h * size : 2 * width + (h + 1) * size] = dot(
            probs[h], gmix[:, h * size : (h + 1) * size]
        ).astype(BF)
        gqkv[:, width + h * size : width + (h + 1) * size] = dot(ds, part(0, h)).astype(BF)
        dqt[h * size : (h + 1) * size, :] = dot(part(1, h), ds, (0, 0)).astype(BF)

    dps = {h: probe(h) for h in range(1)}
    waiting = []
    for h in range(HEADS):
        if h + 1 < HEADS:
            dps[h + 1] = probe(h + 1)
        pf = probs[h].astype(F32)
        dp = dps.pop(h)
        inner = jnp.sum(dp * pf, axis=0, keepdims=True)
        waiting.append((h, (pf * (dp - inner) * factor).astype(BF)))
        if len(waiting) > 0:
            finish(*waiting.pop(0))
    for item in waiting:
        finish(*item)
    gqkv[:, :width] = dqt[...].T
    normed_a, rstd_a = standard(xs[...].astype(F32))
    hid[...] = (normed_a * (1.0 + scale_a) + shift_a).astype(BF).T
    for j in range(3):
        cols = slice(j * width, (j + 1) * width)
        keep_front(j, dot(hid[...], gqkv[:, cols]).astype(BF))
    store(0, 4)
    ready(("w", 0))
    gha = dot(gqkv[...], jnp.concatenate([weight(j) for j in range(3)], axis=1), (1, 1))
    put(0, jnp.sum(gha, 0, keepdims=True))
    put(1, jnp.sum(gha * normed_a, 0, keepdims=True))
    grad_in[0] = (gsum[...] + standard_back(gha * (1.0 + scale_a), normed_a, rstd_a)).astype(BF)
    vec_out[...] = vec[...].astype(BF)
    for copy in stores:
        copy.wait()


def backward(layer, ids, grad, mods, w, saved):
    _, seq, width = grad.shape
    rows = width // SHARDS

    def full(*shape):
        return pl.BlockSpec(shape, lambda i: (0,) * len(shape))

    half = (SHARDS // 2, BLOCKS, rows, width)
    hbm = pl.BlockSpec(memory_space=pl.ANY)
    tensors = (grad, w, *saved)
    return pl.pallas_call(
        functools.partial(backward_kernel, layer),
        grid=(1,),
        in_specs=[pl.BlockSpec(memory_space=pltpu.SMEM), full(*mods.shape)] + [hbm] * len(tensors),
        out_specs=[full(1, seq, width), hbm, hbm, full(48, 128)],
        out_shape=[
            jax.ShapeDtypeStruct((1, seq, width), BF),
            jax.ShapeDtypeStruct(half, BF),
            jax.ShapeDtypeStruct(half, BF),
            jax.ShapeDtypeStruct((48, 128), BF),
        ],
        scratch_shapes=[
            pltpu.VMEM((seq, width), BF),
            pltpu.VMEM((width, seq), BF),
            pltpu.VMEM((seq, width), F32),
            pltpu.VMEM((seq, width), BF),
            pltpu.VMEM((seq, 3 * width), BF),
            pltpu.VMEM((seq, 4 * width), BF),
            pltpu.VMEM((width, seq), BF),
            pltpu.VMEM((2,) + half, BF),
        ]
        + [pltpu.VMEM(a.shape[1:], a.dtype) for a in tensors]
        + [
            pltpu.VMEM((48, 128), F32),
            pltpu.SemaphoreType.DMA((13,)),
            pltpu.SemaphoreType.DMA((4,)),
        ],
        compiler_params=pltpu.CompilerParams(vmem_limit_bytes=VMEM_LIMIT),
        cost_estimate=pl.CostEstimate(
            flops=3_480_000_000, bytes_accessed=20_000_000, transcendentals=0
        ),
        name=f"backward_{layer}",
    )(ids, mods, *tensors)


def embed_lead(steps, width):
    half = width // 2
    freq = jnp.exp(-math.log(10000.0) * jnp.arange(half, dtype=F32) / half)
    angle = 6.0 * steps.astype(F32)[:, None] * freq[None, :]
    return jnp.concatenate([jnp.sin(angle), jnp.cos(angle)], -1)


def over_core(value):
    return lax.ppermute(value, "batch", [(i, i ^ 1) for i in range(8)])


def over_z(value, away):
    return lax.ppermute(value, "batch", [(i, i ^ (2 * away)) for i in range(8)])


def over_section(value, away):
    return lax.ppermute(value, "section", [(i, i ^ away) for i in range(4)])


def after(value, *others):
    return lax.optimization_barrier((value,) + others)[0]


def gather_shards(w, small, exchange):
    x0, y0, z1 = over_section(w, 1), over_section(w, 2), over_z(w, 1)
    z2 = over_z(w, 2)
    z1, small = lax.optimization_barrier((z1, small))
    small = lax.all_to_all(small, BOTH, 0, 0, tiled=True)
    x1, y1 = over_section(z1, 1), over_section(z1, 2)
    z3 = over_z(z2, 1)
    p0, q0 = over_section(y0[:6], 1), over_section(x0[6:], 2)
    x1, small = lax.optimization_barrier((x1, small))
    part = exchange(small)
    x2, y2 = over_section(z2, 1), over_section(z2, 2)
    p1, q1 = over_section(y1[:6], 1), over_section(x1[6:], 2)
    x3, y3 = over_section(z3, 1), over_section(z3, 2)
    p2, q2 = over_section(y2[:6], 1), over_section(x2[6:], 2)
    x3, part = lax.optimization_barrier((x3, part))
    p3, q3 = over_section(y3[:6], 1), over_section(x3[6:], 2)
    names = {}
    for zx, group in enumerate(
        [(w, x0, y0, p0, q0), (z1, x1, y1, p1, q1), (z2, x2, y2, p2, q2), (z3, x3, y3, p3, q3)]
    ):
        names[0, zx], names[1, zx], names[2, zx] = [(group[0], 0)], [(group[1], 0)], [(group[2], 0)]
        names[3, zx] = [(group[3], 0), (group[4], 6)]
    sources, plan = [], {}
    for keys in (
        [(0, 0), (0, 1), (1, 0), (2, 0), (1, 1), (2, 1), (3, 0)],
        [(0, 2), (0, 3), (3, 1), (1, 2), (2, 2)],
        [(1, 3), (2, 3), (3, 2), (3, 3)],
    ):
        bundle = []
        for key in keys:
            plan[key + (0,)], plan[key + (1,)] = [], []
            for array, low in names[key]:
                plan[key + (0,)].append((len(sources), low, 0))
                sources.append(array)
                bundle.append((key, array, low))
        other = over_core(jnp.concatenate([array for _, array, _ in bundle]))
        start = 0
        for key, array, low in bundle:
            plan[key + (1,)].append((len(sources), low, start))
            start += array.shape[0]
        sources.append(other)
    final = {}
    for key, parts in plan.items():
        final[key] = []
        for index, low, start in parts:
            high = BLOCKS if key[0] != 3 else low + 6
            final[key].append((index, start, low, high))
    return final, sources, small, part


def sum_shards(parts, vec):
    def add(*values):
        total = values[0].astype(F32)
        for value in values[1:]:
            total = total + value.astype(F32)
        return total

    def joined(zx, p, q):
        left = jnp.concatenate([parts[1, zx][:6], add(parts[1, zx][6:], q).astype(BF)])
        right = jnp.concatenate([add(parts[2, zx][:6], p).astype(BF), parts[2, zx][6:]])
        return left, right

    p3, q3 = over_section(parts[3, 3][:6], 1), over_section(parts[3, 3][6:], 2)
    d2, d1 = over_section(parts[3, 2], 1), over_section(parts[3, 1], 2)
    left, right = joined(3, p3, q3)
    x3, y3 = over_section(left, 1), over_section(right, 2)
    p0, q0 = over_section(parts[3, 0][:6], 1), over_section(parts[3, 0][6:], 2)
    left, right = parts[1, 2], add(parts[2, 2], d2).astype(BF)
    x3, vec = lax.optimization_barrier((x3, vec))
    vec = lax.all_to_all(vec, BOTH, 0, 0, tiled=True)
    total = add(parts[0, 3], x3, y3).astype(BF)
    left, right, total = lax.optimization_barrier((left, right, total))
    z3 = over_z(total, 1)
    x2, y2 = over_section(left, 1), over_section(right, 2)
    left, right = add(parts[1, 1], d1).astype(BF), parts[2, 1]
    total = add(parts[0, 2], x2, y2, z3).astype(BF)
    left, right, total = lax.optimization_barrier((left, right, total))
    z2, s2 = over_z(total[:6], 2), over_z(total[6:], 2)
    x1, y1 = over_section(left, 1), over_section(right, 2)
    left, right = joined(0, p0, q0)
    total = add(parts[0, 1], x1, y1).astype(BF)
    left, right, total, z2 = lax.optimization_barrier((left, right, total, z2))
    x0, y0 = over_section(left, 1), over_section(right, 2)
    z1 = over_z(total, 1)
    return unpacked(parts[0, 0], x0, y0, z1, z2, s2), vec


def body_permuted(
    tokens, levels, lead, w_qkv, w_o, b_o, w_up, b_up, w_down, b_down, w_ada, b_ada, cotangent
):
    section, batch = lax.axis_index("section"), lax.axis_index("batch")
    place, core = batch // 2, batch % 2
    width = tokens.shape[2]
    rows = width // SHARDS
    ids = jnp.stack([section, place, core, levels[0]]).astype(jnp.int32)
    shard, small = packed(lead, w_qkv, w_o, w_up, w_down, b_o, b_up, b_down)
    mine = []

    def exchange(smalls):
        conds = jax.nn.silu(embed_lead(smalls[:, 4, 0], width))
        mine.append(lax.dynamic_slice_in_dim(conds, batch * rows, rows, axis=1))
        part = jnp.dot(mine[0], w_ada[0].astype(F32), precision=HIGH)
        bias = jnp.zeros((6 * width,), F32)
        bias = lax.dynamic_update_slice_in_dim(
            bias, b_ada[0].astype(F32), batch * 6 * rows, axis=0
        )
        return lax.all_to_all((part + bias).reshape(32, -1, 128), BOTH, 0, 0, tiled=True)

    plan, sources, smalls, part = gather_shards(shard, small, exchange)
    mine = mine[0]
    mods = jnp.sum(part.reshape(4, SHARDS, -1, 128), axis=1).reshape(4, 6, width)
    vectors = smalls.reshape(4, SHARDS, 16 * 128).astype(F32)
    biases = jnp.concatenate(
        [
            vectors[:, :, :rows].reshape(4, 1, width),
            vectors[:, :, 128 : 128 + 4 * rows].reshape(4, 4, width),
            vectors[:, :, 384 : 384 + rows].reshape(4, 1, width),
        ],
        axis=1,
    )

    result, w, *saved = forward(plan, sources, ids, tokens, mods, biases)
    grad = cotangent
    sums = jnp.zeros((4, 4, BLOCKS, rows, width), BF)
    vecs = [None] * 4
    for layer in reversed(range(4)):
        grad, kept, sent, vecs[layer] = backward(layer, ids, grad, mods, w, saved)
        both = (kept.astype(F32) + over_core(sent).astype(F32)).astype(BF)
        sums = lax.dynamic_update_index_in_dim(sums, both, section ^ layer, 0)
    vec = jnp.broadcast_to(jnp.stack(vecs)[:, None], (4, SHARDS, 48, 128)).reshape(32, 48, 128)
    totals, vec = sum_shards({(i, j): sums[i, j] for i in range(4) for j in range(4)}, vec)
    vec = vec[:, :36].astype(F32).reshape(32, 12, width)
    g_ada = jnp.dot(mine.T, vec[:, :6].reshape(32, 6 * width), precision=HIGH)[None]
    flat = jnp.sum(vec, 0)

    def slot(low, high, count):
        return lax.dynamic_slice_in_dim(
            flat[low:high].reshape(-1), batch * count, count, axis=0
        )[None]

    return (
        result,
        grad,
        totals[0],
        totals[1],
        slot(6, 7, rows),
        totals[2],
        slot(7, 11, 4 * rows),
        totals[3],
        slot(11, 12, rows),
        g_ada,
        slot(0, 6, 6 * rows),
    )


def pack_kernel(lead, w_qkv, w_o, w_up, w_down, b_o, b_up, b_down, out, small):
    _, rows, width = w_o.shape
    for j in range(3):
        out[j] = w_qkv[0, :, j * width : (j + 1) * width]
    out[3] = w_o[0]
    for j in range(4):
        out[4 + j] = w_up[0, :, j * width : (j + 1) * width]
        out[8 + j] = w_down[0, j * rows : (j + 1) * rows]
    small[...] = jnp.full(small.shape, lead[0].astype(F32), F32).astype(BF)
    peers = small.shape[0]
    for row, bias in zip((0, 1, 3), (b_o, b_up, b_down)):
        count = bias.shape[1]
        for start in range(0, count, 128):
            size = min(128, count - start)
            value = bias[0, start : start + size].astype(F32).reshape(1, 1, size)
            at = row + start // 128
            small[:, at : at + 1, :size] = jnp.broadcast_to(value, (peers, 1, size)).astype(BF)


def packed(lead, w_qkv, w_o, w_up, w_down, b_o, b_up, b_down):
    _, rows, width = w_o.shape
    vmem = pl.BlockSpec(memory_space=pltpu.VMEM)
    return pl.pallas_call(
        pack_kernel,
        in_specs=[pl.BlockSpec(memory_space=pltpu.SMEM)] + [vmem] * 7,
        out_shape=[
            jax.ShapeDtypeStruct((BLOCKS, rows, width), BF),
            jax.ShapeDtypeStruct((32, 16, 128), BF),
        ],
        name="pack",
    )(lead, w_qkv, w_o, w_up, w_down, b_o, b_up, b_down)


def unpack_kernel(own, x, y, z, low, high, g_qkv, g_o, g_up, g_down):
    _, rows, width = g_o.shape
    for j in range(BLOCKS):
        last = low[j] if j < 6 else high[j - 6]
        total = own[j].astype(F32) + x[j].astype(F32) + y[j].astype(F32)
        total = total + z[j].astype(F32) + last.astype(F32)
        if j < 3:
            g_qkv[0, :, j * width : (j + 1) * width] = total
        elif j == 3:
            g_o[0] = total
        elif j < 8:
            g_up[0, :, (j - 4) * width : (j - 3) * width] = total
        else:
            g_down[0, (j - 8) * rows : (j - 7) * rows] = total


def unpacked(own, x, y, z, low, high):
    _, rows, width = own.shape
    return pl.pallas_call(
        unpack_kernel,
        out_shape=[
            jax.ShapeDtypeStruct((1, rows, 3 * width), F32),
            jax.ShapeDtypeStruct((1, rows, width), F32),
            jax.ShapeDtypeStruct((1, rows, 4 * width), F32),
            jax.ShapeDtypeStruct((1, 4 * rows, width), F32),
        ],
        name="unpack",
    )(own, x, y, z, low, high)


def local_shard(w_qkv, w_o, w_up, w_down):
    _, rows, width = w_o.shape

    def blocks_of(piece):
        return jnp.stack(jnp.split(piece, piece.shape[1] // width, axis=1))

    return jnp.concatenate(
        [blocks_of(w_qkv[0]), w_o, blocks_of(w_up[0]), w_down[0].reshape(4, rows, width)]
    )


def body_general(
    tokens, levels, lead, w_qkv, w_o, b_o, w_up, b_up, w_down, b_down, w_ada, b_ada, cotangent
):
    batch = lax.axis_index("batch")
    sections, batches = lax.axis_size("section"), lax.axis_size("batch")
    width = tokens.shape[2]
    rows, tall = width // batches, width // SHARDS
    zero = jnp.zeros((), jnp.int32)
    ids = jnp.stack([zero, zero, zero, levels[0]])

    shards = lax.all_gather(local_shard(w_qkv, w_o, w_up, w_down), BOTH, axis=0, tiled=False)
    shards = shards.reshape(sections, batches, BLOCKS, rows, width)
    front = jnp.swapaxes(shards[:, :, :8], 1, 2).reshape(sections, 8, SHARDS, tall, width)
    downs = shards[:, :, 8:].reshape(sections, SHARDS, 4, tall, width)
    source = jnp.concatenate([jnp.swapaxes(front, 1, 2), downs], axis=2)
    source = source.reshape(sections * SHARDS * BLOCKS, tall, width)
    plan = {
        (l, z, c): [(0, ((l * 4 + z) * 2 + c) * BLOCKS, 0, BLOCKS)]
        for l in range(4)
        for z in range(4)
        for c in range(2)
    }
    small = jnp.concatenate([b_o[0], b_up[0], b_down[0]])
    smalls = lax.all_gather(small, BOTH, axis=0, tiled=False).reshape(sections, batches, -1)
    smalls = smalls.astype(F32)
    biases = jnp.concatenate(
        [
            smalls[:, :, :rows].reshape(sections, 1, width),
            smalls[:, :, rows : 5 * rows].reshape(sections, 4, width),
            smalls[:, :, 5 * rows :].reshape(sections, 1, width),
        ],
        axis=1,
    )
    leads = lax.all_gather(lead, BOTH, axis=0, tiled=True)
    conds = jax.nn.silu(embed_lead(leads, width))
    mine = lax.dynamic_slice_in_dim(conds, batch * rows, rows, axis=1)
    part = jnp.dot(mine, w_ada[0].astype(F32), precision=HIGH)
    bias = jnp.zeros((6 * width,), F32)
    bias = lax.dynamic_update_slice_in_dim(
        bias, b_ada[0].astype(F32), batch * 6 * rows, axis=0
    )
    part = (part + bias).reshape(sections, batches, 6 * width)
    part = lax.psum_scatter(part, "batch", scatter_dimension=1, tiled=True)
    mods = lax.all_to_all(part[:, 0], "section", 0, 0, tiled=True)
    mods = mods.reshape(sections, 6, width)

    result, w, *saved = forward(plan, [source], ids, tokens, mods, biases)
    grad = cotangent
    grads, vecs = [None] * sections, [None] * sections
    for layer in reversed(range(sections)):
        grad, kept, sent, vecs[layer] = backward(layer, ids, grad, mods, w, saved)
        grads[layer] = jnp.stack([kept, sent], axis=1).reshape(SHARDS, BLOCKS, tall, width)
    grads = jnp.stack(grads)
    front = jnp.swapaxes(grads[:, :, :8], 1, 2).reshape(sections, 8, batches, rows, width)
    downs = grads[:, :, 8:].reshape(sections, batches, 4, rows, width)
    total = jnp.concatenate([jnp.swapaxes(front, 1, 2), downs], axis=2)
    total = total.reshape(sections, batches, BLOCKS * rows, width)
    total = lax.psum_scatter(total, "section", scatter_dimension=0, tiled=True)
    total = lax.psum_scatter(total, "batch", scatter_dimension=1, tiled=True)
    total = total.astype(F32).reshape(BLOCKS, rows, width)

    vec = jnp.stack(vecs)[:, :36].reshape(sections, 12, width)
    vec = lax.all_to_all(vec, "section", 0, 0, tiled=True)
    vec = lax.all_gather(vec, "batch", axis=1, tiled=False).astype(F32)
    vec = vec.reshape(sections * batches, 12, width)
    g_ada = jnp.dot(mine.T, vec[:, :6].reshape(-1, 6 * width), precision=HIGH)[None]
    flat = jnp.sum(vec, 0)

    def slot(low, high, count):
        return lax.dynamic_slice_in_dim(
            flat[low:high].reshape(-1), batch * count, count, axis=0
        )[None]

    return (
        result,
        grad,
        jnp.concatenate([total[0], total[1], total[2]], axis=1)[None],
        total[3][None],
        slot(6, 7, rows),
        jnp.concatenate([total[4 + j] for j in range(4)], axis=1)[None],
        slot(7, 11, 4 * rows),
        total[8:].reshape(1, 4 * rows, width),
        slot(11, 12, rows),
        g_ada,
        slot(0, 6, 6 * rows),
    )


def solution(mesh):
    in_specs = (
        P(("section", "batch"), None, None),
        P(("section", "batch")),
        P(("section", "batch")),
        P("section", "batch", None),
        P("section", "batch", None),
        P("section", "batch"),
        P("section", "batch", None),
        P("section", "batch"),
        P("section", "batch", None),
        P("section", "batch"),
        P("section", "batch", None),
        P("section", "batch"),
        P(("section", "batch"), None, None),
    )
    out_specs = (
        P(("section", "batch"), None, None),
        P(("section", "batch"), None, None),
        P("section", "batch", None),
        P("section", "batch", None),
        P("section", "batch"),
        P("section", "batch", None),
        P("section", "batch"),
        P("section", "batch", None),
        P("section", "batch"),
        P("section", "batch", None),
        P("section", "batch"),
    )
    permuted = mesh.shape["section"] == 4 and mesh.shape["batch"] == SHARDS
    body = body_permuted if permuted else body_general
    return jax.shard_map(body, mesh=mesh, in_specs=in_specs, out_specs=out_specs, check_vma=False)
```

```python
import functools
import math

import jax
import jax.numpy as jnp
from jax import lax
from jax.experimental import pallas as pl
from jax.experimental.pallas import tpu as pltpu
from jax.sharding import PartitionSpec as P

HEADS = 6
LEVELS = 13
BLOCKS = 12
SHARDS = 8
EPS = 1e-06
NEG = -1e30
BF = jnp.bfloat16
F32 = jnp.float32
HIGH = lax.Precision.HIGHEST
BOTH = ("section", "batch")
C0 = math.sqrt(2.0 / math.pi)
C1 = 0.044715
VMEM_LIMIT = 60 * 2**20


def dot(left, right, over=(1, 0)):
    return lax.dot_general(
        left, right, (((over[0],), (over[1],)), ((), ())), preferred_element_type=F32
    )


def standard(value):
    centered = value - jnp.mean(value, -1, keepdims=True)
    rstd = lax.rsqrt(jnp.mean(centered * centered, -1, keepdims=True) + EPS)
    return centered * rstd, rstd


def standard_back(grad, normed, rstd):
    return rstd * (
        grad
        - jnp.mean(grad, -1, keepdims=True)
        - normed * jnp.mean(grad * normed, -1, keepdims=True)
    )


def forward_kernel(plan, ids, tokens, mods, biases, *refs):
    count = len({part[0] for parts in plan.values() for part in parts})
    sources, refs = refs[:count], refs[count:]
    result, w_out, outs, held = refs[0], refs[1], refs[2:10], refs[10:18]
    value, hidden, acc, w, in_sem, out_sem, save_sem = refs[18:]
    layer = pl.program_id(0)
    layers = pl.num_programs(0)
    seq, width = value.shape
    size = width // HEADS
    section, place, core = ids[0], ids[1], ids[2]

    @pl.when(layer == 0)
    def _():
        value[...] = tokens[0]

        @pl.loop(0, layers)
        def _(target):
            for away in range(4):

                @pl.when(jnp.bitwise_xor(section, target) == away)
                def _():
                    for (sx, zx, cx), parts in plan.items():
                        if sx != away:
                            continue
                        shard = 2 * jnp.bitwise_xor(place, zx) + jnp.bitwise_xor(core, cx)
                        for index, lead, low, high in parts:
                            ref = sources[index]
                            top = min(high, 8)
                            if low < top:
                                pltpu.make_async_copy(
                                    ref.at[pl.ds(lead, top - low)],
                                    w.at[target, pl.ds(low, top - low), shard],
                                    in_sem.at[target],
                                ).start()
                            if high > 8:
                                pltpu.make_async_copy(
                                    ref.at[pl.ds(lead + 8 - low, 4)],
                                    w.at[target, 8 + shard // 2, pl.ds(4 * (shard % 2), 4)],
                                    in_sem.at[target],
                                ).start()

    pltpu.make_async_copy(w.at[layer], w.at[layer], in_sem.at[layer]).wait()
    pltpu.make_async_copy(w.at[layer], w_out.at[layer], out_sem.at[layer]).start()

    slot = layer % 2
    xs, qkv, probs, mixed, branch_a, act, slope, branch_b = (ref.at[slot] for ref in held)

    def saving(i, half, target):
        return pltpu.make_async_copy(held[i].at[half], outs[i].at[target], save_sem.at[i, half])

    def reuse(*which):
        @pl.when(layer >= 2)
        def _():
            for i in which:
                saving(i, slot, layer).wait()

    def save(*which):
        for i in which:
            saving(i, slot, layer).start()

    def weight(j):
        return w[layer, j].reshape(width, width)

    def weights(low, high):
        return jnp.concatenate([weight(j) for j in range(low, high)], axis=1)

    mod = mods[layer]
    bias = biases[layer]
    reuse(*range(8))
    xs[...] = value[...]
    save(0)
    x = value[...].astype(F32)
    normed, _ = standard(x)
    hidden[...] = (normed * (1.0 + mod[1:2]) + mod[0:1]).astype(BF)
    qkv[...] = dot(hidden[...], weights(0, 3)).astype(BF)
    save(1)
    limit = ids[3] * (seq // LEVELS)
    row = lax.broadcasted_iota(jnp.int32, (seq, 1), 0)
    mask = jnp.where(row < limit, 0.0, NEG)
    def score(h):
        q = qkv[:, h * size : (h + 1) * size] * (size**-0.5)
        k = qkv[:, width + h * size : width + (h + 1) * size]
        return dot(k, q, (1, 1)) + mask

    def attend(h, raw):
        top = jnp.max(raw, axis=0, keepdims=True)
        e = jnp.exp(raw - top)
        p = (e * (1.0 / jnp.sum(e, axis=0, keepdims=True))).astype(BF)
        probs[h] = p
        return p

    def mix(h, p):
        v = qkv[:, 2 * width + h * size : 2 * width + (h + 1) * size]
        mixed[h * size : (h + 1) * size, :] = dot(v, p, (0, 0)).astype(BF)

    raws = {h: score(h) for h in range(2)}
    held_p = None
    for h in range(HEADS):
        if h + 2 < HEADS:
            raws[h + 2] = score(h + 2)
        p = attend(h, raws.pop(h))
        if held_p is not None:
            mix(h - 1, held_p)
        held_p = p
    mix(HEADS - 1, held_p)
    save(2, 3)
    ba = dot(mixed[...], weight(3), (0, 0)) + bias[0:1]
    branch_a[...] = ba
    save(4)
    middle = value[...].astype(F32) + mod[2:3] * ba
    acc[...] = middle
    normed, _ = standard(middle)
    hidden[...] = (normed * (1.0 + mod[4:5]) + mod[3:4]).astype(BF)
    for j in range(0, 4, 2):
        cols = slice(j * width, (j + 2) * width)
        shift = jnp.concatenate([bias[1 + i : 2 + i] for i in range(j, j + 2)], axis=1)
        pre = dot(hidden[...], weights(4 + j, 4 + j + 2)) + shift
        square = pre * pre
        t = jnp.tanh(pre * (C0 + (C0 * C1) * square))
        half = 0.5 + 0.5 * t
        a = pre * half
        slope[:, cols] = (half + a * (1.0 - t) * (C0 + (3.0 * C0 * C1) * square)).astype(BF)
        act[:, cols] = a.astype(BF)
    save(5, 6)
    bb = dot(act[...], w[layer, 8:12].reshape(4 * width, width)) + bias[5:6]
    branch_b[...] = bb.astype(BF)
    save(7)
    out = (acc[...] + mod[5:6] * bb).astype(BF)
    value[...] = out
    result[0] = out

    @pl.when(layer == layers - 1)
    def _():
        for i in range(8):
            for half in range(2):
                saving(i, half, layer).wait()

        @pl.loop(0, layers)
        def _(target):
            pltpu.make_async_copy(w.at[target], w_out.at[target], out_sem.at[target]).wait()


def forward(plan, sources, ids, tokens, mods, biases):
    layers = mods.shape[0]
    _, seq, width = tokens.shape
    rows = width // SHARDS

    def same(*shape):
        return pl.BlockSpec(shape, lambda l: (0,) * len(shape))

    shapes = [
        ((seq, width), BF),
        ((seq, 3 * width), BF),
        ((HEADS, seq, seq), BF),
        ((width, seq), BF),
        ((seq, width), F32),
        ((seq, 4 * width), BF),
        ((seq, 4 * width), BF),
        ((seq, width), BF),
    ]
    hbm = pl.BlockSpec(memory_space=pl.ANY)
    return pl.pallas_call(
        functools.partial(forward_kernel, plan),
        grid=(layers,),
        in_specs=[
            pl.BlockSpec(memory_space=pltpu.SMEM),
            same(1, seq, width),
            same(layers, 6, width),
            same(layers, 6, width),
        ]
        + [hbm] * len(sources),
        out_specs=[same(1, seq, width), hbm] + [hbm] * len(shapes),
        out_shape=[
            jax.ShapeDtypeStruct((1, seq, width), BF),
            jax.ShapeDtypeStruct((layers, BLOCKS, SHARDS, rows, width), BF),
        ]
        + [jax.ShapeDtypeStruct((layers,) + s, d) for s, d in shapes],
        scratch_shapes=[pltpu.VMEM((2,) + s, d) for s, d in shapes]
        + [
            pltpu.VMEM((seq, width), BF),
            pltpu.VMEM((seq, width), BF),
            pltpu.VMEM((seq, width), F32),
            pltpu.VMEM((layers, BLOCKS, SHARDS, rows, width), BF),
            pltpu.SemaphoreType.DMA((layers,)),
            pltpu.SemaphoreType.DMA((layers,)),
            pltpu.SemaphoreType.DMA((len(shapes), 2)),
        ],
        compiler_params=pltpu.CompilerParams(vmem_limit_bytes=VMEM_LIMIT),
        cost_estimate=pl.CostEstimate(
            flops=layers * 1_740_000_000, bytes_accessed=80_000_000, transcendentals=0
        ),
        name="forward",
    )(ids, tokens, mods, biases, *sources)


def backward_kernel(layer, ids, mods, *refs):
    tensors, refs = refs[:10], refs[10:]
    grad_in, kept, sent, vec_out, gbb, hid, gsum, gmix, gqkv, gpre, dqt, halves = refs[:12]
    held, vec, in_sem, out_sem = refs[12:22], refs[22], refs[23], refs[24]
    grad, w, xs, qkv, probs, mixed, branch_a, act, slope, branch_b = held
    seq, width = gbb.shape
    size = width // HEADS
    place, core = ids[1], ids[2]
    rows = width // SHARDS
    names = ("grad", "w", "xs", "qkv", "probs", "mixed", "branch_a", "act", "slope", "branch_b")
    pieces = {}
    for name, far, near in zip(names, tensors, held):
        far = far.at[0] if name == "grad" else far.at[layer]
        if name == "w":
            for low, high in ((8, 12), (4, 8), (3, 4), (0, 3)):
                cut = pl.ds(low, high - low)
                pieces[name, low] = (far.at[cut], near.at[cut])
        else:
            pieces[name] = (far, near)
    order = (
        "grad", "branch_b", "act", "xs", "branch_a", ("w", 8), "slope",
        ("w", 4), ("w", 3), "mixed", "qkv", "probs", ("w", 0),
    )
    loads = {
        name: pltpu.make_async_copy(*pieces[name], in_sem.at[i]) for i, name in enumerate(order)
    }
    for name in order:
        loads[name].start()

    def ready(*names):
        for name in names:
            loads[name].wait()

    def weight(j):
        return w[j].reshape(width, width)

    def keep(shard, block, value):
        half = jnp.bitwise_xor(core, shard % 2)
        halves[half, jnp.bitwise_xor(place, shard // 2), block] = value

    def keep_front(block, value):
        for shard in range(SHARDS):
            keep(shard, block, value[shard * rows : (shard + 1) * rows])

    def keep_down(j, value):
        for part in range(SHARDS):
            keep(2 * j + part // 4, 8 + part % 4, value[part * rows : (part + 1) * rows])

    def put(row, value):
        for part in range(width // 128):
            at = row * (width // 128) + part
            vec[at : at + 1] = value[:, part * 128 : (part + 1) * 128]

    stores = []

    def store(low, high):
        cut = pl.ds(low, high - low)
        for half, out in ((1, sent), (0, kept)):
            copy = pltpu.make_async_copy(
                halves.at[half, :, cut], out.at[:, cut], out_sem.at[len(stores)]
            )
            copy.start()
            stores.append(copy)

    mod = mods[layer]
    shift_a, scale_a, gate_a, shift_b, scale_b, gate_b = (mod[i : i + 1] for i in range(6))
    vec[...] = jnp.zeros_like(vec)
    ready("grad", "branch_b")
    gout = grad[...].astype(F32)
    put(5, jnp.sum(gout * branch_b[...].astype(F32), 0, keepdims=True))
    gb = (gout * gate_b).astype(BF)
    gbb[...] = gb
    put(11, jnp.sum(gb.astype(F32), 0, keepdims=True))
    ready("act")
    for j in range(4):
        cols = slice(j * width, (j + 1) * width)
        keep_down(j, dot(act[:, cols], gbb[...], (0, 0)).astype(BF))
    ready("xs", "branch_a")
    x = xs[...].astype(F32)
    middle = x + gate_a * branch_a[...]
    normed_b, rstd_b = standard(middle)
    hid[...] = (normed_b * (1.0 + scale_b) + shift_b).astype(BF).T
    ready(("w", 8), "slope")
    for j in range(4):
        cols = slice(j * width, (j + 1) * width)
        gact = dot(gbb[...], weight(8 + j), (1, 1))
        g = (gact * slope[:, cols].astype(F32)).astype(BF)
        gpre[:, cols] = g
        put(7 + j, jnp.sum(g.astype(F32), 0, keepdims=True))
    for j in range(4):
        cols = slice(j * width, (j + 1) * width)
        keep_front(4 + j, dot(hid[...], gpre[:, cols]).astype(BF))
    store(4, 12)
    ready(("w", 4))
    ghb = dot(gpre[...], jnp.concatenate([weight(4 + j) for j in range(4)], axis=1), (1, 1))
    put(3, jnp.sum(ghb, 0, keepdims=True))
    put(4, jnp.sum(ghb * normed_b, 0, keepdims=True))
    gmid = gout + standard_back(ghb * (1.0 + scale_b), normed_b, rstd_b)
    gsum[...] = gmid
    put(2, jnp.sum(gmid * branch_a[...], 0, keepdims=True))
    gba = (gmid * gate_a).astype(BF)
    gbb[...] = gba
    put(6, jnp.sum(gba.astype(F32), 0, keepdims=True))
    ready(("w", 3), "mixed")
    gmix[...] = dot(gbb[...], weight(3), (1, 1)).astype(BF)
    keep_front(3, dot(mixed[...], gbb[...]).astype(BF))
    factor = size**-0.5
    ready("qkv", "probs")
    def part(i, h):
        return qkv[:, i * width + h * size : i * width + (h + 1) * size]

    def probe(h):
        return dot(part(2, h), gmix[:, h * size : (h + 1) * size], (1, 1))

    def finish(h, ds):
        gqkv[:, 2 * width + h * size : 2 * width + (h + 1) * size] = dot(
            probs[h], gmix[:, h * size : (h + 1) * size]
        ).astype(BF)
        gqkv[:, width + h * size : width + (h + 1) * size] = dot(ds, part(0, h)).astype(BF)
        dqt[h * size : (h + 1) * size, :] = dot(part(1, h), ds, (0, 0)).astype(BF)

    dps = {h: probe(h) for h in range(1)}
    waiting = []
    for h in range(HEADS):
        if h + 1 < HEADS:
            dps[h + 1] = probe(h + 1)
        pf = probs[h].astype(F32)
        dp = dps.pop(h)
        inner = jnp.sum(dp * pf, axis=0, keepdims=True)
        waiting.append((h, (pf * (dp - inner) * factor).astype(BF)))
        if len(waiting) > 0:
            finish(*waiting.pop(0))
    for item in waiting:
        finish(*item)
    gqkv[:, :width] = dqt[...].T
    normed_a, rstd_a = standard(xs[...].astype(F32))
    hid[...] = (normed_a * (1.0 + scale_a) + shift_a).astype(BF).T
    for j in range(3):
        cols = slice(j * width, (j + 1) * width)
        keep_front(j, dot(hid[...], gqkv[:, cols]).astype(BF))
    store(0, 4)
    ready(("w", 0))
    gha = dot(gqkv[...], jnp.concatenate([weight(j) for j in range(3)], axis=1), (1, 1))
    put(0, jnp.sum(gha, 0, keepdims=True))
    put(1, jnp.sum(gha * normed_a, 0, keepdims=True))
    grad_in[0] = (gsum[...] + standard_back(gha * (1.0 + scale_a), normed_a, rstd_a)).astype(BF)
    vec_out[...] = vec[...].astype(BF)
    for copy in stores:
        copy.wait()


def backward(layer, ids, grad, mods, w, saved):
    _, seq, width = grad.shape
    rows = width // SHARDS

    def full(*shape):
        return pl.BlockSpec(shape, lambda i: (0,) * len(shape))

    half = (SHARDS // 2, BLOCKS, rows, width)
    hbm = pl.BlockSpec(memory_space=pl.ANY)
    tensors = (grad, w, *saved)
    return pl.pallas_call(
        functools.partial(backward_kernel, layer),
        grid=(1,),
        in_specs=[pl.BlockSpec(memory_space=pltpu.SMEM), full(*mods.shape)] + [hbm] * len(tensors),
        out_specs=[full(1, seq, width), hbm, hbm, full(48, 128)],
        out_shape=[
            jax.ShapeDtypeStruct((1, seq, width), BF),
            jax.ShapeDtypeStruct(half, BF),
            jax.ShapeDtypeStruct(half, BF),
            jax.ShapeDtypeStruct((48, 128), BF),
        ],
        scratch_shapes=[
            pltpu.VMEM((seq, width), BF),
            pltpu.VMEM((width, seq), BF),
            pltpu.VMEM((seq, width), F32),
            pltpu.VMEM((seq, width), BF),
            pltpu.VMEM((seq, 3 * width), BF),
            pltpu.VMEM((seq, 4 * width), BF),
            pltpu.VMEM((width, seq), BF),
            pltpu.VMEM((2,) + half, BF),
        ]
        + [pltpu.VMEM(a.shape[1:], a.dtype) for a in tensors]
        + [
            pltpu.VMEM((48, 128), F32),
            pltpu.SemaphoreType.DMA((13,)),
            pltpu.SemaphoreType.DMA((4,)),
        ],
        compiler_params=pltpu.CompilerParams(vmem_limit_bytes=VMEM_LIMIT),
        cost_estimate=pl.CostEstimate(
            flops=3_480_000_000, bytes_accessed=20_000_000, transcendentals=0
        ),
        name=f"backward_{layer}",
    )(ids, mods, *tensors)


def embed_lead(steps, width):
    half = width // 2
    freq = jnp.exp(-math.log(10000.0) * jnp.arange(half, dtype=F32) / half)
    angle = 6.0 * steps.astype(F32)[:, None] * freq[None, :]
    return jnp.concatenate([jnp.sin(angle), jnp.cos(angle)], -1)


def over_core(value):
    return lax.ppermute(value, "batch", [(i, i ^ 1) for i in range(8)])


def over_z(value, away):
    return lax.ppermute(value, "batch", [(i, i ^ (2 * away)) for i in range(8)])


def over_section(value, away):
    return lax.ppermute(value, "section", [(i, i ^ away) for i in range(4)])


def after(value, *others):
    return lax.optimization_barrier((value,) + others)[0]


def gather_shards(w, small, exchange):
    x0, y0, z1 = over_section(w, 1), over_section(w, 2), over_z(w, 1)
    z2 = over_z(w, 2)
    small = lax.all_to_all(small, BOTH, 0, 0, tiled=True)
    x1, y1 = over_section(z1, 1), over_section(z1, 2)
    z3 = over_z(z2, 1)
    p0, q0 = over_section(y0[:6], 1), over_section(x0[6:], 2)
    x1, small = lax.optimization_barrier((x1, small))
    part = exchange(small)
    x2, y2 = over_section(z2, 1), over_section(z2, 2)
    p1, q1 = over_section(y1[:6], 1), over_section(x1[6:], 2)
    x3, y3 = over_section(z3, 1), over_section(z3, 2)
    p2, q2 = over_section(y2[:6], 1), over_section(x2[6:], 2)
    x3, part = lax.optimization_barrier((x3, part))
    p3, q3 = over_section(y3[:6], 1), over_section(x3[6:], 2)
    names = {}
    for zx, group in enumerate(
        [(w, x0, y0, p0, q0), (z1, x1, y1, p1, q1), (z2, x2, y2, p2, q2), (z3, x3, y3, p3, q3)]
    ):
        names[0, zx], names[1, zx], names[2, zx] = [(group[0], 0)], [(group[1], 0)], [(group[2], 0)]
        names[3, zx] = [(group[3], 0), (group[4], 6)]
    sources, plan = [], {}
    for keys in (
        [(0, 0), (0, 1), (1, 0), (2, 0), (1, 1), (2, 1), (3, 0)],
        [(0, 2), (0, 3), (3, 1), (1, 2), (2, 2)],
        [(1, 3), (2, 3), (3, 2), (3, 3)],
    ):
        bundle = []
        for key in keys:
            plan[key + (0,)], plan[key + (1,)] = [], []
            for array, low in names[key]:
                plan[key + (0,)].append((len(sources), low, 0))
                sources.append(array)
                bundle.append((key, array, low))
        other = over_core(jnp.concatenate([array for _, array, _ in bundle]))
        start = 0
        for key, array, low in bundle:
            plan[key + (1,)].append((len(sources), low, start))
            start += array.shape[0]
        sources.append(other)
    final = {}
    for key, parts in plan.items():
        final[key] = []
        for index, low, start in parts:
            high = BLOCKS if key[0] != 3 else low + 6
            final[key].append((index, start, low, high))
    return final, sources, small, part


def sum_shards(parts, vec):
    def add(*values):
        total = values[0].astype(F32)
        for value in values[1:]:
            total = total + value.astype(F32)
        return total

    def joined(zx, p, q):
        left = jnp.concatenate([parts[1, zx][:6], add(parts[1, zx][6:], q).astype(BF)])
        right = jnp.concatenate([add(parts[2, zx][:6], p).astype(BF), parts[2, zx][6:]])
        return left, right

    p3, q3 = over_section(parts[3, 3][:6], 1), over_section(parts[3, 3][6:], 2)
    d2, d1 = over_section(parts[3, 2], 1), over_section(parts[3, 1], 2)
    left, right = joined(3, p3, q3)
    x3, y3 = over_section(left, 1), over_section(right, 2)
    p0, q0 = over_section(parts[3, 0][:6], 1), over_section(parts[3, 0][6:], 2)
    left, right = parts[1, 2], add(parts[2, 2], d2).astype(BF)
    x3, vec = lax.optimization_barrier((x3, vec))
    vec = lax.all_to_all(vec, BOTH, 0, 0, tiled=True)
    total = add(parts[0, 3], x3, y3).astype(BF)
    left, right, total = lax.optimization_barrier((left, right, total))
    z3 = over_z(total, 1)
    x2, y2 = over_section(left, 1), over_section(right, 2)
    left, right = add(parts[1, 1], d1).astype(BF), parts[2, 1]
    total = add(parts[0, 2], x2, y2, z3).astype(BF)
    left, right, total = lax.optimization_barrier((left, right, total))
    z2, s2 = over_z(total[:6], 2), over_z(total[6:], 2)
    x1, y1 = over_section(left, 1), over_section(right, 2)
    left, right = joined(0, p0, q0)
    total = add(parts[0, 1], x1, y1).astype(BF)
    left, right, total, z2 = lax.optimization_barrier((left, right, total, z2))
    x0, y0 = over_section(left, 1), over_section(right, 2)
    z1 = over_z(total, 1)
    return unpacked(parts[0, 0], x0, y0, z1, z2, s2), vec


def body_permuted(
    tokens, levels, lead, w_qkv, w_o, b_o, w_up, b_up, w_down, b_down, w_ada, b_ada, cotangent
):
    section, batch = lax.axis_index("section"), lax.axis_index("batch")
    place, core = batch // 2, batch % 2
    width = tokens.shape[2]
    rows = width // SHARDS
    ids = jnp.stack([section, place, core, levels[0]]).astype(jnp.int32)
    shard, small = packed(lead, w_qkv, w_o, w_up, w_down, b_o, b_up, b_down)
    mine = []

    def exchange(smalls):
        conds = jax.nn.silu(embed_lead(smalls[:, 4, 0], width))
        mine.append(lax.dynamic_slice_in_dim(conds, batch * rows, rows, axis=1))
        part = jnp.dot(mine[0], w_ada[0].astype(F32), precision=HIGH)
        bias = jnp.zeros((6 * width,), F32)
        bias = lax.dynamic_update_slice_in_dim(
            bias, b_ada[0].astype(F32), batch * 6 * rows, axis=0
        )
        part = (part + bias).astype(BF).reshape(32, -1, 128)
        return lax.all_to_all(part, BOTH, 0, 0, tiled=True)

    plan, sources, smalls, part = gather_shards(shard, small, exchange)
    mine = mine[0]
    mods = jnp.sum(part.astype(F32).reshape(4, SHARDS, -1, 128), axis=1).reshape(4, 6, width)
    vectors = smalls.reshape(4, SHARDS, 16 * 128).astype(F32)
    biases = jnp.concatenate(
        [
            vectors[:, :, :rows].reshape(4, 1, width),
            vectors[:, :, 128 : 128 + 4 * rows].reshape(4, 4, width),
            vectors[:, :, 384 : 384 + rows].reshape(4, 1, width),
        ],
        axis=1,
    )

    result, w, *saved = forward(plan, sources, ids, tokens, mods, biases)
    grad = cotangent
    sums = jnp.zeros((4, 4, BLOCKS, rows, width), BF)
    vecs = [None] * 4
    for layer in reversed(range(4)):
        grad, kept, sent, vecs[layer] = backward(layer, ids, grad, mods, w, saved)
        both = (kept.astype(F32) + over_core(sent).astype(F32)).astype(BF)
        sums = lax.dynamic_update_index_in_dim(sums, both, section ^ layer, 0)
    vec = jnp.broadcast_to(jnp.stack(vecs)[:, None], (4, SHARDS, 48, 128)).reshape(32, 48, 128)
    totals, vec = sum_shards({(i, j): sums[i, j] for i in range(4) for j in range(4)}, vec)
    vec = vec[:, :36].astype(F32).reshape(32, 12, width)
    g_ada = jnp.dot(mine.T, vec[:, :6].reshape(32, 6 * width), precision=HIGH)[None]
    flat = jnp.sum(vec, 0)

    def slot(low, high, count):
        return lax.dynamic_slice_in_dim(
            flat[low:high].reshape(-1), batch * count, count, axis=0
        )[None]

    return (
        result,
        grad,
        totals[0],
        totals[1],
        slot(6, 7, rows),
        totals[2],
        slot(7, 11, 4 * rows),
        totals[3],
        slot(11, 12, rows),
        g_ada,
        slot(0, 6, 6 * rows),
    )


def pack_kernel(lead, w_qkv, w_o, w_up, w_down, b_o, b_up, b_down, out, small):
    _, rows, width = w_o.shape
    for j in range(3):
        out[j] = w_qkv[0, :, j * width : (j + 1) * width]
    out[3] = w_o[0]
    for j in range(4):
        out[4 + j] = w_up[0, :, j * width : (j + 1) * width]
        out[8 + j] = w_down[0, j * rows : (j + 1) * rows]
    small[...] = jnp.full(small.shape, lead[0].astype(F32), F32).astype(BF)
    peers = small.shape[0]
    for row, bias in zip((0, 1, 3), (b_o, b_up, b_down)):
        count = bias.shape[1]
        for start in range(0, count, 128):
            size = min(128, count - start)
            value = bias[0, start : start + size].astype(F32).reshape(1, 1, size)
            at = row + start // 128
            small[:, at : at + 1, :size] = jnp.broadcast_to(value, (peers, 1, size)).astype(BF)


def packed(lead, w_qkv, w_o, w_up, w_down, b_o, b_up, b_down):
    _, rows, width = w_o.shape
    vmem = pl.BlockSpec(memory_space=pltpu.VMEM)
    return pl.pallas_call(
        pack_kernel,
        in_specs=[pl.BlockSpec(memory_space=pltpu.SMEM)] + [vmem] * 7,
        out_shape=[
            jax.ShapeDtypeStruct((BLOCKS, rows, width), BF),
            jax.ShapeDtypeStruct((32, 16, 128), BF),
        ],
        name="pack",
    )(lead, w_qkv, w_o, w_up, w_down, b_o, b_up, b_down)


def unpack_kernel(own, x, y, z, low, high, g_qkv, g_o, g_up, g_down):
    _, rows, width = g_o.shape
    for j in range(BLOCKS):
        last = low[j] if j < 6 else high[j - 6]
        total = own[j].astype(F32) + x[j].astype(F32) + y[j].astype(F32)
        total = total + z[j].astype(F32) + last.astype(F32)
        if j < 3:
            g_qkv[0, :, j * width : (j + 1) * width] = total
        elif j == 3:
            g_o[0] = total
        elif j < 8:
            g_up[0, :, (j - 4) * width : (j - 3) * width] = total
        else:
            g_down[0, (j - 8) * rows : (j - 7) * rows] = total


def unpacked(own, x, y, z, low, high):
    _, rows, width = own.shape
    return pl.pallas_call(
        unpack_kernel,
        out_shape=[
            jax.ShapeDtypeStruct((1, rows, 3 * width), F32),
            jax.ShapeDtypeStruct((1, rows, width), F32),
            jax.ShapeDtypeStruct((1, rows, 4 * width), F32),
            jax.ShapeDtypeStruct((1, 4 * rows, width), F32),
        ],
        name="unpack",
    )(own, x, y, z, low, high)


def local_shard(w_qkv, w_o, w_up, w_down):
    _, rows, width = w_o.shape

    def blocks_of(piece):
        return jnp.stack(jnp.split(piece, piece.shape[1] // width, axis=1))

    return jnp.concatenate(
        [blocks_of(w_qkv[0]), w_o, blocks_of(w_up[0]), w_down[0].reshape(4, rows, width)]
    )


def body_general(
    tokens, levels, lead, w_qkv, w_o, b_o, w_up, b_up, w_down, b_down, w_ada, b_ada, cotangent
):
    batch = lax.axis_index("batch")
    sections, batches = lax.axis_size("section"), lax.axis_size("batch")
    width = tokens.shape[2]
    rows, tall = width // batches, width // SHARDS
    zero = jnp.zeros((), jnp.int32)
    ids = jnp.stack([zero, zero, zero, levels[0]])

    shards = lax.all_gather(local_shard(w_qkv, w_o, w_up, w_down), BOTH, axis=0, tiled=False)
    shards = shards.reshape(sections, batches, BLOCKS, rows, width)
    front = jnp.swapaxes(shards[:, :, :8], 1, 2).reshape(sections, 8, SHARDS, tall, width)
    downs = shards[:, :, 8:].reshape(sections, SHARDS, 4, tall, width)
    source = jnp.concatenate([jnp.swapaxes(front, 1, 2), downs], axis=2)
    source = source.reshape(sections * SHARDS * BLOCKS, tall, width)
    plan = {
        (l, z, c): [(0, ((l * 4 + z) * 2 + c) * BLOCKS, 0, BLOCKS)]
        for l in range(4)
        for z in range(4)
        for c in range(2)
    }
    small = jnp.concatenate([b_o[0], b_up[0], b_down[0]])
    smalls = lax.all_gather(small, BOTH, axis=0, tiled=False).reshape(sections, batches, -1)
    smalls = smalls.astype(F32)
    biases = jnp.concatenate(
        [
            smalls[:, :, :rows].reshape(sections, 1, width),
            smalls[:, :, rows : 5 * rows].reshape(sections, 4, width),
            smalls[:, :, 5 * rows :].reshape(sections, 1, width),
        ],
        axis=1,
    )
    leads = lax.all_gather(lead, BOTH, axis=0, tiled=True)
    conds = jax.nn.silu(embed_lead(leads, width))
    mine = lax.dynamic_slice_in_dim(conds, batch * rows, rows, axis=1)
    part = jnp.dot(mine, w_ada[0].astype(F32), precision=HIGH)
    bias = jnp.zeros((6 * width,), F32)
    bias = lax.dynamic_update_slice_in_dim(
        bias, b_ada[0].astype(F32), batch * 6 * rows, axis=0
    )
    part = (part + bias).reshape(sections, batches, 6 * width)
    part = lax.psum_scatter(part, "batch", scatter_dimension=1, tiled=True)
    mods = lax.all_to_all(part[:, 0], "section", 0, 0, tiled=True)
    mods = mods.reshape(sections, 6, width)

    result, w, *saved = forward(plan, [source], ids, tokens, mods, biases)
    grad = cotangent
    grads, vecs = [None] * sections, [None] * sections
    for layer in reversed(range(sections)):
        grad, kept, sent, vecs[layer] = backward(layer, ids, grad, mods, w, saved)
        grads[layer] = jnp.stack([kept, sent], axis=1).reshape(SHARDS, BLOCKS, tall, width)
    grads = jnp.stack(grads)
    front = jnp.swapaxes(grads[:, :, :8], 1, 2).reshape(sections, 8, batches, rows, width)
    downs = grads[:, :, 8:].reshape(sections, batches, 4, rows, width)
    total = jnp.concatenate([jnp.swapaxes(front, 1, 2), downs], axis=2)
    total = total.reshape(sections, batches, BLOCKS * rows, width)
    total = lax.psum_scatter(total, "section", scatter_dimension=0, tiled=True)
    total = lax.psum_scatter(total, "batch", scatter_dimension=1, tiled=True)
    total = total.astype(F32).reshape(BLOCKS, rows, width)

    vec = jnp.stack(vecs)[:, :36].reshape(sections, 12, width)
    vec = lax.all_to_all(vec, "section", 0, 0, tiled=True)
    vec = lax.all_gather(vec, "batch", axis=1, tiled=False).astype(F32)
    vec = vec.reshape(sections * batches, 12, width)
    g_ada = jnp.dot(mine.T, vec[:, :6].reshape(-1, 6 * width), precision=HIGH)[None]
    flat = jnp.sum(vec, 0)

    def slot(low, high, count):
        return lax.dynamic_slice_in_dim(
            flat[low:high].reshape(-1), batch * count, count, axis=0
        )[None]

    return (
        result,
        grad,
        jnp.concatenate([total[0], total[1], total[2]], axis=1)[None],
        total[3][None],
        slot(6, 7, rows),
        jnp.concatenate([total[4 + j] for j in range(4)], axis=1)[None],
        slot(7, 11, 4 * rows),
        total[8:].reshape(1, 4 * rows, width),
        slot(11, 12, rows),
        g_ada,
        slot(0, 6, 6 * rows),
    )


def solution(mesh):
    in_specs = (
        P(("section", "batch"), None, None),
        P(("section", "batch")),
        P(("section", "batch")),
        P("section", "batch", None),
        P("section", "batch", None),
        P("section", "batch"),
        P("section", "batch", None),
        P("section", "batch"),
        P("section", "batch", None),
        P("section", "batch"),
        P("section", "batch", None),
        P("section", "batch"),
        P(("section", "batch"), None, None),
    )
    out_specs = (
        P(("section", "batch"), None, None),
        P(("section", "batch"), None, None),
        P("section", "batch", None),
        P("section", "batch", None),
        P("section", "batch"),
        P("section", "batch", None),
        P("section", "batch"),
        P("section", "batch", None),
        P("section", "batch"),
        P("section", "batch", None),
        P("section", "batch"),
    )
    permuted = mesh.shape["section"] == 4 and mesh.shape["batch"] == SHARDS
    body = body_permuted if permuted else body_general
    return jax.shard_map(body, mesh=mesh, in_specs=in_specs, out_specs=out_specs, check_vma=False)
```

```python
import functools
import math

import jax
import jax.numpy as jnp
from jax import lax
from jax.experimental import pallas as pl
from jax.experimental.pallas import tpu as pltpu
from jax.sharding import PartitionSpec as P

HEADS = 6
LEVELS = 13
BLOCKS = 12
SHARDS = 8
EPS = 1e-06
NEG = -1e30
BF = jnp.bfloat16
F32 = jnp.float32
HIGH = lax.Precision.HIGHEST
BOTH = ("section", "batch")
C0 = math.sqrt(2.0 / math.pi)
C1 = 0.044715
VMEM_LIMIT = 60 * 2**20


def dot(left, right, over=(1, 0)):
    return lax.dot_general(
        left, right, (((over[0],), (over[1],)), ((), ())), preferred_element_type=F32
    )


def standard(value):
    centered = value - jnp.mean(value, -1, keepdims=True)
    rstd = lax.rsqrt(jnp.mean(centered * centered, -1, keepdims=True) + EPS)
    return centered * rstd, rstd


def standard_back(grad, normed, rstd):
    return rstd * (
        grad
        - jnp.mean(grad, -1, keepdims=True)
        - normed * jnp.mean(grad * normed, -1, keepdims=True)
    )


def forward_kernel(plan, ids, tokens, mods, biases, *refs):
    count = len({part[0] for parts in plan.values() for part in parts})
    sources, refs = refs[:count], refs[count:]
    result, w_out, outs, held = refs[0], refs[1], refs[2:10], refs[10:18]
    value, hidden, acc, w, in_sem, out_sem, save_sem = refs[18:]
    layer = pl.program_id(0)
    layers = pl.num_programs(0)
    seq, width = value.shape
    size = width // HEADS
    section, place, core = ids[0], ids[1], ids[2]

    @pl.when(layer == 0)
    def _():
        value[...] = tokens[0]

        @pl.loop(0, layers)
        def _(target):
            for away in range(4):

                @pl.when(jnp.bitwise_xor(section, target) == away)
                def _():
                    for (sx, zx, cx), parts in plan.items():
                        if sx != away:
                            continue
                        shard = 2 * jnp.bitwise_xor(place, zx) + jnp.bitwise_xor(core, cx)
                        for index, lead, low, high in parts:
                            ref = sources[index]
                            top = min(high, 8)
                            if low < top:
                                pltpu.make_async_copy(
                                    ref.at[pl.ds(lead, top - low)],
                                    w.at[target, pl.ds(low, top - low), shard],
                                    in_sem.at[target],
                                ).start()
                            if high > 8:
                                pltpu.make_async_copy(
                                    ref.at[pl.ds(lead + 8 - low, 4)],
                                    w.at[target, 8 + shard // 2, pl.ds(4 * (shard % 2), 4)],
                                    in_sem.at[target],
                                ).start()

    pltpu.make_async_copy(w.at[layer], w.at[layer], in_sem.at[layer]).wait()
    pltpu.make_async_copy(w.at[layer], w_out.at[layer], out_sem.at[layer]).start()

    slot = layer % 2
    xs, qkv, probs, mixed, branch_a, act, slope, branch_b = (ref.at[slot] for ref in held)

    def saving(i, half, target):
        return pltpu.make_async_copy(held[i].at[half], outs[i].at[target], save_sem.at[i, half])

    def reuse(*which):
        @pl.when(layer >= 2)
        def _():
            for i in which:
                saving(i, slot, layer).wait()

    def save(*which):
        for i in which:
            saving(i, slot, layer).start()

    def weight(j):
        return w[layer, j].reshape(width, width)

    def weights(low, high):
        return jnp.concatenate([weight(j) for j in range(low, high)], axis=1)

    mod = mods[layer]
    bias = biases[layer]
    reuse(*range(8))
    xs[...] = value[...]
    save(0)
    x = value[...].astype(F32)
    normed, _ = standard(x)
    hidden[...] = (normed * (1.0 + mod[1:2]) + mod[0:1]).astype(BF)
    qkv[...] = dot(hidden[...], weights(0, 3)).astype(BF)
    save(1)
    limit = ids[3] * (seq // LEVELS)
    row = lax.broadcasted_iota(jnp.int32, (seq, 1), 0)
    mask = jnp.where(row < limit, 0.0, NEG)
    def score(h):
        q = qkv[:, h * size : (h + 1) * size] * (size**-0.5)
        k = qkv[:, width + h * size : width + (h + 1) * size]
        return dot(k, q, (1, 1)) + mask

    def attend(h, raw):
        top = jnp.max(raw, axis=0, keepdims=True)
        e = jnp.exp(raw - top)
        p = (e * (1.0 / jnp.sum(e, axis=0, keepdims=True))).astype(BF)
        probs[h] = p
        return p

    def mix(h, p):
        v = qkv[:, 2 * width + h * size : 2 * width + (h + 1) * size]
        mixed[h * size : (h + 1) * size, :] = dot(v, p, (0, 0)).astype(BF)

    raws = {h: score(h) for h in range(2)}
    held_p = None
    for h in range(HEADS):
        if h + 2 < HEADS:
            raws[h + 2] = score(h + 2)
        p = attend(h, raws.pop(h))
        if held_p is not None:
            mix(h - 1, held_p)
        held_p = p
    mix(HEADS - 1, held_p)
    save(2, 3)
    ba = dot(mixed[...], weight(3), (0, 0)) + bias[0:1]
    branch_a[...] = ba
    save(4)
    middle = value[...].astype(F32) + mod[2:3] * ba
    acc[...] = middle
    normed, _ = standard(middle)
    hidden[...] = (normed * (1.0 + mod[4:5]) + mod[3:4]).astype(BF)
    for j in range(0, 4, 2):
        cols = slice(j * width, (j + 2) * width)
        shift = jnp.concatenate([bias[1 + i : 2 + i] for i in range(j, j + 2)], axis=1)
        pre = dot(hidden[...], weights(4 + j, 4 + j + 2)) + shift
        square = pre * pre
        t = jnp.tanh(pre * (C0 + (C0 * C1) * square))
        half = 0.5 + 0.5 * t
        a = pre * half
        slope[:, cols] = (half + a * (1.0 - t) * (C0 + (3.0 * C0 * C1) * square)).astype(BF)
        act[:, cols] = a.astype(BF)
    save(5, 6)
    bb = dot(act[...], w[layer, 8:12].reshape(4 * width, width)) + bias[5:6]
    branch_b[...] = bb.astype(BF)
    save(7)
    out = (acc[...] + mod[5:6] * bb).astype(BF)
    value[...] = out
    result[0] = out

    @pl.when(layer == layers - 1)
    def _():
        for i in range(8):
            for half in range(2):
                saving(i, half, layer).wait()

        @pl.loop(0, layers)
        def _(target):
            pltpu.make_async_copy(w.at[target], w_out.at[target], out_sem.at[target]).wait()


def forward(plan, sources, ids, tokens, mods, biases):
    layers = mods.shape[0]
    _, seq, width = tokens.shape
    rows = width // SHARDS

    def same(*shape):
        return pl.BlockSpec(shape, lambda l: (0,) * len(shape))

    shapes = [
        ((seq, width), BF),
        ((seq, 3 * width), BF),
        ((HEADS, seq, seq), BF),
        ((width, seq), BF),
        ((seq, width), F32),
        ((seq, 4 * width), BF),
        ((seq, 4 * width), BF),
        ((seq, width), BF),
    ]
    hbm = pl.BlockSpec(memory_space=pl.ANY)
    return pl.pallas_call(
        functools.partial(forward_kernel, plan),
        grid=(layers,),
        in_specs=[
            pl.BlockSpec(memory_space=pltpu.SMEM),
            same(1, seq, width),
            same(layers, 6, width),
            same(layers, 6, width),
        ]
        + [hbm] * len(sources),
        out_specs=[same(1, seq, width), hbm] + [hbm] * len(shapes),
        out_shape=[
            jax.ShapeDtypeStruct((1, seq, width), BF),
            jax.ShapeDtypeStruct((layers, BLOCKS, SHARDS, rows, width), BF),
        ]
        + [jax.ShapeDtypeStruct((layers,) + s, d) for s, d in shapes],
        scratch_shapes=[pltpu.VMEM((2,) + s, d) for s, d in shapes]
        + [
            pltpu.VMEM((seq, width), BF),
            pltpu.VMEM((seq, width), BF),
            pltpu.VMEM((seq, width), F32),
            pltpu.VMEM((layers, BLOCKS, SHARDS, rows, width), BF),
            pltpu.SemaphoreType.DMA((layers,)),
            pltpu.SemaphoreType.DMA((layers,)),
            pltpu.SemaphoreType.DMA((len(shapes), 2)),
        ],
        compiler_params=pltpu.CompilerParams(vmem_limit_bytes=VMEM_LIMIT),
        cost_estimate=pl.CostEstimate(
            flops=layers * 1_740_000_000, bytes_accessed=80_000_000, transcendentals=0
        ),
        name="forward",
    )(ids, tokens, mods, biases, *sources)


def backward_kernel(layer, ids, mods, *refs):
    tensors, refs = refs[:10], refs[10:]
    grad_in, kept, sent, vec_out, gbb, hid, gsum, gmix, gqkv, gpre, dqt, halves = refs[:12]
    held, vec, in_sem, out_sem = refs[12:22], refs[22], refs[23], refs[24]
    grad, w, xs, qkv, probs, mixed, branch_a, act, slope, branch_b = held
    seq, width = gbb.shape
    size = width // HEADS
    place, core = ids[1], ids[2]
    rows = width // SHARDS
    names = ("grad", "w", "xs", "qkv", "probs", "mixed", "branch_a", "act", "slope", "branch_b")
    pieces = {}
    for name, far, near in zip(names, tensors, held):
        far = far.at[0] if name == "grad" else far.at[layer]
        if name == "w":
            for low, high in ((8, 12), (4, 8), (3, 4), (0, 3)):
                cut = pl.ds(low, high - low)
                pieces[name, low] = (far.at[cut], near.at[cut])
        else:
            pieces[name] = (far, near)
    order = (
        "grad", "branch_b", "act", "xs", "branch_a", ("w", 8), "slope",
        ("w", 4), ("w", 3), "mixed", "qkv", "probs", ("w", 0),
    )
    loads = {
        name: pltpu.make_async_copy(*pieces[name], in_sem.at[i]) for i, name in enumerate(order)
    }
    for name in order:
        loads[name].start()

    def ready(*names):
        for name in names:
            loads[name].wait()

    def weight(j):
        return w[j].reshape(width, width)

    def keep(shard, block, value):
        half = jnp.bitwise_xor(core, shard % 2)
        halves[half, jnp.bitwise_xor(place, shard // 2), block] = value

    def keep_front(block, value):
        for shard in range(SHARDS):
            keep(shard, block, value[shard * rows : (shard + 1) * rows])

    def keep_down(j, value):
        for part in range(SHARDS):
            keep(2 * j + part // 4, 8 + part % 4, value[part * rows : (part + 1) * rows])

    def put(row, value):
        for part in range(width // 128):
            at = row * (width // 128) + part
            vec[at : at + 1] = value[:, part * 128 : (part + 1) * 128]

    stores = []

    def store(low, high):
        cut = pl.ds(low, high - low)
        for half, out in ((1, sent), (0, kept)):
            copy = pltpu.make_async_copy(
                halves.at[half, :, cut], out.at[:, cut], out_sem.at[len(stores)]
            )
            copy.start()
            stores.append(copy)

    mod = mods[layer]
    shift_a, scale_a, gate_a, shift_b, scale_b, gate_b = (mod[i : i + 1] for i in range(6))
    vec[...] = jnp.zeros_like(vec)
    ready("grad", "branch_b")
    gout = grad[...].astype(F32)
    put(5, jnp.sum(gout * branch_b[...].astype(F32), 0, keepdims=True))
    gb = (gout * gate_b).astype(BF)
    gbb[...] = gb
    put(11, jnp.sum(gb.astype(F32), 0, keepdims=True))
    ready("act")
    for j in range(4):
        cols = slice(j * width, (j + 1) * width)
        keep_down(j, dot(act[:, cols], gbb[...], (0, 0)).astype(BF))
    ready("xs", "branch_a")
    x = xs[...].astype(F32)
    middle = x + gate_a * branch_a[...]
    normed_b, rstd_b = standard(middle)
    hid[...] = (normed_b * (1.0 + scale_b) + shift_b).astype(BF).T
    ready(("w", 8), "slope")
    for j in range(4):
        cols = slice(j * width, (j + 1) * width)
        gact = dot(gbb[...], weight(8 + j), (1, 1))
        g = (gact * slope[:, cols].astype(F32)).astype(BF)
        gpre[:, cols] = g
        put(7 + j, jnp.sum(g.astype(F32), 0, keepdims=True))
    for j in range(4):
        cols = slice(j * width, (j + 1) * width)
        keep_front(4 + j, dot(hid[...], gpre[:, cols]).astype(BF))
    store(4, 12)
    ready(("w", 4))
    ghb = dot(gpre[...], jnp.concatenate([weight(4 + j) for j in range(4)], axis=1), (1, 1))
    put(3, jnp.sum(ghb, 0, keepdims=True))
    put(4, jnp.sum(ghb * normed_b, 0, keepdims=True))
    gmid = gout + standard_back(ghb * (1.0 + scale_b), normed_b, rstd_b)
    gsum[...] = gmid
    put(2, jnp.sum(gmid * branch_a[...], 0, keepdims=True))
    gba = (gmid * gate_a).astype(BF)
    gbb[...] = gba
    put(6, jnp.sum(gba.astype(F32), 0, keepdims=True))
    ready(("w", 3), "mixed")
    gmix[...] = dot(gbb[...], weight(3), (1, 1)).astype(BF)
    keep_front(3, dot(mixed[...], gbb[...]).astype(BF))
    factor = size**-0.5
    ready("qkv", "probs")
    def part(i, h):
        return qkv[:, i * width + h * size : i * width + (h + 1) * size]

    def probe(h):
        return dot(part(2, h), gmix[:, h * size : (h + 1) * size], (1, 1))

    def finish(h, ds):
        gqkv[:, 2 * width + h * size : 2 * width + (h + 1) * size] = dot(
            probs[h], gmix[:, h * size : (h + 1) * size]
        ).astype(BF)
        gqkv[:, width + h * size : width + (h + 1) * size] = dot(ds, part(0, h)).astype(BF)
        dqt[h * size : (h + 1) * size, :] = dot(part(1, h), ds, (0, 0)).astype(BF)

    dps = {h: probe(h) for h in range(1)}
    waiting = []
    for h in range(HEADS):
        if h + 1 < HEADS:
            dps[h + 1] = probe(h + 1)
        pf = probs[h].astype(F32)
        dp = dps.pop(h)
        inner = jnp.sum(dp * pf, axis=0, keepdims=True)
        waiting.append((h, (pf * (dp - inner) * factor).astype(BF)))
        if len(waiting) > 0:
            finish(*waiting.pop(0))
    for item in waiting:
        finish(*item)
    gqkv[:, :width] = dqt[...].T
    normed_a, rstd_a = standard(xs[...].astype(F32))
    hid[...] = (normed_a * (1.0 + scale_a) + shift_a).astype(BF).T
    for j in range(3):
        cols = slice(j * width, (j + 1) * width)
        keep_front(j, dot(hid[...], gqkv[:, cols]).astype(BF))
    store(0, 4)
    ready(("w", 0))
    gha = dot(gqkv[...], jnp.concatenate([weight(j) for j in range(3)], axis=1), (1, 1))
    put(0, jnp.sum(gha, 0, keepdims=True))
    put(1, jnp.sum(gha * normed_a, 0, keepdims=True))
    grad_in[0] = (gsum[...] + standard_back(gha * (1.0 + scale_a), normed_a, rstd_a)).astype(BF)
    vec_out[...] = vec[...].astype(BF)
    for copy in stores:
        copy.wait()


def backward(layer, ids, grad, mods, w, saved):
    _, seq, width = grad.shape
    rows = width // SHARDS

    def full(*shape):
        return pl.BlockSpec(shape, lambda i: (0,) * len(shape))

    half = (SHARDS // 2, BLOCKS, rows, width)
    hbm = pl.BlockSpec(memory_space=pl.ANY)
    tensors = (grad, w, *saved)
    return pl.pallas_call(
        functools.partial(backward_kernel, layer),
        grid=(1,),
        in_specs=[pl.BlockSpec(memory_space=pltpu.SMEM), full(*mods.shape)] + [hbm] * len(tensors),
        out_specs=[full(1, seq, width), hbm, hbm, full(48, 128)],
        out_shape=[
            jax.ShapeDtypeStruct((1, seq, width), BF),
            jax.ShapeDtypeStruct(half, BF),
            jax.ShapeDtypeStruct(half, BF),
            jax.ShapeDtypeStruct((48, 128), BF),
        ],
        scratch_shapes=[
            pltpu.VMEM((seq, width), BF),
            pltpu.VMEM((width, seq), BF),
            pltpu.VMEM((seq, width), F32),
            pltpu.VMEM((seq, width), BF),
            pltpu.VMEM((seq, 3 * width), BF),
            pltpu.VMEM((seq, 4 * width), BF),
            pltpu.VMEM((width, seq), BF),
            pltpu.VMEM((2,) + half, BF),
        ]
        + [pltpu.VMEM(a.shape[1:], a.dtype) for a in tensors]
        + [
            pltpu.VMEM((48, 128), F32),
            pltpu.SemaphoreType.DMA((13,)),
            pltpu.SemaphoreType.DMA((4,)),
        ],
        compiler_params=pltpu.CompilerParams(vmem_limit_bytes=VMEM_LIMIT),
        cost_estimate=pl.CostEstimate(
            flops=3_480_000_000, bytes_accessed=20_000_000, transcendentals=0
        ),
        name=f"backward_{layer}",
    )(ids, mods, *tensors)


def embed_lead(steps, width):
    half = width // 2
    freq = jnp.exp(-math.log(10000.0) * jnp.arange(half, dtype=F32) / half)
    angle = 6.0 * steps.astype(F32)[:, None] * freq[None, :]
    return jnp.concatenate([jnp.sin(angle), jnp.cos(angle)], -1)


def over_core(value):
    return lax.ppermute(value, "batch", [(i, i ^ 1) for i in range(8)])


def over_z(value, away):
    return lax.ppermute(value, "batch", [(i, i ^ (2 * away)) for i in range(8)])


def over_section(value, away):
    return lax.ppermute(value, "section", [(i, i ^ away) for i in range(4)])


def after(value, *others):
    return lax.optimization_barrier((value,) + others)[0]


def gather_shards(w, small, exchange):
    x0, y0, z1 = over_section(w, 1), over_section(w, 2), over_z(w, 1)
    z2 = over_z(w, 2)
    small = lax.all_to_all(small, BOTH, 0, 0, tiled=True)
    x1, y1 = over_section(z1, 1), over_section(z1, 2)
    z3 = over_z(z2, 1)
    p0, q0 = over_section(y0[:6], 1), over_section(x0[6:], 2)
    x1, small = lax.optimization_barrier((x1, small))
    part = exchange(small)
    x2, y2 = over_section(z2, 1), over_section(z2, 2)
    p1, q1 = over_section(y1[:6], 1), over_section(x1[6:], 2)
    x3, y3 = over_section(z3, 1), over_section(z3, 2)
    p2, q2 = over_section(y2[:6], 1), over_section(x2[6:], 2)
    x3, part = lax.optimization_barrier((x3, part))
    p3, q3 = over_section(y3[:6], 1), over_section(x3[6:], 2)
    names = {}
    for zx, group in enumerate(
        [(w, x0, y0, p0, q0), (z1, x1, y1, p1, q1), (z2, x2, y2, p2, q2), (z3, x3, y3, p3, q3)]
    ):
        names[0, zx], names[1, zx], names[2, zx] = [(group[0], 0)], [(group[1], 0)], [(group[2], 0)]
        names[3, zx] = [(group[3], 0), (group[4], 6)]
    sources, plan = [], {}
    for keys in (
        [(0, 0), (0, 1), (1, 0), (2, 0), (1, 1), (2, 1), (3, 0)],
        [(0, 2), (0, 3), (3, 1), (1, 2), (2, 2)],
        [(1, 3), (2, 3), (3, 2), (3, 3)],
    ):
        bundle = []
        for key in keys:
            plan[key + (0,)], plan[key + (1,)] = [], []
            for array, low in names[key]:
                plan[key + (0,)].append((len(sources), low, 0))
                sources.append(array)
                bundle.append((key, array, low))
        other = over_core(jnp.concatenate([array for _, array, _ in bundle]))
        start = 0
        for key, array, low in bundle:
            plan[key + (1,)].append((len(sources), low, start))
            start += array.shape[0]
        sources.append(other)
    final = {}
    for key, parts in plan.items():
        final[key] = []
        for index, low, start in parts:
            high = BLOCKS if key[0] != 3 else low + 6
            final[key].append((index, start, low, high))
    return final, sources, small, part


def sum_shards(parts, vec):
    def add(*values):
        total = values[0].astype(F32)
        for value in values[1:]:
            total = total + value.astype(F32)
        return total

    def joined(zx, p, q):
        left = jnp.concatenate([parts[1, zx][:6], add(parts[1, zx][6:], q).astype(BF)])
        right = jnp.concatenate([add(parts[2, zx][:6], p).astype(BF), parts[2, zx][6:]])
        return left, right

    p3, q3 = over_section(parts[3, 3][:6], 1), over_section(parts[3, 3][6:], 2)
    d2, d1 = over_section(parts[3, 2], 1), over_section(parts[3, 1], 2)
    left, right = joined(3, p3, q3)
    x3, y3 = over_section(left, 1), over_section(right, 2)
    p0, q0 = over_section(parts[3, 0][:6], 1), over_section(parts[3, 0][6:], 2)
    left, right = parts[1, 2], add(parts[2, 2], d2).astype(BF)
    x3, vec = lax.optimization_barrier((x3, vec))
    vec = lax.all_to_all(vec, BOTH, 0, 0, tiled=True)
    total = add(parts[0, 3], x3, y3).astype(BF)
    left, right, total = lax.optimization_barrier((left, right, total))
    z3 = over_z(total, 1)
    x2, y2 = over_section(left, 1), over_section(right, 2)
    left, right = add(parts[1, 1], d1).astype(BF), parts[2, 1]
    total = add(parts[0, 2], x2, y2, z3).astype(BF)
    left, right, total = lax.optimization_barrier((left, right, total))
    z2, s2 = over_z(total[:6], 2), over_z(total[6:], 2)
    x1, y1 = over_section(left, 1), over_section(right, 2)
    left, right = joined(0, p0, q0)
    total = add(parts[0, 1], x1, y1).astype(BF)
    left, right, total, z2 = lax.optimization_barrier((left, right, total, z2))
    x0, y0 = over_section(left, 1), over_section(right, 2)
    z1 = over_z(total, 1)
    return unpacked(parts[0, 0], x0, y0, z1, z2, s2), vec


def body_permuted(
    tokens, levels, lead, w_qkv, w_o, b_o, w_up, b_up, w_down, b_down, w_ada, b_ada, cotangent
):
    section, batch = lax.axis_index("section"), lax.axis_index("batch")
    place, core = batch // 2, batch % 2
    width = tokens.shape[2]
    rows = width // SHARDS
    ids = jnp.stack([section, place, core, levels[0]]).astype(jnp.int32)
    shard, small = packed(lead, w_qkv, w_o, w_up, w_down, b_o, b_up, b_down)
    mine = []

    def exchange(smalls):
        conds = jax.nn.silu(embed_lead(smalls[:, 4, 0], width))
        mine.append(lax.dynamic_slice_in_dim(conds, batch * rows, rows, axis=1))
        part = jnp.dot(mine[0], w_ada[0].astype(F32), precision=HIGH)
        bias = jnp.zeros((6 * width,), F32)
        bias = lax.dynamic_update_slice_in_dim(
            bias, b_ada[0].astype(F32), batch * 6 * rows, axis=0
        )
        return lax.all_to_all((part + bias).reshape(32, -1, 128), BOTH, 0, 0, tiled=True)

    plan, sources, smalls, part = gather_shards(shard, small, exchange)
    mine = mine[0]
    mods = jnp.sum(part.reshape(4, SHARDS, -1, 128), axis=1).reshape(4, 6, width)
    vectors = smalls.reshape(4, SHARDS, 16 * 128).astype(F32)
    biases = jnp.concatenate(
        [
            vectors[:, :, :rows].reshape(4, 1, width),
            vectors[:, :, 128 : 128 + 4 * rows].reshape(4, 4, width),
            vectors[:, :, 384 : 384 + rows].reshape(4, 1, width),
        ],
        axis=1,
    )

    result, w, *saved = forward(plan, sources, ids, tokens, mods, biases)
    grad = cotangent
    sums = jnp.zeros((4, 4, BLOCKS, rows, width), BF)
    vecs = [None] * 4
    for layer in reversed(range(4)):
        grad, kept, sent, vecs[layer] = backward(layer, ids, grad, mods, w, saved)
        both = (kept.astype(F32) + over_core(sent).astype(F32)).astype(BF)
        sums = lax.dynamic_update_index_in_dim(sums, both, section ^ layer, 0)
    vec = jnp.broadcast_to(jnp.stack(vecs)[:, None], (4, SHARDS, 48, 128)).reshape(32, 48, 128)
    totals, vec = sum_shards({(i, j): sums[i, j] for i in range(4) for j in range(4)}, vec)
    vec = vec[:, :36].astype(F32).reshape(32, 12, width)
    g_ada = jnp.dot(mine.T, vec[:, :6].reshape(32, 6 * width), precision=HIGH)[None]
    flat = jnp.sum(vec, 0)

    def slot(low, high, count):
        return lax.dynamic_slice_in_dim(
            flat[low:high].reshape(-1), batch * count, count, axis=0
        )[None]

    return (
        result,
        grad,
        totals[0],
        totals[1],
        slot(6, 7, rows),
        totals[2],
        slot(7, 11, 4 * rows),
        totals[3],
        slot(11, 12, rows),
        g_ada,
        slot(0, 6, 6 * rows),
    )


def pack_kernel(lead, w_qkv, w_o, w_up, w_down, b_o, b_up, b_down, out, small):
    _, rows, width = w_o.shape
    for j in range(3):
        out[j] = w_qkv[0, :, j * width : (j + 1) * width]
    out[3] = w_o[0]
    for j in range(4):
        out[4 + j] = w_up[0, :, j * width : (j + 1) * width]
        out[8 + j] = w_down[0, j * rows : (j + 1) * rows]
    small[...] = jnp.full(small.shape, lead[0].astype(F32), F32).astype(BF)
    peers = small.shape[0]
    for row, bias in zip((0, 1, 3), (b_o, b_up, b_down)):
        count = bias.shape[1]
        for start in range(0, count, 128):
            size = min(128, count - start)
            value = bias[0, start : start + size].astype(F32).reshape(1, 1, size)
            at = row + start // 128
            small[:, at : at + 1, :size] = jnp.broadcast_to(value, (peers, 1, size)).astype(BF)


def packed(lead, w_qkv, w_o, w_up, w_down, b_o, b_up, b_down):
    _, rows, width = w_o.shape
    vmem = pl.BlockSpec(memory_space=pltpu.VMEM)
    return pl.pallas_call(
        pack_kernel,
        in_specs=[pl.BlockSpec(memory_space=pltpu.SMEM)] + [vmem] * 7,
        out_shape=[
            jax.ShapeDtypeStruct((BLOCKS, rows, width), BF),
            jax.ShapeDtypeStruct((32, 16, 128), BF),
        ],
        name="pack",
    )(lead, w_qkv, w_o, w_up, w_down, b_o, b_up, b_down)


def unpack_kernel(own, x, y, z, low, high, g_qkv, g_o, g_up, g_down):
    _, rows, width = g_o.shape
    for j in range(BLOCKS):
        last = low[j] if j < 6 else high[j - 6]
        total = own[j].astype(F32) + x[j].astype(F32) + y[j].astype(F32)
        total = total + z[j].astype(F32) + last.astype(F32)
        if j < 3:
            g_qkv[0, :, j * width : (j + 1) * width] = total
        elif j == 3:
            g_o[0] = total
        elif j < 8:
            g_up[0, :, (j - 4) * width : (j - 3) * width] = total
        else:
            g_down[0, (j - 8) * rows : (j - 7) * rows] = total


def unpacked(own, x, y, z, low, high):
    _, rows, width = own.shape
    return pl.pallas_call(
        unpack_kernel,
        out_shape=[
            jax.ShapeDtypeStruct((1, rows, 3 * width), F32),
            jax.ShapeDtypeStruct((1, rows, width), F32),
            jax.ShapeDtypeStruct((1, rows, 4 * width), F32),
            jax.ShapeDtypeStruct((1, 4 * rows, width), F32),
        ],
        name="unpack",
    )(own, x, y, z, low, high)


def local_shard(w_qkv, w_o, w_up, w_down):
    _, rows, width = w_o.shape

    def blocks_of(piece):
        return jnp.stack(jnp.split(piece, piece.shape[1] // width, axis=1))

    return jnp.concatenate(
        [blocks_of(w_qkv[0]), w_o, blocks_of(w_up[0]), w_down[0].reshape(4, rows, width)]
    )


def body_general(
    tokens, levels, lead, w_qkv, w_o, b_o, w_up, b_up, w_down, b_down, w_ada, b_ada, cotangent
):
    batch = lax.axis_index("batch")
    sections, batches = lax.axis_size("section"), lax.axis_size("batch")
    width = tokens.shape[2]
    rows, tall = width // batches, width // SHARDS
    zero = jnp.zeros((), jnp.int32)
    ids = jnp.stack([zero, zero, zero, levels[0]])

    shards = lax.all_gather(local_shard(w_qkv, w_o, w_up, w_down), BOTH, axis=0, tiled=False)
    shards = shards.reshape(sections, batches, BLOCKS, rows, width)
    front = jnp.swapaxes(shards[:, :, :8], 1, 2).reshape(sections, 8, SHARDS, tall, width)
    downs = shards[:, :, 8:].reshape(sections, SHARDS, 4, tall, width)
    source = jnp.concatenate([jnp.swapaxes(front, 1, 2), downs], axis=2)
    source = source.reshape(sections * SHARDS * BLOCKS, tall, width)
    plan = {
        (l, z, c): [(0, ((l * 4 + z) * 2 + c) * BLOCKS, 0, BLOCKS)]
        for l in range(4)
        for z in range(4)
        for c in range(2)
    }
    small = jnp.concatenate([b_o[0], b_up[0], b_down[0]])
    smalls = lax.all_gather(small, BOTH, axis=0, tiled=False).reshape(sections, batches, -1)
    smalls = smalls.astype(F32)
    biases = jnp.concatenate(
        [
            smalls[:, :, :rows].reshape(sections, 1, width),
            smalls[:, :, rows : 5 * rows].reshape(sections, 4, width),
            smalls[:, :, 5 * rows :].reshape(sections, 1, width),
        ],
        axis=1,
    )
    leads = lax.all_gather(lead, BOTH, axis=0, tiled=True)
    conds = jax.nn.silu(embed_lead(leads, width))
    mine = lax.dynamic_slice_in_dim(conds, batch * rows, rows, axis=1)
    part = jnp.dot(mine, w_ada[0].astype(F32), precision=HIGH)
    bias = jnp.zeros((6 * width,), F32)
    bias = lax.dynamic_update_slice_in_dim(
        bias, b_ada[0].astype(F32), batch * 6 * rows, axis=0
    )
    part = (part + bias).reshape(sections, batches, 6 * width)
    part = lax.psum_scatter(part, "batch", scatter_dimension=1, tiled=True)
    mods = lax.all_to_all(part[:, 0], "section", 0, 0, tiled=True)
    mods = mods.reshape(sections, 6, width)

    result, w, *saved = forward(plan, [source], ids, tokens, mods, biases)
    grad = cotangent
    grads, vecs = [None] * sections, [None] * sections
    for layer in reversed(range(sections)):
        grad, kept, sent, vecs[layer] = backward(layer, ids, grad, mods, w, saved)
        grads[layer] = jnp.stack([kept, sent], axis=1).reshape(SHARDS, BLOCKS, tall, width)
    grads = jnp.stack(grads)
    front = jnp.swapaxes(grads[:, :, :8], 1, 2).reshape(sections, 8, batches, rows, width)
    downs = grads[:, :, 8:].reshape(sections, batches, 4, rows, width)
    total = jnp.concatenate([jnp.swapaxes(front, 1, 2), downs], axis=2)
    total = total.reshape(sections, batches, BLOCKS * rows, width)
    total = lax.psum_scatter(total, "section", scatter_dimension=0, tiled=True)
    total = lax.psum_scatter(total, "batch", scatter_dimension=1, tiled=True)
    total = total.astype(F32).reshape(BLOCKS, rows, width)

    vec = jnp.stack(vecs)[:, :36].reshape(sections, 12, width)
    vec = lax.all_to_all(vec, "section", 0, 0, tiled=True)
    vec = lax.all_gather(vec, "batch", axis=1, tiled=False).astype(F32)
    vec = vec.reshape(sections * batches, 12, width)
    g_ada = jnp.dot(mine.T, vec[:, :6].reshape(-1, 6 * width), precision=HIGH)[None]
    flat = jnp.sum(vec, 0)

    def slot(low, high, count):
        return lax.dynamic_slice_in_dim(
            flat[low:high].reshape(-1), batch * count, count, axis=0
        )[None]

    return (
        result,
        grad,
        jnp.concatenate([total[0], total[1], total[2]], axis=1)[None],
        total[3][None],
        slot(6, 7, rows),
        jnp.concatenate([total[4 + j] for j in range(4)], axis=1)[None],
        slot(7, 11, 4 * rows),
        total[8:].reshape(1, 4 * rows, width),
        slot(11, 12, rows),
        g_ada,
        slot(0, 6, 6 * rows),
    )


def solution(mesh):
    in_specs = (
        P(("section", "batch"), None, None),
        P(("section", "batch")),
        P(("section", "batch")),
        P("section", "batch", None),
        P("section", "batch", None),
        P("section", "batch"),
        P("section", "batch", None),
        P("section", "batch"),
        P("section", "batch", None),
        P("section", "batch"),
        P("section", "batch", None),
        P("section", "batch"),
        P(("section", "batch"), None, None),
    )
    out_specs = (
        P(("section", "batch"), None, None),
        P(("section", "batch"), None, None),
        P("section", "batch", None),
        P("section", "batch", None),
        P("section", "batch"),
        P("section", "batch", None),
        P("section", "batch"),
        P("section", "batch", None),
        P("section", "batch"),
        P("section", "batch", None),
        P("section", "batch"),
    )
    permuted = mesh.shape["section"] == 4 and mesh.shape["batch"] == SHARDS
    body = body_permuted if permuted else body_general
    return jax.shard_map(body, mesh=mesh, in_specs=in_specs, out_specs=out_specs, check_vma=False)
```

```python
import functools
import math

import jax
import jax.numpy as jnp
from jax import lax
from jax.experimental import pallas as pl
from jax.experimental.pallas import tpu as pltpu
from jax.sharding import PartitionSpec as P

HEADS = 6
LEVELS = 13
BLOCKS = 12
SHARDS = 8
EPS = 1e-06
NEG = -1e30
BF = jnp.bfloat16
F32 = jnp.float32
HIGH = lax.Precision.HIGHEST
BOTH = ("section", "batch")
C0 = math.sqrt(2.0 / math.pi)
C1 = 0.044715
VMEM_LIMIT = 60 * 2**20


def dot(left, right, over=(1, 0)):
    return lax.dot_general(
        left, right, (((over[0],), (over[1],)), ((), ())), preferred_element_type=F32
    )


def standard(value):
    centered = value - jnp.mean(value, -1, keepdims=True)
    rstd = lax.rsqrt(jnp.mean(centered * centered, -1, keepdims=True) + EPS)
    return centered * rstd, rstd


def standard_back(grad, normed, rstd):
    return rstd * (
        grad
        - jnp.mean(grad, -1, keepdims=True)
        - normed * jnp.mean(grad * normed, -1, keepdims=True)
    )


def forward_kernel(plan, ids, tokens, mods, biases, *refs):
    count = len({part[0] for parts in plan.values() for part in parts})
    sources, refs = refs[:count], refs[count:]
    result, w_out, outs, held = refs[0], refs[1], refs[2:10], refs[10:18]
    value, hidden, acc, w, in_sem, out_sem, save_sem = refs[18:]
    layer = pl.program_id(0)
    layers = pl.num_programs(0)
    seq, width = value.shape
    size = width // HEADS
    section, place, core = ids[0], ids[1], ids[2]

    @pl.when(layer == 0)
    def _():
        value[...] = tokens[0]

        @pl.loop(0, layers)
        def _(target):
            for away in range(4):

                @pl.when(jnp.bitwise_xor(section, target) == away)
                def _():
                    for (sx, zx, cx), parts in plan.items():
                        if sx != away:
                            continue
                        shard = 2 * jnp.bitwise_xor(place, zx) + jnp.bitwise_xor(core, cx)
                        for index, lead, low, high in parts:
                            ref = sources[index]
                            top = min(high, 8)
                            if low < top:
                                pltpu.make_async_copy(
                                    ref.at[pl.ds(lead, top - low)],
                                    w.at[target, pl.ds(low, top - low), shard],
                                    in_sem.at[target],
                                ).start()
                            if high > 8:
                                pltpu.make_async_copy(
                                    ref.at[pl.ds(lead + 8 - low, 4)],
                                    w.at[target, 8 + shard // 2, pl.ds(4 * (shard % 2), 4)],
                                    in_sem.at[target],
                                ).start()

    pltpu.make_async_copy(w.at[layer], w.at[layer], in_sem.at[layer]).wait()
    pltpu.make_async_copy(w.at[layer], w_out.at[layer], out_sem.at[layer]).start()

    slot = layer % 2
    xs, qkv, probs, mixed, branch_a, act, slope, branch_b = (ref.at[slot] for ref in held)

    def saving(i, half, target):
        return pltpu.make_async_copy(held[i].at[half], outs[i].at[target], save_sem.at[i, half])

    def reuse(*which):
        @pl.when(layer >= 2)
        def _():
            for i in which:
                saving(i, slot, layer).wait()

    def save(*which):
        for i in which:
            saving(i, slot, layer).start()

    def weight(j):
        return w[layer, j].reshape(width, width)

    def weights(low, high):
        return jnp.concatenate([weight(j) for j in range(low, high)], axis=1)

    mod = mods[layer]
    bias = biases[layer]
    reuse(*range(8))
    xs[...] = value[...]
    save(0)
    x = value[...].astype(F32)
    normed, _ = standard(x)
    hidden[...] = (normed * (1.0 + mod[1:2]) + mod[0:1]).astype(BF)
    qkv[...] = dot(hidden[...], weights(0, 3)).astype(BF)
    save(1)
    limit = ids[3] * (seq // LEVELS)
    row = lax.broadcasted_iota(jnp.int32, (seq, 1), 0)
    mask = jnp.where(row < limit, 0.0, NEG)
    def score(h):
        q = qkv[:, h * size : (h + 1) * size] * (size**-0.5)
        k = qkv[:, width + h * size : width + (h + 1) * size]
        return dot(k, q, (1, 1)) + mask

    def attend(h, raw):
        top = jnp.max(raw, axis=0, keepdims=True)
        e = jnp.exp(raw - top)
        p = (e * (1.0 / jnp.sum(e, axis=0, keepdims=True))).astype(BF)
        probs[h] = p
        return p

    def mix(h, p):
        v = qkv[:, 2 * width + h * size : 2 * width + (h + 1) * size]
        mixed[h * size : (h + 1) * size, :] = dot(v, p, (0, 0)).astype(BF)

    raws = {h: score(h) for h in range(2)}
    held_p = None
    for h in range(HEADS):
        if h + 2 < HEADS:
            raws[h + 2] = score(h + 2)
        p = attend(h, raws.pop(h))
        if held_p is not None:
            mix(h - 1, held_p)
        held_p = p
    mix(HEADS - 1, held_p)
    save(2, 3)
    ba = dot(mixed[...], weight(3), (0, 0)) + bias[0:1]
    branch_a[...] = ba
    save(4)
    middle = value[...].astype(F32) + mod[2:3] * ba
    acc[...] = middle
    normed, _ = standard(middle)
    hidden[...] = (normed * (1.0 + mod[4:5]) + mod[3:4]).astype(BF)
    for j in range(0, 4, 2):
        cols = slice(j * width, (j + 2) * width)
        shift = jnp.concatenate([bias[1 + i : 2 + i] for i in range(j, j + 2)], axis=1)
        pre = dot(hidden[...], weights(4 + j, 4 + j + 2)) + shift
        square = pre * pre
        t = jnp.tanh(pre * (C0 + (C0 * C1) * square))
        half = 0.5 + 0.5 * t
        a = pre * half
        slope[:, cols] = (half + a * (1.0 - t) * (C0 + (3.0 * C0 * C1) * square)).astype(BF)
        act[:, cols] = a.astype(BF)
    save(5, 6)
    bb = dot(act[...], w[layer, 8:12].reshape(4 * width, width)) + bias[5:6]
    branch_b[...] = bb.astype(BF)
    save(7)
    out = (acc[...] + mod[5:6] * bb).astype(BF)
    value[...] = out
    result[0] = out

    @pl.when(layer == layers - 1)
    def _():
        for i in range(8):
            for half in range(2):
                saving(i, half, layer).wait()

        @pl.loop(0, layers)
        def _(target):
            pltpu.make_async_copy(w.at[target], w_out.at[target], out_sem.at[target]).wait()


def forward(plan, sources, ids, tokens, mods, biases):
    layers = mods.shape[0]
    _, seq, width = tokens.shape
    rows = width // SHARDS

    def same(*shape):
        return pl.BlockSpec(shape, lambda l: (0,) * len(shape))

    shapes = [
        ((seq, width), BF),
        ((seq, 3 * width), BF),
        ((HEADS, seq, seq), BF),
        ((width, seq), BF),
        ((seq, width), F32),
        ((seq, 4 * width), BF),
        ((seq, 4 * width), BF),
        ((seq, width), BF),
    ]
    hbm = pl.BlockSpec(memory_space=pl.ANY)
    return pl.pallas_call(
        functools.partial(forward_kernel, plan),
        grid=(layers,),
        in_specs=[
            pl.BlockSpec(memory_space=pltpu.SMEM),
            same(1, seq, width),
            same(layers, 6, width),
            same(layers, 6, width),
        ]
        + [hbm] * len(sources),
        out_specs=[same(1, seq, width), hbm] + [hbm] * len(shapes),
        out_shape=[
            jax.ShapeDtypeStruct((1, seq, width), BF),
            jax.ShapeDtypeStruct((layers, BLOCKS, SHARDS, rows, width), BF),
        ]
        + [jax.ShapeDtypeStruct((layers,) + s, d) for s, d in shapes],
        scratch_shapes=[pltpu.VMEM((2,) + s, d) for s, d in shapes]
        + [
            pltpu.VMEM((seq, width), BF),
            pltpu.VMEM((seq, width), BF),
            pltpu.VMEM((seq, width), F32),
            pltpu.VMEM((layers, BLOCKS, SHARDS, rows, width), BF),
            pltpu.SemaphoreType.DMA((layers,)),
            pltpu.SemaphoreType.DMA((layers,)),
            pltpu.SemaphoreType.DMA((len(shapes), 2)),
        ],
        compiler_params=pltpu.CompilerParams(vmem_limit_bytes=VMEM_LIMIT),
        cost_estimate=pl.CostEstimate(
            flops=layers * 1_740_000_000, bytes_accessed=80_000_000, transcendentals=0
        ),
        name="forward",
    )(ids, tokens, mods, biases, *sources)


def backward_kernel(layer, ids, mods, *refs):
    tensors, refs = refs[:10], refs[10:]
    grad_in, kept, sent, vec_out, gbb, hid, gsum, gmix, gqkv, gpre, dqt, halves = refs[:12]
    held, vec, in_sem, out_sem = refs[12:22], refs[22], refs[23], refs[24]
    grad, w, xs, qkv, probs, mixed, branch_a, act, slope, branch_b = held
    seq, width = gbb.shape
    size = width // HEADS
    place, core = ids[1], ids[2]
    rows = width // SHARDS
    names = ("grad", "w", "xs", "qkv", "probs", "mixed", "branch_a", "act", "slope", "branch_b")
    pieces = {}
    for name, far, near in zip(names, tensors, held):
        far = far.at[0] if name == "grad" else far.at[layer]
        if name == "w":
            for low, high in ((8, 12), (4, 8), (3, 4), (0, 3)):
                cut = pl.ds(low, high - low)
                pieces[name, low] = (far.at[cut], near.at[cut])
        else:
            pieces[name] = (far, near)
    order = (
        "grad", "branch_b", "act", "xs", "branch_a", ("w", 8), "slope",
        ("w", 4), ("w", 3), "mixed", "qkv", "probs", ("w", 0),
    )
    loads = {
        name: pltpu.make_async_copy(*pieces[name], in_sem.at[i]) for i, name in enumerate(order)
    }
    for name in order:
        loads[name].start()

    def ready(*names):
        for name in names:
            loads[name].wait()

    def weight(j):
        return w[j].reshape(width, width)

    def keep(shard, block, value):
        half = jnp.bitwise_xor(core, shard % 2)
        halves[half, jnp.bitwise_xor(place, shard // 2), block] = value

    def keep_front(block, value):
        for shard in range(SHARDS):
            keep(shard, block, value[shard * rows : (shard + 1) * rows])

    def keep_down(j, value):
        for part in range(SHARDS):
            keep(2 * j + part // 4, 8 + part % 4, value[part * rows : (part + 1) * rows])

    def put(row, value):
        for part in range(width // 128):
            at = row * (width // 128) + part
            vec[at : at + 1] = value[:, part * 128 : (part + 1) * 128]

    stores = []

    def store(low, high):
        cut = pl.ds(low, high - low)
        for half, out in ((1, sent), (0, kept)):
            copy = pltpu.make_async_copy(
                halves.at[half, :, cut], out.at[:, cut], out_sem.at[len(stores)]
            )
            copy.start()
            stores.append(copy)

    mod = mods[layer]
    shift_a, scale_a, gate_a, shift_b, scale_b, gate_b = (mod[i : i + 1] for i in range(6))
    vec[...] = jnp.zeros_like(vec)
    ready("grad", "branch_b")
    gout = grad[...].astype(F32)
    put(5, jnp.sum(gout * branch_b[...].astype(F32), 0, keepdims=True))
    gb = (gout * gate_b).astype(BF)
    gbb[...] = gb
    put(11, jnp.sum(gb.astype(F32), 0, keepdims=True))
    ready("act")
    for j in range(4):
        cols = slice(j * width, (j + 1) * width)
        keep_down(j, dot(act[:, cols], gbb[...], (0, 0)).astype(BF))
    ready("xs", "branch_a")
    x = xs[...].astype(F32)
    middle = x + gate_a * branch_a[...]
    normed_b, rstd_b = standard(middle)
    hid[...] = (normed_b * (1.0 + scale_b) + shift_b).astype(BF).T
    ready(("w", 8), "slope")
    for j in range(4):
        cols = slice(j * width, (j + 1) * width)
        gact = dot(gbb[...], weight(8 + j), (1, 1))
        g = (gact * slope[:, cols].astype(F32)).astype(BF)
        gpre[:, cols] = g
        put(7 + j, jnp.sum(g.astype(F32), 0, keepdims=True))
    for j in range(4):
        cols = slice(j * width, (j + 1) * width)
        keep_front(4 + j, dot(hid[...], gpre[:, cols]).astype(BF))
    store(4, 12)
    ready(("w", 4))
    ghb = dot(gpre[...], jnp.concatenate([weight(4 + j) for j in range(4)], axis=1), (1, 1))
    put(3, jnp.sum(ghb, 0, keepdims=True))
    put(4, jnp.sum(ghb * normed_b, 0, keepdims=True))
    gmid = gout + standard_back(ghb * (1.0 + scale_b), normed_b, rstd_b)
    gsum[...] = gmid
    put(2, jnp.sum(gmid * branch_a[...], 0, keepdims=True))
    gba = (gmid * gate_a).astype(BF)
    gbb[...] = gba
    put(6, jnp.sum(gba.astype(F32), 0, keepdims=True))
    ready(("w", 3), "mixed")
    gmix[...] = dot(gbb[...], weight(3), (1, 1)).astype(BF)
    keep_front(3, dot(mixed[...], gbb[...]).astype(BF))
    factor = size**-0.5
    ready("qkv", "probs")
    def part(i, h):
        return qkv[:, i * width + h * size : i * width + (h + 1) * size]

    def probe(h):
        return dot(part(2, h), gmix[:, h * size : (h + 1) * size], (1, 1))

    def finish(h, ds):
        gqkv[:, 2 * width + h * size : 2 * width + (h + 1) * size] = dot(
            probs[h], gmix[:, h * size : (h + 1) * size]
        ).astype(BF)
        gqkv[:, width + h * size : width + (h + 1) * size] = dot(ds, part(0, h)).astype(BF)
        dqt[h * size : (h + 1) * size, :] = dot(part(1, h), ds, (0, 0)).astype(BF)

    dps = {h: probe(h) for h in range(1)}
    waiting = []
    for h in range(HEADS):
        if h + 1 < HEADS:
            dps[h + 1] = probe(h + 1)
        pf = probs[h].astype(F32)
        dp = dps.pop(h)
        inner = jnp.sum(dp * pf, axis=0, keepdims=True)
        waiting.append((h, (pf * (dp - inner) * factor).astype(BF)))
        if len(waiting) > 0:
            finish(*waiting.pop(0))
    for item in waiting:
        finish(*item)
    gqkv[:, :width] = dqt[...].T
    normed_a, rstd_a = standard(xs[...].astype(F32))
    hid[...] = (normed_a * (1.0 + scale_a) + shift_a).astype(BF).T
    for j in range(3):
        cols = slice(j * width, (j + 1) * width)
        keep_front(j, dot(hid[...], gqkv[:, cols]).astype(BF))
    store(0, 4)
    ready(("w", 0))
    gha = dot(gqkv[...], jnp.concatenate([weight(j) for j in range(3)], axis=1), (1, 1))
    put(0, jnp.sum(gha, 0, keepdims=True))
    put(1, jnp.sum(gha * normed_a, 0, keepdims=True))
    grad_in[0] = (gsum[...] + standard_back(gha * (1.0 + scale_a), normed_a, rstd_a)).astype(BF)
    vec_out[...] = vec[...].astype(BF)
    for copy in stores:
        copy.wait()


def backward(layer, ids, grad, mods, w, saved):
    _, seq, width = grad.shape
    rows = width // SHARDS

    def full(*shape):
        return pl.BlockSpec(shape, lambda i: (0,) * len(shape))

    half = (SHARDS // 2, BLOCKS, rows, width)
    hbm = pl.BlockSpec(memory_space=pl.ANY)
    tensors = (grad, w, *saved)
    return pl.pallas_call(
        functools.partial(backward_kernel, layer),
        grid=(1,),
        in_specs=[pl.BlockSpec(memory_space=pltpu.SMEM), full(*mods.shape)] + [hbm] * len(tensors),
        out_specs=[full(1, seq, width), hbm, hbm, full(48, 128)],
        out_shape=[
            jax.ShapeDtypeStruct((1, seq, width), BF),
            jax.ShapeDtypeStruct(half, BF),
            jax.ShapeDtypeStruct(half, BF),
            jax.ShapeDtypeStruct((48, 128), BF),
        ],
        scratch_shapes=[
            pltpu.VMEM((seq, width), BF),
            pltpu.VMEM((width, seq), BF),
            pltpu.VMEM((seq, width), F32),
            pltpu.VMEM((seq, width), BF),
            pltpu.VMEM((seq, 3 * width), BF),
            pltpu.VMEM((seq, 4 * width), BF),
            pltpu.VMEM((width, seq), BF),
            pltpu.VMEM((2,) + half, BF),
        ]
        + [pltpu.VMEM(a.shape[1:], a.dtype) for a in tensors]
        + [
            pltpu.VMEM((48, 128), F32),
            pltpu.SemaphoreType.DMA((13,)),
            pltpu.SemaphoreType.DMA((4,)),
        ],
        compiler_params=pltpu.CompilerParams(vmem_limit_bytes=VMEM_LIMIT),
        cost_estimate=pl.CostEstimate(
            flops=3_480_000_000, bytes_accessed=20_000_000, transcendentals=0
        ),
        name=f"backward_{layer}",
    )(ids, mods, *tensors)


def embed_lead(steps, width):
    half = width // 2
    freq = jnp.exp(-math.log(10000.0) * jnp.arange(half, dtype=F32) / half)
    angle = 6.0 * steps.astype(F32)[:, None] * freq[None, :]
    return jnp.concatenate([jnp.sin(angle), jnp.cos(angle)], -1)


def over_core(value):
    return lax.ppermute(value, "batch", [(i, i ^ 1) for i in range(8)])


def over_z(value, away):
    return lax.ppermute(value, "batch", [(i, i ^ (2 * away)) for i in range(8)])


def over_section(value, away):
    return lax.ppermute(value, "section", [(i, i ^ away) for i in range(4)])


def after(value, *others):
    return lax.optimization_barrier((value,) + others)[0]


def gather_shards(w, small, exchange):
    z2, z1 = over_z(w, 2), over_z(w, 1)
    y0, x0 = over_section(w, 2), over_section(w, 1)
    small = lax.all_to_all(small, BOTH, 0, 0, tiled=True)
    x1, y1 = over_section(z1, 1), over_section(z1, 2)
    z3 = over_z(z2, 1)
    p0, q0 = over_section(y0[:6], 1), over_section(x0[6:], 2)
    y1, small = lax.optimization_barrier((y1, small))
    part = exchange(small)
    x2, y2 = over_section(z2, 1), over_section(z2, 2)
    p1, q1 = over_section(y1[:6], 1), over_section(x1[6:], 2)
    x3, y3 = over_section(z3, 1), over_section(z3, 2)
    p2, q2 = over_section(y2[:6], 1), over_section(x2[6:], 2)
    x3, part = lax.optimization_barrier((x3, part))
    p3, q3 = over_section(y3[:6], 1), over_section(x3[6:], 2)
    names = {}
    for zx, group in enumerate(
        [(w, x0, y0, p0, q0), (z1, x1, y1, p1, q1), (z2, x2, y2, p2, q2), (z3, x3, y3, p3, q3)]
    ):
        names[0, zx], names[1, zx], names[2, zx] = [(group[0], 0)], [(group[1], 0)], [(group[2], 0)]
        names[3, zx] = [(group[3], 0), (group[4], 6)]
    sources, plan = [], {}
    for keys in (
        [(0, 0), (0, 1), (1, 0), (2, 0), (1, 1), (2, 1), (3, 0)],
        [(0, 2), (0, 3), (3, 1), (1, 2), (2, 2)],
        [(1, 3), (2, 3), (3, 2), (3, 3)],
    ):
        bundle = []
        for key in keys:
            plan[key + (0,)], plan[key + (1,)] = [], []
            for array, low in names[key]:
                plan[key + (0,)].append((len(sources), low, 0))
                sources.append(array)
                bundle.append((key, array, low))
        other = over_core(jnp.concatenate([array for _, array, _ in bundle]))
        start = 0
        for key, array, low in bundle:
            plan[key + (1,)].append((len(sources), low, start))
            start += array.shape[0]
        sources.append(other)
    final = {}
    for key, parts in plan.items():
        final[key] = []
        for index, low, start in parts:
            high = BLOCKS if key[0] != 3 else low + 6
            final[key].append((index, start, low, high))
    return final, sources, small, part


def sum_shards(parts, vec):
    def add(*values):
        total = values[0].astype(F32)
        for value in values[1:]:
            total = total + value.astype(F32)
        return total

    def joined(zx, p, q):
        left = jnp.concatenate([parts[1, zx][:6], add(parts[1, zx][6:], q).astype(BF)])
        right = jnp.concatenate([add(parts[2, zx][:6], p).astype(BF), parts[2, zx][6:]])
        return left, right

    p3, q3 = over_section(parts[3, 3][:6], 1), over_section(parts[3, 3][6:], 2)
    d2, d1 = over_section(parts[3, 2], 1), over_section(parts[3, 1], 2)
    left, right = joined(3, p3, q3)
    x3, y3 = over_section(left, 1), over_section(right, 2)
    p0, q0 = over_section(parts[3, 0][:6], 1), over_section(parts[3, 0][6:], 2)
    left, right = parts[1, 2], add(parts[2, 2], d2).astype(BF)
    x3, vec = lax.optimization_barrier((x3, vec))
    vec = lax.all_to_all(vec, BOTH, 0, 0, tiled=True)
    total = add(parts[0, 3], x3, y3).astype(BF)
    left, right, total = lax.optimization_barrier((left, right, total))
    z3 = over_z(total, 1)
    x2, y2 = over_section(left, 1), over_section(right, 2)
    left, right = add(parts[1, 1], d1).astype(BF), parts[2, 1]
    total = add(parts[0, 2], x2, y2, z3).astype(BF)
    left, right, total = lax.optimization_barrier((left, right, total))
    z2, s2 = over_z(total[:6], 2), over_z(total[6:], 2)
    x1, y1 = over_section(left, 1), over_section(right, 2)
    left, right = joined(0, p0, q0)
    total = add(parts[0, 1], x1, y1).astype(BF)
    left, right, total, z2 = lax.optimization_barrier((left, right, total, z2))
    x0, y0 = over_section(left, 1), over_section(right, 2)
    z1 = over_z(total, 1)
    return unpacked(parts[0, 0], x0, y0, z1, z2, s2), vec


def body_permuted(
    tokens, levels, lead, w_qkv, w_o, b_o, w_up, b_up, w_down, b_down, w_ada, b_ada, cotangent
):
    section, batch = lax.axis_index("section"), lax.axis_index("batch")
    place, core = batch // 2, batch % 2
    width = tokens.shape[2]
    rows = width // SHARDS
    ids = jnp.stack([section, place, core, levels[0]]).astype(jnp.int32)
    shard, small = packed(lead, w_qkv, w_o, w_up, w_down, b_o, b_up, b_down)
    mine = []

    def exchange(smalls):
        conds = jax.nn.silu(embed_lead(smalls[:, 4, 0], width))
        mine.append(lax.dynamic_slice_in_dim(conds, batch * rows, rows, axis=1))
        part = jnp.dot(mine[0], w_ada[0].astype(F32), precision=HIGH)
        bias = jnp.zeros((6 * width,), F32)
        bias = lax.dynamic_update_slice_in_dim(
            bias, b_ada[0].astype(F32), batch * 6 * rows, axis=0
        )
        return lax.all_to_all((part + bias).reshape(32, -1, 128), BOTH, 0, 0, tiled=True)

    plan, sources, smalls, part = gather_shards(shard, small, exchange)
    mine = mine[0]
    mods = jnp.sum(part.reshape(4, SHARDS, -1, 128), axis=1).reshape(4, 6, width)
    vectors = smalls.reshape(4, SHARDS, 16 * 128).astype(F32)
    biases = jnp.concatenate(
        [
            vectors[:, :, :rows].reshape(4, 1, width),
            vectors[:, :, 128 : 128 + 4 * rows].reshape(4, 4, width),
            vectors[:, :, 384 : 384 + rows].reshape(4, 1, width),
        ],
        axis=1,
    )

    result, w, *saved = forward(plan, sources, ids, tokens, mods, biases)
    grad = cotangent
    sums = jnp.zeros((4, 4, BLOCKS, rows, width), BF)
    vecs = [None] * 4
    for layer in reversed(range(4)):
        grad, kept, sent, vecs[layer] = backward(layer, ids, grad, mods, w, saved)
        both = (kept.astype(F32) + over_core(sent).astype(F32)).astype(BF)
        sums = lax.dynamic_update_index_in_dim(sums, both, section ^ layer, 0)
    vec = jnp.broadcast_to(jnp.stack(vecs)[:, None], (4, SHARDS, 48, 128)).reshape(32, 48, 128)
    totals, vec = sum_shards({(i, j): sums[i, j] for i in range(4) for j in range(4)}, vec)
    vec = vec[:, :36].astype(F32).reshape(32, 12, width)
    g_ada = jnp.dot(mine.T, vec[:, :6].reshape(32, 6 * width), precision=HIGH)[None]
    flat = jnp.sum(vec, 0)

    def slot(low, high, count):
        return lax.dynamic_slice_in_dim(
            flat[low:high].reshape(-1), batch * count, count, axis=0
        )[None]

    return (
        result,
        grad,
        totals[0],
        totals[1],
        slot(6, 7, rows),
        totals[2],
        slot(7, 11, 4 * rows),
        totals[3],
        slot(11, 12, rows),
        g_ada,
        slot(0, 6, 6 * rows),
    )


def pack_kernel(lead, w_qkv, w_o, w_up, w_down, b_o, b_up, b_down, out, small):
    _, rows, width = w_o.shape
    for j in range(3):
        out[j] = w_qkv[0, :, j * width : (j + 1) * width]
    out[3] = w_o[0]
    for j in range(4):
        out[4 + j] = w_up[0, :, j * width : (j + 1) * width]
        out[8 + j] = w_down[0, j * rows : (j + 1) * rows]
    small[...] = jnp.full(small.shape, lead[0].astype(F32), F32).astype(BF)
    peers = small.shape[0]
    for row, bias in zip((0, 1, 3), (b_o, b_up, b_down)):
        count = bias.shape[1]
        for start in range(0, count, 128):
            size = min(128, count - start)
            value = bias[0, start : start + size].astype(F32).reshape(1, 1, size)
            at = row + start // 128
            small[:, at : at + 1, :size] = jnp.broadcast_to(value, (peers, 1, size)).astype(BF)


def packed(lead, w_qkv, w_o, w_up, w_down, b_o, b_up, b_down):
    _, rows, width = w_o.shape
    vmem = pl.BlockSpec(memory_space=pltpu.VMEM)
    return pl.pallas_call(
        pack_kernel,
        in_specs=[pl.BlockSpec(memory_space=pltpu.SMEM)] + [vmem] * 7,
        out_shape=[
            jax.ShapeDtypeStruct((BLOCKS, rows, width), BF),
            jax.ShapeDtypeStruct((32, 16, 128), BF),
        ],
        name="pack",
    )(lead, w_qkv, w_o, w_up, w_down, b_o, b_up, b_down)


def unpack_kernel(own, x, y, z, low, high, g_qkv, g_o, g_up, g_down):
    _, rows, width = g_o.shape
    for j in range(BLOCKS):
        last = low[j] if j < 6 else high[j - 6]
        total = own[j].astype(F32) + x[j].astype(F32) + y[j].astype(F32)
        total = total + z[j].astype(F32) + last.astype(F32)
        if j < 3:
            g_qkv[0, :, j * width : (j + 1) * width] = total
        elif j == 3:
            g_o[0] = total
        elif j < 8:
            g_up[0, :, (j - 4) * width : (j - 3) * width] = total
        else:
            g_down[0, (j - 8) * rows : (j - 7) * rows] = total


def unpacked(own, x, y, z, low, high):
    _, rows, width = own.shape
    return pl.pallas_call(
        unpack_kernel,
        out_shape=[
            jax.ShapeDtypeStruct((1, rows, 3 * width), F32),
            jax.ShapeDtypeStruct((1, rows, width), F32),
            jax.ShapeDtypeStruct((1, rows, 4 * width), F32),
            jax.ShapeDtypeStruct((1, 4 * rows, width), F32),
        ],
        name="unpack",
    )(own, x, y, z, low, high)


def local_shard(w_qkv, w_o, w_up, w_down):
    _, rows, width = w_o.shape

    def blocks_of(piece):
        return jnp.stack(jnp.split(piece, piece.shape[1] // width, axis=1))

    return jnp.concatenate(
        [blocks_of(w_qkv[0]), w_o, blocks_of(w_up[0]), w_down[0].reshape(4, rows, width)]
    )


def body_general(
    tokens, levels, lead, w_qkv, w_o, b_o, w_up, b_up, w_down, b_down, w_ada, b_ada, cotangent
):
    batch = lax.axis_index("batch")
    sections, batches = lax.axis_size("section"), lax.axis_size("batch")
    width = tokens.shape[2]
    rows, tall = width // batches, width // SHARDS
    zero = jnp.zeros((), jnp.int32)
    ids = jnp.stack([zero, zero, zero, levels[0]])

    shards = lax.all_gather(local_shard(w_qkv, w_o, w_up, w_down), BOTH, axis=0, tiled=False)
    shards = shards.reshape(sections, batches, BLOCKS, rows, width)
    front = jnp.swapaxes(shards[:, :, :8], 1, 2).reshape(sections, 8, SHARDS, tall, width)
    downs = shards[:, :, 8:].reshape(sections, SHARDS, 4, tall, width)
    source = jnp.concatenate([jnp.swapaxes(front, 1, 2), downs], axis=2)
    source = source.reshape(sections * SHARDS * BLOCKS, tall, width)
    plan = {
        (l, z, c): [(0, ((l * 4 + z) * 2 + c) * BLOCKS, 0, BLOCKS)]
        for l in range(4)
        for z in range(4)
        for c in range(2)
    }
    small = jnp.concatenate([b_o[0], b_up[0], b_down[0]])
    smalls = lax.all_gather(small, BOTH, axis=0, tiled=False).reshape(sections, batches, -1)
    smalls = smalls.astype(F32)
    biases = jnp.concatenate(
        [
            smalls[:, :, :rows].reshape(sections, 1, width),
            smalls[:, :, rows : 5 * rows].reshape(sections, 4, width),
            smalls[:, :, 5 * rows :].reshape(sections, 1, width),
        ],
        axis=1,
    )
    leads = lax.all_gather(lead, BOTH, axis=0, tiled=True)
    conds = jax.nn.silu(embed_lead(leads, width))
    mine = lax.dynamic_slice_in_dim(conds, batch * rows, rows, axis=1)
    part = jnp.dot(mine, w_ada[0].astype(F32), precision=HIGH)
    bias = jnp.zeros((6 * width,), F32)
    bias = lax.dynamic_update_slice_in_dim(
        bias, b_ada[0].astype(F32), batch * 6 * rows, axis=0
    )
    part = (part + bias).reshape(sections, batches, 6 * width)
    part = lax.psum_scatter(part, "batch", scatter_dimension=1, tiled=True)
    mods = lax.all_to_all(part[:, 0], "section", 0, 0, tiled=True)
    mods = mods.reshape(sections, 6, width)

    result, w, *saved = forward(plan, [source], ids, tokens, mods, biases)
    grad = cotangent
    grads, vecs = [None] * sections, [None] * sections
    for layer in reversed(range(sections)):
        grad, kept, sent, vecs[layer] = backward(layer, ids, grad, mods, w, saved)
        grads[layer] = jnp.stack([kept, sent], axis=1).reshape(SHARDS, BLOCKS, tall, width)
    grads = jnp.stack(grads)
    front = jnp.swapaxes(grads[:, :, :8], 1, 2).reshape(sections, 8, batches, rows, width)
    downs = grads[:, :, 8:].reshape(sections, batches, 4, rows, width)
    total = jnp.concatenate([jnp.swapaxes(front, 1, 2), downs], axis=2)
    total = total.reshape(sections, batches, BLOCKS * rows, width)
    total = lax.psum_scatter(total, "section", scatter_dimension=0, tiled=True)
    total = lax.psum_scatter(total, "batch", scatter_dimension=1, tiled=True)
    total = total.astype(F32).reshape(BLOCKS, rows, width)

    vec = jnp.stack(vecs)[:, :36].reshape(sections, 12, width)
    vec = lax.all_to_all(vec, "section", 0, 0, tiled=True)
    vec = lax.all_gather(vec, "batch", axis=1, tiled=False).astype(F32)
    vec = vec.reshape(sections * batches, 12, width)
    g_ada = jnp.dot(mine.T, vec[:, :6].reshape(-1, 6 * width), precision=HIGH)[None]
    flat = jnp.sum(vec, 0)

    def slot(low, high, count):
        return lax.dynamic_slice_in_dim(
            flat[low:high].reshape(-1), batch * count, count, axis=0
        )[None]

    return (
        result,
        grad,
        jnp.concatenate([total[0], total[1], total[2]], axis=1)[None],
        total[3][None],
        slot(6, 7, rows),
        jnp.concatenate([total[4 + j] for j in range(4)], axis=1)[None],
        slot(7, 11, 4 * rows),
        total[8:].reshape(1, 4 * rows, width),
        slot(11, 12, rows),
        g_ada,
        slot(0, 6, 6 * rows),
    )


def solution(mesh):
    in_specs = (
        P(("section", "batch"), None, None),
        P(("section", "batch")),
        P(("section", "batch")),
        P("section", "batch", None),
        P("section", "batch", None),
        P("section", "batch"),
        P("section", "batch", None),
        P("section", "batch"),
        P("section", "batch", None),
        P("section", "batch"),
        P("section", "batch", None),
        P("section", "batch"),
        P(("section", "batch"), None, None),
    )
    out_specs = (
        P(("section", "batch"), None, None),
        P(("section", "batch"), None, None),
        P("section", "batch", None),
        P("section", "batch", None),
        P("section", "batch"),
        P("section", "batch", None),
        P("section", "batch"),
        P("section", "batch", None),
        P("section", "batch"),
        P("section", "batch", None),
        P("section", "batch"),
    )
    permuted = mesh.shape["section"] == 4 and mesh.shape["batch"] == SHARDS
    body = body_permuted if permuted else body_general
    return jax.shard_map(body, mesh=mesh, in_specs=in_specs, out_specs=out_specs, check_vma=False)
```
